32 devices in a mesh: dp: 8 (over z, y), blk: 4 (over x, core).
Axes of the slice: x: 2, y: 2, z: 4, core: 2. Of those that a mesh axis runs over, the one named last changes fastest.
Arguments:
- tokens: float32 [96, 488, 768], P('dp', 'blk'), may hold values from -6 to 6
- kept_time: int32 [96, 48], P('dp'), may hold values from 0 to 1, as said below
- kept_bands: int32 [96, 10], P('dp'), may hold values from 0 to 1, as said below
- cotangent: float32 [96, 488, 768], P('dp', 'blk'), may hold values from -6 to 6
- weight_merged: float32 [768, 2304], P(('dp', 'blk')), may hold values from -0.21875 to 0.21875
- weight_output: float32 [768, 768], P(('dp', 'blk')), may hold values from -1.25 to 1.25
- weight_expand: float32 [768, 3072], P(('dp', 'blk')), may hold values from -0.21875 to 0.21875
- weight_shrink: float32 [3072, 768], P(('dp', 'blk')), may hold values from -0.109375 to 0.109375
- vectors: float32 [12, 768], P(None, ('dp', 'blk'))
- first_merged: float32 [768, 2304], P(('dp', 'blk')), may hold values from -0.0024414062 to 0.0024414062
- first_output: float32 [768, 768], P(('dp', 'blk')), may hold values from -0.00048828125 to 0.00048828125
- first_expand: float32 [768, 3072], P(('dp', 'blk')), may hold values from -0.0017089844 to 0.0017089844
- first_shrink: float32 [3072, 768], P(('dp', 'blk')), may hold values from -0.0029296875 to 0.0029296875
- first_vectors: float32 [12, 768], P(None, ('dp', 'blk')), may hold values from -0.0048828125 to 0.0048828125
- second_merged: float32 [768, 2304], P(('dp', 'blk')), may hold values from 1.4717196e-07 to 5.8868784e-07
- second_output: float32 [768, 768], P(('dp', 'blk')), may hold values from 5.8868785e-09 to 2.3547514e-08
- second_expand: float32 [768, 3072], P(('dp', 'blk')), may hold values from 7.211426e-08 to 2.8845704e-07
- second_shrink: float32 [3072, 768], P(('dp', 'blk')), may hold values from 2.4872062e-07 to 9.948825e-07
- second_vectors: float32 [12, 768], P(None, ('dp', 'blk')), may hold values from 5.8868784e-07 to 2.3547514e-06
Outputs:
- activations: float32 [96, 488, 768], P('dp', 'blk')
- token_grads: float32 [96, 488, 768], P('dp', 'blk')
- gradient_norm: float32 [], replicated
- clipped_merged: float32 [768, 2304], P(('dp', 'blk'))
- clipped_output: float32 [768, 768], P(('dp', 'blk'))
- clipped_expand: float32 [768, 3072], P(('dp', 'blk'))
- clipped_shrink: float32 [3072, 768], P(('dp', 'blk'))
- clipped_vectors: float32 [12, 768], P(None, ('dp', 'blk'))
- momentum_merged: float32 [768, 2304], P(('dp', 'blk'))
- momentum_output: float32 [768, 768], P(('dp', 'blk'))
- momentum_expand: float32 [768, 3072], P(('dp', 'blk'))
- momentum_shrink: float32 [3072, 768], P(('dp', 'blk'))
- momentum_vectors: float32 [12, 768], P(None, ('dp', 'blk'))
- variance_merged: float32 [768, 2304], P(('dp', 'blk'))
- variance_output: float32 [768, 768], P(('dp', 'blk'))
- variance_expand: float32 [768, 3072], P(('dp', 'blk'))
- variance_shrink: float32 [3072, 768], P(('dp', 'blk'))
- variance_vectors: float32 [12, 768], P(None, ('dp', 'blk'))
- updated_merged: float32 [768, 2304], P(('dp', 'blk'))
- updated_output: float32 [768, 768], P(('dp', 'blk'))
- updated_expand: float32 [768, 3072], P(('dp', 'blk'))
- updated_shrink: float32 [3072, 768], P(('dp', 'blk'))
- updated_vectors: float32 [12, 768], P(None, ('dp', 'blk'))
The draws below stay inside these ranges and needn't reach their ends.
Inputs may be any that keep to these rules, and one draw needn't show every extreme that they name: `kept_time`: 0 or 1; in every clip each aligned run of 12 time columns holds at least one 1. `kept_bands`: 0 or 1; every clip keeps at least one frequency row.
All inputs are finite; a program needn't handle non-finite values.
Results may differ from the reference program's by a relative error of at most 0.012.
The reference program's roundings to bfloat16 on the way count: a program that leaves them out, or rounds other values in their place, can miss the bound.
Values may be sent and summed in bfloat16 or wider, within the bound.
A program may use at most 320 MiB of HBM per device.

```python
import math
import jax
import jax.numpy as jnp
from jax import lax

D = 768
FF = 3072
HEADS = 12
HEAD_DIM = 64
FREQ = 10
TCOL = 12
STEP = 5
TIME = 48
SEQ = 488
CLIPS = 96
N_BLK = 4


def draw_kept_time(key, part):
    key = jax.random.fold_in(key, 11)
    rate_key, coin_key, pick_key = jax.random.split(key, 3)
    threshold = jax.random.randint(rate_key, (CLIPS, 1), 3, 9)
    coin_draws = jax.random.randint(coin_key, (CLIPS, TIME), 0, 8)
    chosen = jax.random.randint(pick_key, (CLIPS, TIME // TCOL, 1), 0, TCOL)
    forced = (jnp.arange(TCOL, dtype=jnp.int32)[None, None, :] == chosen).reshape(CLIPS, TIME)
    return jnp.where((coin_draws < threshold) | forced, 1, 0).astype(jnp.int32)


def draw_kept_bands(key, part):
    key = jax.random.fold_in(key, 23)
    rate_key, coin_key, pick_key = jax.random.split(key, 3)
    threshold = jax.random.randint(rate_key, (CLIPS, 1), 3, 9)
    coin_draws = jax.random.randint(coin_key, (CLIPS, FREQ), 0, 8)
    chosen = jax.random.randint(pick_key, (CLIPS, 1), 0, FREQ)
    forced = jnp.arange(FREQ, dtype=jnp.int32)[None, :] == chosen
    return jnp.where((coin_draws < threshold) | forced, 1, 0).astype(jnp.int32)


def draw_vectors(key, part):
    key = jax.random.fold_in(key, 37)
    jitter_key, shift_key = jax.random.split(key)
    ramp = jnp.arange(D, dtype=jnp.float32) / D
    rising = 0.5 + ramp
    shifts = 0.3 * jax.random.normal(shift_key, (8 + FF // D, D), jnp.float32)
    jitter = jnp.exp(jax.random.uniform(jitter_key, (2, D), jnp.float32, -0.2, 0.2))
    gains = rising[None, :] * jitter
    return jnp.concatenate([gains[0:1], shifts[1:5], gains[1:2], shifts[6:]], 0)


def shard_levels(key, shape, cuts, low, top_value):
    factor_of = 1.0
    for position, parts in cuts:
        heights = jax.random.uniform(jax.random.fold_in(jax.random.fold_in(key, 6), position), (parts,), jnp.float32, low / len(cuts), top_value / len(cuts))
        factor_of = factor_of * jnp.repeat(jnp.exp(heights), shape[position] // parts).reshape((-1,) + (1,) * (len(shape) - 1 - position))
    return factor_of


def gaussian(key, dims, scale, bound, pieces=(), held_as=jnp.bfloat16):
    level = shard_levels(key, dims, pieces, -0.22, 0.18) if pieces else 1.0
    array = jax.random.normal(key, dims, jnp.float32) * scale * level
    return jnp.minimum(jnp.maximum(array, -bound), bound).astype(held_as)


def setup_inputs(seed: int = 0) -> dict:
    seeds = jax.random.split(jax.random.key(seed), 20)
    return {
        "tokens": gaussian(seeds[0], (CLIPS, SEQ, D), 1.0, 6.0, ((0, 8), (1, 4)), jnp.float32),
        "kept_time": draw_kept_time(jax.random.fold_in(seeds[19], 71), 0),
        "kept_bands": draw_kept_bands(jax.random.fold_in(seeds[19], 71), 0),
        "cotangent": gaussian(seeds[3], (CLIPS, SEQ, D), 1.0, 6.0, ((0, 8), (1, 4)), jnp.float32),
        "weight_merged": gaussian(seeds[4], (D, 3 * D), D ** -0.5, 0.21875, ((0, 32),), jnp.float32),
        "weight_output": gaussian(seeds[5], (D, D), (D // 32) ** -0.5, 1.25, ((0, 32),), jnp.float32),
        "weight_expand": gaussian(seeds[6], (D, FF), D ** -0.5, 0.21875, ((0, 32),), jnp.float32),
        "weight_shrink": gaussian(seeds[7], (FF, D), FF ** -0.5, 0.109375, ((0, 32),), jnp.float32),
        "vectors": draw_vectors(jax.random.fold_in(seeds[19], 71), 0),
        "first_merged": gaussian(seeds[9], (D, 3 * D), (10 * (212 * D * FF + 304 * D * D) ** -0.5), 0.0024414062, ((0, 32),), jnp.float32),
        "first_output": gaussian(seeds[10], (D, D), (2 * (212 * D * FF + 304 * D * D) ** -0.5), 0.00048828125, ((0, 32),), jnp.float32),
        "first_expand": gaussian(seeds[11], (D, FF), (7 * (212 * D * FF + 304 * D * D) ** -0.5), 0.0017089844, ((0, 32),), jnp.float32),
        "first_shrink": gaussian(seeds[12], (FF, D), (13 * (212 * D * FF + 304 * D * D) ** -0.5), 0.0029296875, ((0, 32),), jnp.float32),
        "first_vectors": gaussian(seeds[13], (8 + FF // D, D), (20 * (212 * D * FF + 304 * D * D) ** -0.5), 0.0048828125, ((1, 32),), jnp.float32),
        "second_merged": jnp.clip(jnp.exp(math.log(5.886878398086992e-07) - 1.3862944 * jax.random.uniform(seeds[14], (D, 3 * D), jnp.float32) ** shard_levels(seeds[14], (D, 3 * D), ((0, 32),), -0.2, 0.2)), 1.471719599521748e-07, 5.886878398086992e-07),
        "second_output": jnp.clip(jnp.exp(math.log(2.3547514160782157e-08) - 1.3862944 * jax.random.uniform(seeds[15], (D, D), jnp.float32) ** shard_levels(seeds[15], (D, D), ((0, 32),), -0.2, 0.2)), 5.886878540195539e-09, 2.3547514160782157e-08),
        "second_expand": jnp.clip(jnp.exp(math.log(2.8845704491686774e-07) - 1.3862944 * jax.random.uniform(seeds[16], (D, FF), jnp.float32) ** shard_levels(seeds[16], (D, FF), ((0, 32),), -0.2, 0.2)), 7.211426122921694e-08, 2.8845704491686774e-07),
        "second_shrink": jnp.clip(jnp.exp(math.log(9.948824981620419e-07) - 1.3862944 * jax.random.uniform(seeds[17], (FF, D), jnp.float32) ** shard_levels(seeds[17], (FF, D), ((0, 32),), -0.2, 0.2)), 2.4872062454051047e-07, 9.948824981620419e-07),
        "second_vectors": jnp.clip(jnp.exp(math.log(2.354751359234797e-06) - 1.3862944 * jax.random.uniform(seeds[18], (8 + FF // D, D), jnp.float32) ** shard_levels(seeds[18], (8 + FF // D, D), ((1, 32),), -0.2, 0.2)), 5.886878398086992e-07, 2.354751359234797e-06),
    }


@jax.custom_vjp
def low(v):
    return lax.optimization_barrier(v.astype(jnp.bfloat16)).astype(jnp.float32)

@jax.custom_vjp
def low_back(v):
    return v

def low_keep(v):
    return (low(v), None)

def low_pass(kept, grad):
    return (grad,)

def back_keep(v):
    return (v, None)

def back_low(kept, grad):
    return (low(grad),)
low.defvjp(low_keep, low_pass)
low_back.defvjp(back_keep, back_low)
CLIP_LIMIT = 1.0
BETA_ONE = 0.5
BETA_TWO = 0.5
ADAM_EPS = 1e-08
MATRIX_RATE = 0.1
VECTOR_RATE = 0.3
MATRIX_DECAY = 0.05
HIGHEST = lax.Precision.HIGHEST

def layer_norm(values, scale_row, shift_row):
    centre = lax.optimization_barrier(jnp.mean(values, -1, keepdims=True))
    centred = values - centre
    spread = lax.optimization_barrier(jnp.mean(centred * centred, -1, keepdims=True))
    return centred * lax.rsqrt(spread + 1e-06) * scale_row + shift_row

def key_flags(kept_time, kept_bands, blocks):
    clip_count = kept_time.shape[0]
    columns = kept_time.shape[1] // blocks
    patches = kept_time.reshape(clip_count, blocks, columns, 1) * kept_bands[:, None, None, :]
    patches = patches.reshape(clip_count, blocks, columns * kept_bands.shape[1])
    leading = (jnp.arange(blocks, dtype=jnp.int32) == 0).astype(jnp.int32)
    special = jnp.broadcast_to(leading[None, :, None], (clip_count, blocks, 2))
    return jnp.concatenate([special, patches], 2).reshape(clip_count, -1)

def forward(weights_in, tokens_in, live_keys):
    merged, output, expand, shrink, params_vec = [low(weight) for weight in weights_in]
    clip_count, length, width = tokens_in.shape
    rows_in = tokens_in.reshape(clip_count * length, width)
    normed_one = low(layer_norm(rows_in, params_vec[0], params_vec[1]))
    qkv_bias = jnp.concatenate([params_vec[2], jnp.zeros_like(params_vec[2]), params_vec[3]])
    packed = low(low_back(jnp.dot(normed_one, merged, precision=HIGHEST) + qkv_bias))
    packed = packed.reshape(clip_count, length, 3, HEADS, HEAD_DIM)
    queries = packed[:, :, 0]
    keys_all = packed[:, :, 1]
    values_all = packed[:, :, 2]
    scores = jnp.einsum('cqhe,ckhe->chqk', queries, keys_all, precision=HIGHEST) * 0.125
    scores = low_back(scores + jnp.where(live_keys > 0, 0.0, -1e+30)[:, None, None, :])
    attention = low(jax.nn.softmax(scores, axis=-1))
    mixed = jnp.einsum('chqk,ckhe->cqhe', attention, values_all, precision=HIGHEST)
    mixed = low(low_back(mixed.reshape(clip_count * length, width)))
    middle = rows_in + low_back(jnp.dot(mixed, output, precision=HIGHEST) + params_vec[4])
    normed_two = low(layer_norm(middle, params_vec[5], params_vec[6]))
    hidden = low_back(jnp.dot(normed_two, expand, precision=HIGHEST) + params_vec[8:].reshape(-1))
    gelu_out = low(jax.nn.gelu(hidden, approximate=False))
    result = middle + low_back(jnp.dot(gelu_out, shrink, precision=HIGHEST) + params_vec[7])
    return result.reshape(clip_count, length, width)

def adamw(weight, first_old, second_old, grad_share, factor, step_rate, decay_rate):
    clipped = grad_share * factor
    momentum = BETA_ONE * first_old + (1.0 - BETA_ONE) * clipped
    variance = BETA_TWO * second_old + (1.0 - BETA_TWO) * clipped * clipped
    mean_hat = momentum / (1.0 - BETA_ONE ** STEP)
    var_hat = variance / (1.0 - BETA_TWO ** STEP)
    updated = weight - step_rate * (mean_hat / (jnp.sqrt(var_hat) + ADAM_EPS) + decay_rate * weight)
    return (clipped, momentum, variance, updated)

def reference(tokens, kept_time, kept_bands, cotangent, weight_merged, weight_output, weight_expand, weight_shrink, vectors, first_merged, first_output, first_expand, first_shrink, first_vectors, second_merged, second_output, second_expand, second_shrink, second_vectors):
    weights = (weight_merged, weight_output, weight_expand, weight_shrink, vectors)
    live_all = key_flags(kept_time, kept_bands, N_BLK)
    group_size = math.gcd(CLIPS, 8)
    passes = CLIPS // group_size
    shaped = (passes, group_size) + tokens.shape[1:]

    def one_pass(running, batch):
        part_tokens, part_live, part_cot = batch

        def apply_layer(weights_in, tokens_in):
            return forward(weights_in, tokens_in, part_live)
        result, pullback = jax.vjp(apply_layer, weights, part_tokens)
        d_weights, d_tokens = pullback(part_cot)
        return (jax.tree.map(jnp.add, running, d_weights), (result, d_tokens))
    start = jax.tree.map(jnp.zeros_like, weights)
    grads, (results, d_tokens) = lax.scan(one_pass, start, (tokens.reshape(shaped), live_all.reshape(passes, group_size, -1), cotangent.reshape(shaped)))
    total = sum((jnp.sum(grad_share * grad_share) for grad_share in grads))
    gradient_norm = jnp.sqrt(total)
    factor = CLIP_LIMIT / jnp.maximum(gradient_norm, CLIP_LIMIT)
    firsts = (first_merged, first_output, first_expand, first_shrink, first_vectors)
    seconds = (second_merged, second_output, second_expand, second_shrink, second_vectors)
    rates = (MATRIX_RATE, MATRIX_RATE, MATRIX_RATE, MATRIX_RATE, VECTOR_RATE)
    decays = (MATRIX_DECAY, MATRIX_DECAY, MATRIX_DECAY, MATRIX_DECAY, 0.0)
    steps_out = [adamw(weights[index], firsts[index], seconds[index], grads[index], factor, rates[index], decays[index]) for index in range(5)]
    return (results.reshape(tokens.shape), d_tokens.reshape(tokens.shape), gradient_norm, steps_out[0][0], steps_out[1][0], steps_out[2][0], steps_out[3][0], steps_out[4][0], steps_out[0][1], steps_out[1][1], steps_out[2][1], steps_out[3][1], steps_out[4][1], steps_out[0][2], steps_out[1][2], steps_out[2][2], steps_out[3][2], steps_out[4][2], steps_out[0][3], steps_out[1][3], steps_out[2][3], steps_out[3][3], steps_out[4][3])
```

```python
import functools
import jax
import jax.numpy as jnp
from jax import lax
from jax.experimental import pallas as pl
from jax.experimental.pallas import tpu as pltpu
from jax.sharding import PartitionSpec as P

HEADS = 12
STEP = 5
CLIP_LIMIT = 1.0
BETA_ONE = 0.5
BETA_TWO = 0.5
ADAM_EPS = 1e-08
MATRIX_RATE = 0.1
VECTOR_RATE = 0.3
MATRIX_DECAY = 0.05

F32, BF16 = jnp.float32, jnp.bfloat16
EPS = 1e-06
HALF = 64
LANES = 128
LIMIT = 60 * 1024 * 1024


def nn(a, b):
    return lax.dot_general(a, b, (((1,), (0,)), ((), ())), preferred_element_type=F32)


def nt(a, b):
    return lax.dot_general(a, b, (((1,), (1,)), ((), ())), preferred_element_type=F32)


def tn(a, b):
    return lax.dot_general(a, b, (((0,), (0,)), ((), ())), preferred_element_type=F32)


def norm_stats(v):
    centre = jnp.mean(v, -1, keepdims=True)
    c = v - centre
    spread = jnp.mean(c * c, -1, keepdims=True)
    r = lax.rsqrt(spread + EPS)
    return c * r, r


def norm_back(xhat, r, dy, gain):
    dx = dy * gain
    m1 = jnp.mean(dx, -1, keepdims=True)
    m2 = jnp.mean(dx * xhat, -1, keepdims=True)
    return (dx - m1 - xhat * m2) * r


def gelu_pair(x):
    z = jnp.abs(x)
    t = 1.0 / (1.0 + 0.3275911 * 0.7071067811865476 * z)
    e = jnp.exp(-0.5 * x * x)
    poly = t * (0.127414796 + t * (-0.142248368 + t * (0.7107068705 + t * (-0.7265760135 + t * 0.5307027145))))
    tail = poly * e
    phi = jnp.where(x >= 0, 1.0 - tail, tail)
    return x * phi, phi + (0.3989422804014327 * x) * e


def ffn_kernel(mid_ref, xc_ref, cot_ref, exp_ref, shr_ref, vec_ref,
               act_ref, dmid_ref, ge_ref, gs_ref, sums_ref,
               n2_s, y_s, dn_s, ae_s, as_s):
    f, i = pl.program_id(0), pl.program_id(1)
    nf, ni = pl.num_programs(0), pl.num_programs(1)
    rows = mid_ref.shape[0]
    here = pl.ds(pl.multiple_of(i * rows, rows), rows)

    @pl.when((f == 0) & (i == 0))
    def _():
        sums_ref[...] = jnp.zeros_like(sums_ref)

    @pl.when(f == 0)
    def _():
        xhat, _ = norm_stats(mid_ref[...])
        n2_s[here, :] = (xhat * vec_ref[5:6, :] + vec_ref[6:7, :]).astype(BF16)

    n2 = n2_s[here, :]
    d2 = cot_ref[...]
    h = nn(n2, exp_ref[...]) + vec_ref[pl.ds(8 + f, 1), :]
    dg = nt(d2, shr_ref[...])
    g, gp = gelu_pair(h)
    g = g.astype(BF16)
    dh32 = gp * dg
    dh = dh32.astype(BF16)
    sums_ref[pl.ds(8 + f, 1), :] += jnp.sum(dh32, 0, keepdims=True)
    y = nn(g, shr_ref[...])
    dn = nt(dh, exp_ref[...])
    ge = tn(n2, dh)
    gs = tn(g, d2)

    @pl.when(f == 0)
    def _():
        y_s[here, :] = y
        dn_s[here, :] = dn

    @pl.when(f > 0)
    def _():
        y_s[here, :] += y
        dn_s[here, :] += dn

    @pl.when(i == 0)
    def _():
        ae_s[...] = ge
        as_s[...] = gs

    @pl.when((i > 0) & (i < ni - 1))
    def _():
        ae_s[...] += ge
        as_s[...] += gs

    @pl.when(i == ni - 1)
    def _():
        ge_ref[...] = (ae_s[...] + ge).astype(ge_ref.dtype)
        gs_ref[...] = (as_s[...] + gs).astype(gs_ref.dtype)

    @pl.when(f == nf - 1)
    def _():
        mid = mid_ref[...]
        cot = d2.astype(F32)
        xhat, r = norm_stats(mid)
        dy = dn_s[here, :]
        act_ref[...] = ((mid - xc_ref[...].astype(F32)) + (y_s[here, :] + vec_ref[7:8, :])).astype(BF16)
        dmid_ref[...] = cot + norm_back(xhat, r, dy, vec_ref[5:6, :])
        sums_ref[5:6, :] += jnp.sum(dy * xhat, 0, keepdims=True)
        sums_ref[6:7, :] += jnp.sum(dy, 0, keepdims=True)
        sums_ref[7:8, :] += jnp.sum(cot, 0, keepdims=True)


def ffn(mid, xc, cot, expand, shrink, vec, rows):
    total, width = mid.shape
    ff = expand.shape[1] - width
    nf, ni = ff // width, total // rows
    first = lambda f, i: (jnp.where((f == 0) | (f == nf - 1), i, ni - 1), 0)
    last = lambda f, i: (jnp.where(f == nf - 1, i, 0), 0)
    return pl.pallas_call(
        ffn_kernel,
        grid=(nf, ni),
        in_specs=[
            pl.BlockSpec((rows, width), first),
            pl.BlockSpec((rows, width), last),
            pl.BlockSpec((rows, width), lambda f, i: (i, 0)),
            pl.BlockSpec((width, width), lambda f, i: (0, f + 1)),
            pl.BlockSpec((width, width), lambda f, i: (f, 0)),
            pl.BlockSpec(vec.shape, lambda f, i: (0, 0)),
        ],
        out_specs=[
            pl.BlockSpec((rows, width), last),
            pl.BlockSpec((rows, width), last),
            pl.BlockSpec((width, width), lambda f, i: (0, f)),
            pl.BlockSpec((width, width), lambda f, i: (f, 0)),
            pl.BlockSpec((16, width), lambda f, i: (0, 0)),
        ],
        out_shape=[
            jax.ShapeDtypeStruct((total, width), BF16),
            jax.ShapeDtypeStruct((total, width), F32),
            jax.ShapeDtypeStruct((width, ff), BF16),
            jax.ShapeDtypeStruct((ff, width), BF16),
            jax.ShapeDtypeStruct((16, width), F32),
        ],
        scratch_shapes=[
            pltpu.VMEM((total, width), BF16),
            pltpu.VMEM((total, width), F32),
            pltpu.VMEM((total, width), F32),
            pltpu.VMEM((width, width), F32),
            pltpu.VMEM((width, width), F32),
        ],
        compiler_params=pltpu.CompilerParams(
            dimension_semantics=("arbitrary", "arbitrary"), vmem_limit_bytes=LIMIT),
        name="ffn",
    )(mid, xc, cot, expand, shrink, vec)


def attn_fwd_kernel(heads, xc_ref, dead_ref, mrg_ref, out_ref, vec_ref,
                    n1_ref, qa_ref, kv_ref, mix_ref, mid_ref, pk_s):
    width = xc_ref.shape[1]
    seq = xc_ref.shape[0]
    pairs = heads // 2
    xc = xc_ref[...].astype(F32)
    xhat, _ = norm_stats(xc)
    n1 = (xhat * vec_ref[0:1, :] + vec_ref[1:2, :]).astype(BF16)
    n1_ref[...] = n1
    for third in range(3):
        cols = pl.ds(third * width, width)
        part = nn(n1, mrg_ref[:, cols])
        if third != 1:
            part = part + vec_ref[2 + third // 2:3 + third // 2, :]
        part = part.astype(BF16)
        pk_s[:, cols] = part
        if third:
            kv_ref[:, pl.ds((third - 1) * width, width)] = part
    lane = lax.broadcasted_iota(jnp.int32, (seq, LANES), 1)
    low = lane < HALF
    in_half = lane % HALF
    dead = dead_ref[...]
    ones = jnp.ones((seq, LANES), BF16)

    def pair(p, _):
        qcols = pl.ds(pl.multiple_of(p * LANES, LANES), LANES)
        kcols = pl.ds(pl.multiple_of(width + p * LANES, LANES), LANES)
        vcols = pl.ds(pl.multiple_of(2 * width + p * LANES, LANES), LANES)
        q = pk_s[:, qcols] * jnp.array(0.125, BF16)
        k = pk_s[:, kcols]
        v = pk_s[:, vcols]
        outs = []
        for side in range(2):
            mine = low if side == 0 else ~low
            qs = jnp.where(mine, q, jnp.where(in_half == 0, 1.0, 0.0).astype(BF16))
            ks = jnp.where(mine, k, dead)
            vs = jnp.where(mine, v, ones)
            s = nt(qs, ks)
            top = jnp.max(s, -1, keepdims=True)
            e = jnp.exp(s - top).astype(BF16)
            o = nn(e, vs)
            swapped = pltpu.roll(o, HALF, 1)
            outs.append(o / swapped)
            lse = top + jnp.log(jnp.where(mine, swapped, o))
            hi = (-lse).astype(BF16)
            rest = -lse - hi.astype(F32)
            mid_part = rest.astype(BF16)
            lo = (rest - mid_part.astype(F32)).astype(BF16)
            extra = jnp.where(in_half == 0, 1.0, 0.0).astype(BF16)
            extra = jnp.where(in_half == 1, hi, extra)
            extra = jnp.where(in_half == 2, mid_part, extra)
            extra = jnp.where(in_half == 3, lo, extra)
            qa_ref[2 * p + side] = jnp.where(mine, q, extra)
        mix_ref[:, qcols] = jnp.where(low, outs[0], outs[1]).astype(BF16)
        return 0

    lax.fori_loop(0, pairs, pair, 0)
    mid_ref[...] = xc + nn(mix_ref[...], out_ref[...]) + vec_ref[4:5, :]


def attn_fwd(xc, dead, merged, output, vec, clips, heads):
    total, width = xc.shape
    seq = total // clips
    whole = lambda c: (0, 0)
    row = lambda c: (c, 0)
    return pl.pallas_call(
        functools.partial(attn_fwd_kernel, heads),
        grid=(clips,),
        in_specs=[
            pl.BlockSpec((seq, width), row),
            pl.BlockSpec((seq, LANES), row),
            pl.BlockSpec(merged.shape, whole),
            pl.BlockSpec((width, width), whole),
            pl.BlockSpec(vec.shape, whole),
        ],
        out_specs=[
            pl.BlockSpec((seq, width), row),
            pl.BlockSpec((heads, seq, LANES), lambda c: (0, c, 0)),
            pl.BlockSpec((seq, 2 * width), row),
            pl.BlockSpec((seq, width), row),
            pl.BlockSpec((seq, width), row),
        ],
        out_shape=[
            jax.ShapeDtypeStruct((total, width), BF16),
            jax.ShapeDtypeStruct((heads, total, LANES), BF16),
            jax.ShapeDtypeStruct((total, 2 * width), BF16),
            jax.ShapeDtypeStruct((total, width), BF16),
            jax.ShapeDtypeStruct((total, width), F32),
        ],
        scratch_shapes=[pltpu.VMEM((seq, 3 * width), BF16)],
        compiler_params=pltpu.CompilerParams(
            dimension_semantics=("arbitrary",), vmem_limit_bytes=LIMIT),
        name="attn_fwd",
    )(xc, dead, merged, output, vec)


def attn_bwd_kernel(heads, xc_ref, cot_ref, dmid_ref, dead_ref, n1_ref, qa_ref, kv_ref, mix_ref,
                    mrg_ref, out_ref, vec_ref, early_ref,
                    dlt_ref, gm_ref, go_ref,
                    dm_s, dp_s, am_s, ao_s, sums_ref):
    c = pl.program_id(0)
    n = pl.num_programs(0)
    seq, width = xc_ref.shape
    pairs = heads // 2

    @pl.when(c == 0)
    def _():
        sums_ref[...] = early_ref[...]
        am_s[...] = jnp.zeros_like(am_s)
        ao_s[...] = jnp.zeros_like(ao_s)

    d_one = dmid_ref[...].astype(BF16)
    dm_s[...] = nt(d_one, out_ref[...]).astype(BF16)
    ao_s[...] += tn(mix_ref[...], d_one)
    sums_ref[4:5, :] += jnp.sum(d_one.astype(F32), 0, keepdims=True)

    lane = lax.broadcasted_iota(jnp.int32, (seq, LANES), 1)
    low = lane < HALF
    in_half = lane % HALF
    dead = dead_ref[...]
    vone = jnp.where(in_half < 2, 1.0, 0.0).astype(BF16)

    def pair(p, _):
        qcols = pl.ds(pl.multiple_of(p * LANES, LANES), LANES)
        kcols = pl.ds(pl.multiple_of(width + p * LANES, LANES), LANES)
        vcols = pl.ds(pl.multiple_of(2 * width + p * LANES, LANES), LANES)
        k = kv_ref[:, qcols]
        v = kv_ref[:, kcols]
        dm = dm_s[:, qcols]
        prod = dm.astype(F32) * mix_ref[:, qcols].astype(F32)
        k_t = jnp.transpose(k)
        dks, dvs, dqs = [], [], []
        for side in range(2):
            mine = low if side == 0 else ~low
            qa = qa_ref[2 * p + side]
            ka = jnp.where(mine, k, dead)
            va = jnp.where(mine, v, vone)
            dd = -jnp.sum(jnp.where(mine, prod, 0.0), -1, keepdims=True)
            hi = dd.astype(BF16)
            lo = (dd - hi.astype(F32)).astype(BF16)
            da = jnp.where(mine, dm, jnp.where(in_half == 0, hi, lo))
            p_t = jnp.exp(nt(ka, qa))
            ds_t = (p_t * nt(va, da)).astype(BF16)
            dvs.append(nn(p_t.astype(BF16), da))
            dks.append(nn(ds_t, qa))
            dqs.append(nn(k_t[side * HALF:(side + 1) * HALF, :], ds_t))
        dq = jnp.transpose(jnp.concatenate(dqs, 0)) * 0.125
        dk = jnp.where(low, dks[0], dks[1])
        dv = jnp.where(low, dvs[0], dvs[1])
        sums_ref[2:3, qcols] += jnp.sum(dq, 0, keepdims=True)
        sums_ref[3:4, qcols] += jnp.sum(dv, 0, keepdims=True)
        dp_s[:, qcols] = dq.astype(BF16)
        dp_s[:, kcols] = dk.astype(BF16)
        dp_s[:, vcols] = dv.astype(BF16)
        return 0

    lax.fori_loop(0, pairs, pair, 0)
    dp = dp_s[...]
    am_s[...] += tn(n1_ref[...], dp)
    dy = nt(dp, mrg_ref[:, :3 * width])
    xhat, r = norm_stats(xc_ref[...].astype(F32))
    sums_ref[0:1, :] += jnp.sum(dy * xhat, 0, keepdims=True)
    sums_ref[1:2, :] += jnp.sum(dy, 0, keepdims=True)
    dlt_ref[...] = ((dmid_ref[...] - cot_ref[...].astype(F32))
                    + norm_back(xhat, r, dy, vec_ref[0:1, :])).astype(BF16)

    @pl.when(c == n - 1)
    def _():
        gm_ref[:, :3 * width] = am_s[...].astype(gm_ref.dtype)
        columns = jnp.transpose(sums_ref[...])
        gm_ref[:, 3 * width:] = jnp.concatenate(
            [columns, jnp.zeros((width, LANES - columns.shape[1]), F32)], 1).astype(gm_ref.dtype)
        go_ref[...] = ao_s[...].astype(go_ref.dtype)


def attn_bwd(xc, cot, dmid, dead, n1, qa, kv, mix, merged, output, vec, early, clips, heads):
    total, width = xc.shape
    seq = total // clips
    whole = lambda c: (0, 0)
    row = lambda c: (c, 0)
    return pl.pallas_call(
        functools.partial(attn_bwd_kernel, heads),
        grid=(clips,),
        in_specs=[
            pl.BlockSpec((seq, width), row),
            pl.BlockSpec((seq, width), row),
            pl.BlockSpec((seq, width), row),
            pl.BlockSpec((seq, LANES), row),
            pl.BlockSpec((seq, width), row),
            pl.BlockSpec((heads, seq, LANES), lambda c: (0, c, 0)),
            pl.BlockSpec((seq, 2 * width), row),
            pl.BlockSpec((seq, width), row),
            pl.BlockSpec(merged.shape, whole),
            pl.BlockSpec((width, width), whole),
            pl.BlockSpec(vec.shape, whole),
            pl.BlockSpec(early.shape, whole),
        ],
        out_specs=[
            pl.BlockSpec((seq, width), row),
            pl.BlockSpec(merged.shape, whole),
            pl.BlockSpec((width, width), whole),
        ],
        out_shape=[
            jax.ShapeDtypeStruct((total, width), BF16),
            jax.ShapeDtypeStruct(merged.shape, BF16),
            jax.ShapeDtypeStruct((width, width), BF16),
        ],
        scratch_shapes=[
            pltpu.VMEM((seq, width), BF16),
            pltpu.VMEM((seq, 3 * width), BF16),
            pltpu.VMEM((width, 3 * width), F32),
            pltpu.VMEM((width, width), F32),
            pltpu.VMEM((16, width), F32),
        ],
        compiler_params=pltpu.CompilerParams(
            dimension_semantics=("arbitrary",), vmem_limit_bytes=LIMIT),
        name="attn_bwd",
    )(xc, cot, dmid, dead, n1, qa, kv, mix, merged, output, vec, early)


def adamw(weight, first_old, second_old, grad_share, factor, step_rate, decay_rate):
    clipped = grad_share * factor
    momentum = BETA_ONE * first_old + (1.0 - BETA_ONE) * clipped
    variance = BETA_TWO * second_old + (1.0 - BETA_TWO) * clipped * clipped
    mean_hat = momentum / (1.0 - BETA_ONE**STEP)
    var_hat = variance / (1.0 - BETA_TWO**STEP)
    updated = weight - step_rate * (mean_hat / (jnp.sqrt(var_hat) + ADAM_EPS) + decay_rate * weight)
    return (clipped, momentum, variance, updated)


def key_columns(kept_time, kept_bands, blocks, own, segment, padded):
    clips = kept_time.shape[0] // blocks
    kept_time = lax.dynamic_slice_in_dim(kept_time, own * clips, clips)
    kept_bands = lax.dynamic_slice_in_dim(kept_bands, own * clips, clips)
    columns = kept_time.shape[1] // blocks
    patches = kept_time.reshape(clips, blocks, columns, 1) * kept_bands[:, None, None, :]
    patches = patches.reshape(clips, blocks, columns * kept_bands.shape[1])
    leading = (jnp.arange(blocks, dtype=jnp.int32) == 0).astype(jnp.int32)
    special = jnp.broadcast_to(leading[None, :, None], (clips, blocks, segment - patches.shape[2]))
    live = jnp.concatenate([special, patches, jnp.zeros((clips, blocks, padded - segment), jnp.int32)], 2)
    bias = jnp.where(live > 0, 0.0, -1e30).reshape(-1, 1)
    lane = jnp.arange(LANES, dtype=jnp.int32)[None, :] % HALF
    return jnp.where(lane == 0, bias, jnp.where(lane < 4, 1.0, 0.0)).astype(BF16)


def shards(
    tokens, kept_time, kept_bands, cotangent,
    weight_merged, weight_output, weight_expand, weight_shrink, vectors,
    first_merged, first_output, first_expand, first_shrink, first_vectors,
    second_merged, second_output, second_expand, second_shrink, second_vectors,
):
    clip_count, segment, width = tokens.shape
    blocks = lax.axis_size("blk")
    own = lax.axis_index("blk")
    clips = clip_count // blocks
    padded = -(-segment // 16) * 16
    total = clips * blocks * padded
    axes = ("dp", "blk")

    def to_clips(values):
        values = jnp.pad(values.astype(BF16), ((0, 0), (0, padded - segment), (0, 0)))
        return lax.all_to_all(values, "blk", 0, 1, tiled=True).reshape(total, width)

    def to_home(values):
        values = values.reshape(clips, blocks * padded, width)
        return lax.all_to_all(values, "blk", 1, 0, tiled=True)[:, :segment].astype(F32)

    columns = jnp.pad(vectors.T, ((0, 0), (0, LANES - vectors.shape[0])))
    merged = lax.all_gather(
        jnp.concatenate([weight_merged, columns], 1).astype(BF16), axes, axis=0, tiled=True)
    wide = lax.all_gather(
        jnp.concatenate([weight_output, weight_expand], 1).astype(BF16), axes, axis=0, tiled=True)
    shrink = lax.all_gather(weight_shrink.astype(BF16), axes, axis=0, tiled=True)
    vec = merged[:, 3 * width:3 * width + vectors.shape[0]].T.astype(F32)
    xc = to_clips(tokens - jnp.mean(tokens, -1, keepdims=True))
    cot = to_clips(cotangent)
    dead = key_columns(kept_time, kept_bands, blocks, own, segment, padded)
    n1, qa, kv, mix, mid = attn_fwd(xc, dead, merged, wide, vec, clips, HEADS)
    act, dmid, grad_expand, grad_shrink, early = ffn(mid, xc, cot, wide, shrink, vec, blocks * padded)
    dlt, grad_merged, grad_output = attn_bwd(
        xc, cot, dmid, dead, n1, qa, kv, mix, merged, wide, vec, early, clips, HEADS)
    activations = tokens + to_home(act)
    token_grads = cotangent + to_home(dlt)
    scattered = [
        lax.psum_scatter(grad, axes, scatter_dimension=0, tiled=True).astype(F32)
        for grad in (grad_merged, grad_output, grad_expand, grad_shrink)
    ]
    shares = (
        scattered[0][:, :3 * width], scattered[1], scattered[2], scattered[3],
        scattered[0][:, 3 * width:3 * width + vectors.shape[0]].T,
    )
    squares = sum(jnp.sum(share_part * share_part) for share_part in shares)
    gradient_norm = jnp.sqrt(lax.psum(squares, axes))
    factor = CLIP_LIMIT / jnp.maximum(gradient_norm, CLIP_LIMIT)
    weights = (weight_merged, weight_output, weight_expand, weight_shrink, vectors)
    firsts = (first_merged, first_output, first_expand, first_shrink, first_vectors)
    seconds = (second_merged, second_output, second_expand, second_shrink, second_vectors)
    rates = (MATRIX_RATE, MATRIX_RATE, MATRIX_RATE, MATRIX_RATE, VECTOR_RATE)
    decays = (MATRIX_DECAY, MATRIX_DECAY, MATRIX_DECAY, MATRIX_DECAY, 0.0)
    steps_out = [
        adamw(*parts, factor, rate, decay)
        for *parts, rate, decay in zip(weights, firsts, seconds, shares, rates, decays)
    ]
    return (activations, token_grads, gradient_norm) + tuple(
        steps_out[index][kind] for kind in range(4) for index in range(5))


def solution(mesh):
    return jax.shard_map(
        shards,
        mesh=mesh,
        in_specs=(
            P("dp", "blk", None),
            P("dp", None),
            P("dp", None),
            P("dp", "blk", None),
            P(("dp", "blk"), None),
            P(("dp", "blk"), None),
            P(("dp", "blk"), None),
            P(("dp", "blk"), None),
            P(None, ("dp", "blk")),
            P(("dp", "blk"), None),
            P(("dp", "blk"), None),
            P(("dp", "blk"), None),
            P(("dp", "blk"), None),
            P(None, ("dp", "blk")),
            P(("dp", "blk"), None),
            P(("dp", "blk"), None),
            P(("dp", "blk"), None),
            P(("dp", "blk"), None),
            P(None, ("dp", "blk")),
        ),
        out_specs=(
            P("dp", "blk", None),
            P("dp", "blk", None),
            P(),
            P(("dp", "blk"), None),
            P(("dp", "blk"), None),
            P(("dp", "blk"), None),
            P(("dp", "blk"), None),
            P(None, ("dp", "blk")),
            P(("dp", "blk"), None),
            P(("dp", "blk"), None),
            P(("dp", "blk"), None),
            P(("dp", "blk"), None),
            P(None, ("dp", "blk")),
            P(("dp", "blk"), None),
            P(("dp", "blk"), None),
            P(("dp", "blk"), None),
            P(("dp", "blk"), None),
            P(None, ("dp", "blk")),
            P(("dp", "blk"), None),
            P(("dp", "blk"), None),
            P(("dp", "blk"), None),
            P(("dp", "blk"), None),
            P(None, ("dp", "blk")),
        ),
        check_vma=False,
    )
```

```python
import functools
import jax
import jax.numpy as jnp
from jax import lax
from jax.experimental import pallas as pl
from jax.experimental.pallas import tpu as pltpu
from jax.sharding import PartitionSpec as P

HEADS = 12
STEP = 5
CLIP_LIMIT = 1.0
BETA_ONE = 0.5
BETA_TWO = 0.5
ADAM_EPS = 1e-08
MATRIX_RATE = 0.1
VECTOR_RATE = 0.3
MATRIX_DECAY = 0.05

F32, BF16 = jnp.float32, jnp.bfloat16
EPS = 1e-06
HALF = 64
LANES = 128
LIMIT = 60 * 1024 * 1024
MESH = pl.DeviceIdType.MESH


def nn(a, b):
    return lax.dot_general(a, b, (((1,), (0,)), ((), ())), preferred_element_type=F32)


def nt(a, b):
    return lax.dot_general(a, b, (((1,), (1,)), ((), ())), preferred_element_type=F32)


def tn(a, b):
    return lax.dot_general(a, b, (((0,), (0,)), ((), ())), preferred_element_type=F32)


def norm_stats(v):
    centre = jnp.mean(v, -1, keepdims=True)
    c = v - centre
    spread = jnp.mean(c * c, -1, keepdims=True)
    r = lax.rsqrt(spread + EPS)
    return c * r, r


def norm_back(xhat, r, dy, gain):
    dx = dy * gain
    m1 = jnp.mean(dx, -1, keepdims=True)
    m2 = jnp.mean(dx * xhat, -1, keepdims=True)
    return (dx - m1 - xhat * m2) * r


def gelu_pair(x):
    z = jnp.abs(x)
    t = 1.0 / (1.0 + 0.3275911 * 0.7071067811865476 * z)
    e = jnp.exp(-0.5 * x * x)
    poly = t * (0.127414796 + t * (-0.142248368 + t * (0.7107068705 + t * (-0.7265760135 + t * 0.5307027145))))
    tail = poly * e
    phi = jnp.where(x >= 0, 1.0 - tail, tail)
    return x * phi, phi + (0.3989422804014327 * x) * e


def ffn_kernel(mid_ref, xc_ref, cot_ref, exp_ref, shr_ref, vec_ref,
               act_ref, dmid_ref, ge_ref, gs_ref, sums_ref,
               n2_s, y_s, dn_s, ae_s, as_s):
    f, i = pl.program_id(0), pl.program_id(1)
    nf, ni = pl.num_programs(0), pl.num_programs(1)
    rows = mid_ref.shape[0]
    here = pl.ds(pl.multiple_of(i * rows, rows), rows)

    @pl.when((f == 0) & (i == 0))
    def _():
        sums_ref[...] = jnp.zeros_like(sums_ref)

    @pl.when(f == 0)
    def _():
        xhat, _ = norm_stats(mid_ref[...])
        n2_s[here, :] = (xhat * vec_ref[5:6, :] + vec_ref[6:7, :]).astype(BF16)

    n2 = n2_s[here, :]
    d2 = cot_ref[...]
    h = nn(n2, exp_ref[...]) + vec_ref[pl.ds(8 + f, 1), :]
    dg = nt(d2, shr_ref[...])
    g, gp = gelu_pair(h)
    g = g.astype(BF16)
    dh32 = gp * dg
    dh = dh32.astype(BF16)
    sums_ref[pl.ds(8 + f, 1), :] += jnp.sum(dh32, 0, keepdims=True)
    y = nn(g, shr_ref[...])
    dn = nt(dh, exp_ref[...])
    ge = tn(n2, dh)
    gs = tn(g, d2)

    @pl.when(f == 0)
    def _():
        y_s[here, :] = y
        dn_s[here, :] = dn

    @pl.when(f > 0)
    def _():
        y_s[here, :] += y
        dn_s[here, :] += dn

    @pl.when(i == 0)
    def _():
        ae_s[...] = ge
        as_s[...] = gs

    @pl.when((i > 0) & (i < ni - 1))
    def _():
        ae_s[...] += ge
        as_s[...] += gs

    @pl.when(i == ni - 1)
    def _():
        ge_ref[...] = (ae_s[...] + ge).astype(ge_ref.dtype)
        gs_ref[...] = (as_s[...] + gs).astype(gs_ref.dtype)

    @pl.when(f == nf - 1)
    def _():
        mid = mid_ref[...]
        cot = d2.astype(F32)
        xhat, r = norm_stats(mid)
        dy = dn_s[here, :]
        act_ref[...] = ((mid - xc_ref[...].astype(F32)) + (y_s[here, :] + vec_ref[7:8, :])).astype(BF16)
        dmid_ref[...] = cot + norm_back(xhat, r, dy, vec_ref[5:6, :])
        sums_ref[5:6, :] += jnp.sum(dy * xhat, 0, keepdims=True)
        sums_ref[6:7, :] += jnp.sum(dy, 0, keepdims=True)
        sums_ref[7:8, :] += jnp.sum(cot, 0, keepdims=True)


def ffn(mid, xc, cot, expand, shrink, vec, rows):
    total, width = mid.shape
    ff = expand.shape[1] - width
    nf, ni = ff // width, total // rows
    first = lambda f, i: (jnp.where((f == 0) | (f == nf - 1), i, ni - 1), 0)
    last = lambda f, i: (jnp.where(f == nf - 1, i, 0), 0)
    return pl.pallas_call(
        ffn_kernel,
        grid=(nf, ni),
        in_specs=[
            pl.BlockSpec((rows, width), first),
            pl.BlockSpec((rows, width), last),
            pl.BlockSpec((rows, width), lambda f, i: (i, 0)),
            pl.BlockSpec((width, width), lambda f, i: (0, f + 1)),
            pl.BlockSpec((width, width), lambda f, i: (f, 0)),
            pl.BlockSpec(vec.shape, lambda f, i: (0, 0)),
        ],
        out_specs=[
            pl.BlockSpec((rows, width), last),
            pl.BlockSpec((rows, width), last),
            pl.BlockSpec((width, width), lambda f, i: (0, f)),
            pl.BlockSpec((width, width), lambda f, i: (f, 0)),
            pl.BlockSpec((16, width), lambda f, i: (0, 0)),
        ],
        out_shape=[
            jax.ShapeDtypeStruct((total, width), BF16),
            jax.ShapeDtypeStruct((total, width), F32),
            jax.ShapeDtypeStruct((width, ff), BF16),
            jax.ShapeDtypeStruct((ff, width), BF16),
            jax.ShapeDtypeStruct((16, width), F32),
        ],
        scratch_shapes=[
            pltpu.VMEM((total, width), BF16),
            pltpu.VMEM((total, width), F32),
            pltpu.VMEM((total, width), F32),
            pltpu.VMEM((width, width), F32),
            pltpu.VMEM((width, width), F32),
        ],
        compiler_params=pltpu.CompilerParams(
            dimension_semantics=("arbitrary", "arbitrary"), vmem_limit_bytes=LIMIT),
        name="ffn",
    )(mid, xc, cot, expand, shrink, vec)


def attn_fwd_kernel(heads, xc_ref, dead_ref, mrg_ref, out_ref, vec_ref,
                    n1_ref, qa_ref, kv_ref, mix_ref, mid_ref, pk_s):
    width = xc_ref.shape[1]
    seq = xc_ref.shape[0]
    pairs = heads // 2
    xc = xc_ref[...].astype(F32)
    xhat, _ = norm_stats(xc)
    n1 = (xhat * vec_ref[0:1, :] + vec_ref[1:2, :]).astype(BF16)
    n1_ref[...] = n1
    for third in range(3):
        cols = pl.ds(third * width, width)
        part = nn(n1, mrg_ref[:, cols])
        if third != 1:
            part = part + vec_ref[2 + third // 2:3 + third // 2, :]
        part = part.astype(BF16)
        pk_s[:, cols] = part
        if third:
            kv_ref[:, pl.ds((third - 1) * width, width)] = part
    lane = lax.broadcasted_iota(jnp.int32, (seq, LANES), 1)
    low = lane < HALF
    in_half = lane % HALF
    dead = dead_ref[...]
    ones = jnp.ones((seq, LANES), BF16)

    def pair(p, _):
        qcols = pl.ds(pl.multiple_of(p * LANES, LANES), LANES)
        kcols = pl.ds(pl.multiple_of(width + p * LANES, LANES), LANES)
        vcols = pl.ds(pl.multiple_of(2 * width + p * LANES, LANES), LANES)
        q = pk_s[:, qcols] * jnp.array(0.125, BF16)
        k = pk_s[:, kcols]
        v = pk_s[:, vcols]
        outs = []
        for side in range(2):
            mine = low if side == 0 else ~low
            qs = jnp.where(mine, q, jnp.where(in_half == 0, 1.0, 0.0).astype(BF16))
            ks = jnp.where(mine, k, dead)
            vs = jnp.where(mine, v, ones)
            s = nt(qs, ks)
            top = jnp.max(s, -1, keepdims=True)
            e = jnp.exp(s - top).astype(BF16)
            o = nn(e, vs)
            swapped = pltpu.roll(o, HALF, 1)
            outs.append(o / swapped)
            lse = top + jnp.log(jnp.where(mine, swapped, o))
            hi = (-lse).astype(BF16)
            rest = -lse - hi.astype(F32)
            mid_part = rest.astype(BF16)
            lo = (rest - mid_part.astype(F32)).astype(BF16)
            extra = jnp.where(in_half == 0, 1.0, 0.0).astype(BF16)
            extra = jnp.where(in_half == 1, hi, extra)
            extra = jnp.where(in_half == 2, mid_part, extra)
            extra = jnp.where(in_half == 3, lo, extra)
            qa_ref[2 * p + side] = jnp.where(mine, q, extra)
        mix_ref[:, qcols] = jnp.where(low, outs[0], outs[1]).astype(BF16)
        return 0

    lax.fori_loop(0, pairs, pair, 0)
    mid_ref[...] = xc + nn(mix_ref[...], out_ref[...]) + vec_ref[4:5, :]


def attn_fwd(xc, dead, merged, output, vec, clips, heads):
    total, width = xc.shape
    seq = total // clips
    whole = lambda c: (0, 0)
    row = lambda c: (c, 0)
    return pl.pallas_call(
        functools.partial(attn_fwd_kernel, heads),
        grid=(clips,),
        in_specs=[
            pl.BlockSpec((seq, width), row),
            pl.BlockSpec((seq, LANES), row),
            pl.BlockSpec(merged.shape, whole),
            pl.BlockSpec((width, width), whole),
            pl.BlockSpec(vec.shape, whole),
        ],
        out_specs=[
            pl.BlockSpec((seq, width), row),
            pl.BlockSpec((heads, seq, LANES), lambda c: (0, c, 0)),
            pl.BlockSpec((seq, 2 * width), row),
            pl.BlockSpec((seq, width), row),
            pl.BlockSpec((seq, width), row),
        ],
        out_shape=[
            jax.ShapeDtypeStruct((total, width), BF16),
            jax.ShapeDtypeStruct((heads, total, LANES), BF16),
            jax.ShapeDtypeStruct((total, 2 * width), BF16),
            jax.ShapeDtypeStruct((total, width), BF16),
            jax.ShapeDtypeStruct((total, width), F32),
        ],
        scratch_shapes=[pltpu.VMEM((seq, 3 * width), BF16)],
        compiler_params=pltpu.CompilerParams(
            dimension_semantics=("arbitrary",), vmem_limit_bytes=LIMIT),
        name="attn_fwd",
    )(xc, dead, merged, output, vec)


def attn_bwd_kernel(heads, xc_ref, cot_ref, dmid_ref, dead_ref, n1_ref, qa_ref, kv_ref, mix_ref,
                    mrg_ref, out_ref, vec_ref, early_ref,
                    dlt_ref, gm_ref, go_ref,
                    dm_s, dp_s, am_s, ao_s, sums_ref):
    c = pl.program_id(0)
    n = pl.num_programs(0)
    seq, width = xc_ref.shape
    pairs = heads // 2

    @pl.when(c == 0)
    def _():
        sums_ref[...] = early_ref[...]
        am_s[...] = jnp.zeros_like(am_s)
        ao_s[...] = jnp.zeros_like(ao_s)

    d_one = dmid_ref[...].astype(BF16)
    dm_s[...] = nt(d_one, out_ref[...]).astype(BF16)
    ao_s[...] += tn(mix_ref[...], d_one)
    sums_ref[4:5, :] += jnp.sum(d_one.astype(F32), 0, keepdims=True)

    lane = lax.broadcasted_iota(jnp.int32, (seq, LANES), 1)
    low = lane < HALF
    in_half = lane % HALF
    dead = dead_ref[...]
    vone = jnp.where(in_half < 2, 1.0, 0.0).astype(BF16)

    def pair(p, _):
        qcols = pl.ds(pl.multiple_of(p * LANES, LANES), LANES)
        kcols = pl.ds(pl.multiple_of(width + p * LANES, LANES), LANES)
        vcols = pl.ds(pl.multiple_of(2 * width + p * LANES, LANES), LANES)
        k = kv_ref[:, qcols]
        v = kv_ref[:, kcols]
        dm = dm_s[:, qcols]
        prod = dm.astype(F32) * mix_ref[:, qcols].astype(F32)
        k_t = jnp.transpose(k)
        dks, dvs, dqs = [], [], []
        for side in range(2):
            mine = low if side == 0 else ~low
            qa = qa_ref[2 * p + side]
            ka = jnp.where(mine, k, dead)
            va = jnp.where(mine, v, vone)
            dd = -jnp.sum(jnp.where(mine, prod, 0.0), -1, keepdims=True)
            hi = dd.astype(BF16)
            lo = (dd - hi.astype(F32)).astype(BF16)
            da = jnp.where(mine, dm, jnp.where(in_half == 0, hi, lo))
            p_t = jnp.exp(nt(ka, qa))
            ds_t = (p_t * nt(va, da)).astype(BF16)
            dvs.append(nn(p_t.astype(BF16), da))
            dks.append(nn(ds_t, qa))
            dqs.append(nn(k_t[side * HALF:(side + 1) * HALF, :], ds_t))
        dq = jnp.transpose(jnp.concatenate(dqs, 0)) * 0.125
        dk = jnp.where(low, dks[0], dks[1])
        dv = jnp.where(low, dvs[0], dvs[1])
        sums_ref[2:3, qcols] += jnp.sum(dq, 0, keepdims=True)
        sums_ref[3:4, qcols] += jnp.sum(dv, 0, keepdims=True)
        dp_s[:, qcols] = dq.astype(BF16)
        dp_s[:, kcols] = dk.astype(BF16)
        dp_s[:, vcols] = dv.astype(BF16)
        return 0

    lax.fori_loop(0, pairs, pair, 0)
    dp = dp_s[...]
    am_s[...] += tn(n1_ref[...], dp)
    dy = nt(dp, mrg_ref[:, :3 * width])
    xhat, r = norm_stats(xc_ref[...].astype(F32))
    sums_ref[0:1, :] += jnp.sum(dy * xhat, 0, keepdims=True)
    sums_ref[1:2, :] += jnp.sum(dy, 0, keepdims=True)
    dlt_ref[...] = ((dmid_ref[...] - cot_ref[...].astype(F32))
                    + norm_back(xhat, r, dy, vec_ref[0:1, :])).astype(BF16)

    @pl.when(c == n - 1)
    def _():
        gm_ref[:, :3 * width] = am_s[...].astype(gm_ref.dtype)
        columns = jnp.transpose(sums_ref[...])
        gm_ref[:, 3 * width:] = jnp.concatenate(
            [columns, jnp.zeros((width, LANES - columns.shape[1]), F32)], 1).astype(gm_ref.dtype)
        go_ref[...] = ao_s[...].astype(go_ref.dtype)


def attn_bwd(xc, cot, dmid, dead, n1, qa, kv, mix, merged, output, vec, early, clips, heads):
    total, width = xc.shape
    seq = total // clips
    whole = lambda c: (0, 0)
    row = lambda c: (c, 0)
    return pl.pallas_call(
        functools.partial(attn_bwd_kernel, heads),
        grid=(clips,),
        in_specs=[
            pl.BlockSpec((seq, width), row),
            pl.BlockSpec((seq, width), row),
            pl.BlockSpec((seq, width), row),
            pl.BlockSpec((seq, LANES), row),
            pl.BlockSpec((seq, width), row),
            pl.BlockSpec((heads, seq, LANES), lambda c: (0, c, 0)),
            pl.BlockSpec((seq, 2 * width), row),
            pl.BlockSpec((seq, width), row),
            pl.BlockSpec(merged.shape, whole),
            pl.BlockSpec((width, width), whole),
            pl.BlockSpec(vec.shape, whole),
            pl.BlockSpec(early.shape, whole),
        ],
        out_specs=[
            pl.BlockSpec((seq, width), row),
            pl.BlockSpec(merged.shape, whole),
            pl.BlockSpec((width, width), whole),
        ],
        out_shape=[
            jax.ShapeDtypeStruct((total, width), BF16),
            jax.ShapeDtypeStruct(merged.shape, BF16),
            jax.ShapeDtypeStruct((width, width), BF16),
        ],
        scratch_shapes=[
            pltpu.VMEM((seq, width), BF16),
            pltpu.VMEM((seq, 3 * width), BF16),
            pltpu.VMEM((width, 3 * width), F32),
            pltpu.VMEM((width, width), F32),
            pltpu.VMEM((16, width), F32),
        ],
        compiler_params=pltpu.CompilerParams(
            dimension_semantics=("arbitrary",), vmem_limit_bytes=LIMIT),
        name="attn_bwd",
    )(xc, cot, dmid, dead, n1, qa, kv, mix, merged, output, vec, early)


def bits_of(size):
    return size.bit_length() - 1


class Cube:
    def __init__(self, dp, blk):
        self.sizes = (dp, blk)
        self.n_dp, self.n_blk = bits_of(dp), bits_of(blk)
        self.count = self.n_dp + self.n_blk
        self.core = self.count - 1
        self.cross = self.count - 2

    def bind(self):
        self.at_dp, self.at_blk = lax.axis_index("dp"), lax.axis_index("blk")
        self.mine = [lax.rem(self.at_dp // (1 << (self.n_dp - 1 - k)), 2) for k in range(self.n_dp)]
        self.mine += [lax.rem(self.at_blk // (1 << (self.n_blk - 1 - k)), 2) for k in range(self.n_blk)]
        return self

    def partner(self, bit):
        if bit < self.n_dp:
            step = 1 << (self.n_dp - 1 - bit)
            return (self.at_dp + step - 2 * step * self.mine[bit], self.at_blk)
        step = 1 << (self.count - 1 - bit)
        return (self.at_dp, self.at_blk + step - 2 * step * self.mine[bit])

    def row_peer(self, offset):
        return (self.at_dp, lax.rem(self.at_blk + offset, self.sizes[1]))

    def column_peer(self, offset):
        return (lax.rem(self.at_dp + offset, self.sizes[0]), self.at_blk)

    def barrier(self):
        sem = pltpu.get_barrier_semaphore()
        others = [self.row_peer(k) for k in range(1, self.sizes[1])]
        others += [self.column_peer(k) for k in range(1, self.sizes[0])]
        for other in others:
            pl.semaphore_signal(sem, inc=1, device_id=other, device_id_type=MESH)
        pl.semaphore_wait(sem, len(others))

    def order(self, letters):
        far = [bit for bit in range(self.n_dp - 1)]
        near = {"Y": [self.n_dp - 1], "X": [k for k in range(self.n_dp, self.count - 1)],
                "a": far[-1:], "b": far[:-1]}
        return [bit for letter in letters for bit in near[letter]]


def remote(src, dst, send, recv, device):
    return pltpu.make_async_remote_copy(
        src_ref=src, dst_ref=dst, send_sem=send, recv_sem=recv, device_id=device, device_id_type=MESH)


class Gather:
    def __init__(self, cube, src, dst, cols, order, send, recv):
        self.cube, self.src, self.dst, self.cols = cube, src, dst, cols
        self.order = list(order) + [cube.core]
        self.send, self.recv, self.step = send, recv, 0

    def start(self):
        cube, s = self.cube, self.step
        sel = tuple(slice(None) if bit in self.order[:s] else cube.mine[bit] for bit in range(cube.count))
        there = self.dst.at[sel + (slice(None), self.cols)]
        here = self.src.at[:, self.cols] if s == 0 else there
        self.copy = remote(here, there, self.send.at[s], self.recv.at[s], cube.partner(self.order[s]))
        self.copy.start()

    def advance(self):
        self.copy.wait()
        self.step += 1
        if self.step < len(self.order):
            self.start()


class Reduce:
    def __init__(self, cube, src, cols, order, held, landed, out, out_cols, send, recv, local):
        self.cube, self.src, self.cols, self.held, self.landed = cube, src, cols, held, landed
        self.order = [cube.core] + list(order)
        self.out, self.out_cols = out, out_cols
        self.send, self.recv, self.local, self.step = send, recv, local, 0

    def part(self, kept):
        cube, s = self.cube, self.step
        sel = []
        for bit in range(cube.count):
            if bit in self.order[:s]:
                pick = cube.mine[bit]
            elif bit == self.order[s]:
                pick = cube.mine[bit] if kept else 1 - cube.mine[bit]
            else:
                pick = slice(None)
            sel.append(pick)
        return tuple(sel)

    def start(self):
        s = self.step
        if s == 0:
            here = self.src.at[self.part(False) + (slice(None), self.cols)]
            self.own = pltpu.make_async_copy(
                self.src.at[self.part(True) + (slice(None), self.cols)], self.held, self.local)
            self.own.start()
        else:
            here = self.held.at[self.part(False)[:-1]]
        self.copy = remote(here, self.landed[s], self.send.at[s], self.recv.at[s],
                           self.cube.partner(self.order[s]))
        self.copy.start()

    def advance(self):
        s = self.step
        self.copy.wait()
        if s == 0:
            self.own.wait()
        keep = self.part(True)[:-1]
        width = self.held.shape[-1]
        if s + 1 == len(self.order):
            self.out[:, self.out_cols] = self.held[keep].astype(F32) + self.landed[s][...].astype(F32)
        else:
            wide = [slice(None)] * (len(self.landed[s].shape) - 1)
            tile = LANES * max(k for k in (1, 2, 3) if width % (LANES * k) == 0)

            def add(j, _):
                cols = (pl.ds(pl.multiple_of(j * tile, tile), tile),)
                at = keep + (slice(None),) + cols
                self.held[at] = self.held[at] + self.landed[s][tuple(wide) + cols]
                return 0

            lax.fori_loop(0, width // tile, add, 0)
        self.step += 1
        if self.step < len(self.order):
            self.start()


def comm_in_kernel(cube, parts, n_w, n_t, *refs):
    cube.bind()
    w_in, t_in = refs[:n_w], refs[n_w:n_w + n_t]
    refs = refs[n_w + n_t:]
    w_out, t_out = refs[:n_w], refs[n_w:n_w + n_t]
    send, recv, local, t_send, t_recv, t_local = refs[n_w + n_t:]
    cube.barrier()
    gathers = [Gather(cube, w_in[a], w_out[a], pl.ds(start, size), cube.order(order), send.at[k], recv.at[k])
               for k, (a, start, size, order) in enumerate(parts)]
    for gather in gathers:
        gather.start()
    kept = []
    for a in range(n_w):
        kept.append(pltpu.make_async_copy(w_in[a], w_out[a].at[tuple(cube.mine)], local.at[a]))
    exchanges = []
    blk = cube.sizes[1]
    for a in range(n_t):
        clips = t_out[a].shape[0]
        kept.append(pltpu.make_async_copy(
            t_in[a].at[pl.ds(cube.at_blk * clips, clips)], t_out[a].at[:, cube.at_blk], t_local.at[a]))
        for k in range(1, blk):
            other = cube.row_peer(k)
            exchanges.append(remote(
                t_in[a].at[pl.ds(other[1] * clips, clips)], t_out[a].at[:, cube.at_blk],
                t_send.at[a, k - 1], t_recv.at[a, k - 1], other))
    for copy in kept + exchanges:
        copy.start()
    for copy in kept:
        copy.wait()
    for _ in range(cube.count):
        for gather in gathers:
            gather.advance()
    for copy in exchanges:
        copy.wait()


def comm_in(weights, toks, dp, blk, parts, cid):
    cube = Cube(dp, blk)
    n_w, n_t, n_p = len(weights), len(toks), len(parts)
    anywhere = pl.BlockSpec(memory_space=pl.ANY)
    outs = [jax.ShapeDtypeStruct((2,) * cube.count + w.shape, w.dtype) for w in weights]
    outs += [jax.ShapeDtypeStruct((t.shape[0] // blk, blk) + t.shape[1:], t.dtype) for t in toks]
    return pl.pallas_call(
        functools.partial(comm_in_kernel, cube, parts, n_w, n_t),
        in_specs=[anywhere] * (n_w + n_t),
        out_specs=[anywhere] * (n_w + n_t),
        out_shape=outs,
        scratch_shapes=[
            pltpu.SemaphoreType.DMA((n_p, cube.count)),
            pltpu.SemaphoreType.DMA((n_p, cube.count)),
            pltpu.SemaphoreType.DMA((n_w,)),
            pltpu.SemaphoreType.DMA((max(n_t, 1), blk)),
            pltpu.SemaphoreType.DMA((max(n_t, 1), blk)),
            pltpu.SemaphoreType.DMA((max(n_t, 1),)),
        ],
        compiler_params=pltpu.CompilerParams(collective_id=cid, has_side_effects=True, vmem_limit_bytes=LIMIT),
        name="comm_in",
    )(*weights, *toks)


def comm_out_kernel(cube, parts, n_w, n_t, *refs):
    cube.bind()
    w_in, t_in = refs[:n_w], refs[n_w:n_w + n_t]
    refs = refs[n_w + n_t:]
    w_out, norm, t_out = refs[:n_w], refs[n_w], refs[n_w + 1:n_w + 1 + n_t]
    refs = refs[n_w + 1 + n_t:]
    n_p = len(parts)
    held = refs[:n_p]
    landed = [refs[n_p + k * cube.count:n_p + (k + 1) * cube.count] for k in range(n_p)]
    send, recv, local, t_send, t_recv, t_local, sums, s_send, s_recv = refs[n_p * (1 + cube.count):]
    dp, blk = cube.sizes
    cube.barrier()
    reduces = [
        Reduce(cube, w_in[a], pl.ds(start, size), cube.order(order), held[k], landed[k], w_out[a],
               pl.ds(start, size), send.at[k], recv.at[k], local.at[k])
        for k, (a, start, size, order) in enumerate(parts)]
    for reduce in reduces:
        reduce.start()
    kept, exchanges = [], []
    for a in range(n_t):
        clips = t_in[a].shape[0]
        here = pl.ds(cube.at_blk * clips, clips)
        kept.append(pltpu.make_async_copy(t_in[a].at[:, cube.at_blk], t_out[a].at[here], t_local.at[a]))
        for k in range(1, blk):
            other = cube.row_peer(k)
            exchanges.append(remote(t_in[a].at[:, other[1]], t_out[a].at[here],
                                    t_send.at[a, k - 1], t_recv.at[a, k - 1], other))
    for copy in kept + exchanges:
        copy.start()
    for _ in range(cube.count):
        for reduce in reduces:
            reduce.advance()
    for copy in kept + exchanges:
        copy.wait()
    total = jnp.zeros((), F32)
    for out in w_out:
        total = total + jnp.sum(out[...] * out[...])
    for axis, (size, peer, at) in enumerate(((dp, cube.column_peer, cube.at_dp), (blk, cube.row_peer, cube.at_blk))):
        box = sums[axis]
        box[at] = jnp.full(box.shape[1:], total, F32)
        copies = [remote(box.at[at], box.at[at], s_send[axis].at[k - 1], s_recv[axis].at[k - 1], peer(k))
                  for k in range(1, size)]
        for copy in copies:
            copy.start()
        for copy in copies:
            copy.wait()
        whole = box[0]
        for k in range(1, size):
            whole = whole + box[k]
        total = whole[0, 0]
    norm[...] = whole


def comm_out(grads, toks, dp, blk, parts, cid):
    cube = Cube(dp, blk)
    n_w, n_t, n_p = len(grads), len(toks), len(parts)
    anywhere = pl.BlockSpec(memory_space=pl.ANY)
    inside = pl.BlockSpec(memory_space=pltpu.VMEM)
    shards = [g.shape[-2:] for g in grads]
    outs = [jax.ShapeDtypeStruct(s, F32) for s in shards] + [jax.ShapeDtypeStruct((8, LANES), F32)]
    outs += [jax.ShapeDtypeStruct((t.shape[0] * blk,) + t.shape[2:], t.dtype) for t in toks]
    held, landed = [], []
    for a, _, size, _ in parts:
        tail = (shards[a][0], size)
        held.append(pltpu.VMEM((2,) * (cube.count - 1) + tail, BF16))
        landed += [pltpu.VMEM((2,) * (cube.count - 1 - s) + tail, BF16) for s in range(cube.count)]
    return pl.pallas_call(
        functools.partial(comm_out_kernel, cube, parts, n_w, n_t),
        in_specs=[anywhere] * (n_w + n_t),
        out_specs=[inside] * (n_w + 1) + [anywhere] * n_t,
        out_shape=outs,
        scratch_shapes=held + landed + [
            pltpu.SemaphoreType.DMA((n_p, cube.count)),
            pltpu.SemaphoreType.DMA((n_p, cube.count)),
            pltpu.SemaphoreType.DMA((n_p,)),
            pltpu.SemaphoreType.DMA((max(n_t, 1), blk)),
            pltpu.SemaphoreType.DMA((max(n_t, 1), blk)),
            pltpu.SemaphoreType.DMA((max(n_t, 1),)),
            [pltpu.VMEM((dp, 8, LANES), F32), pltpu.VMEM((blk, 8, LANES), F32)],
            [pltpu.SemaphoreType.DMA((dp,)), pltpu.SemaphoreType.DMA((blk,))],
            [pltpu.SemaphoreType.DMA((dp,)), pltpu.SemaphoreType.DMA((blk,))],
        ],
        compiler_params=pltpu.CompilerParams(collective_id=cid, has_side_effects=True, vmem_limit_bytes=LIMIT),
        name="comm_out",
    )(*grads, *toks)


def key_columns(kept_time, kept_bands, blocks, own, segment, padded):
    clips = kept_time.shape[0] // blocks
    kept_time = lax.dynamic_slice_in_dim(kept_time, own * clips, clips)
    kept_bands = lax.dynamic_slice_in_dim(kept_bands, own * clips, clips)
    columns = kept_time.shape[1] // blocks
    patches = kept_time.reshape(clips, blocks, columns, 1) * kept_bands[:, None, None, :]
    patches = patches.reshape(clips, blocks, columns * kept_bands.shape[1])
    leading = (jnp.arange(blocks, dtype=jnp.int32) == 0).astype(jnp.int32)
    special = jnp.broadcast_to(leading[None, :, None], (clips, blocks, segment - patches.shape[2]))
    live = jnp.concatenate([special, patches, jnp.zeros((clips, blocks, padded - segment), jnp.int32)], 2)
    bias = jnp.where(live > 0, 0.0, -1e30).reshape(-1, 1)
    lane = jnp.arange(LANES, dtype=jnp.int32)[None, :] % HALF
    return jnp.where(lane == 0, bias, jnp.where(lane < 4, 1.0, 0.0)).astype(BF16)


def prepare_kernel(tok_ref, cot_ref, xc_ref, low_ref):
    segment, extra = tok_ref.shape[1], xc_ref.shape[1] - tok_ref.shape[1]
    values = tok_ref[...]
    centred = (values - jnp.mean(values, -1, keepdims=True)).astype(BF16)
    blank = jnp.zeros((values.shape[0], extra, values.shape[2]), BF16)
    xc_ref[...] = jnp.concatenate([centred, blank], 1)
    low_ref[...] = jnp.concatenate([cot_ref[...].astype(BF16), blank], 1)


def prepare(tokens, cotangent, padded):
    clips, segment, width = tokens.shape
    wide = pl.BlockSpec((2, segment, width), lambda i: (i, 0, 0))
    out = pl.BlockSpec((2, padded, width), lambda i: (i, 0, 0))
    shape = jax.ShapeDtypeStruct((clips, padded, width), BF16)
    return pl.pallas_call(
        prepare_kernel, grid=(clips // 2,), in_specs=[wide, wide], out_specs=[out, out], out_shape=[shape, shape],
        compiler_params=pltpu.CompilerParams(dimension_semantics=("arbitrary",), vmem_limit_bytes=LIMIT),
        name="prepare")(tokens, cotangent)


def finish_kernel(tok_ref, cot_ref, act_ref, dlt_ref, out_ref, grad_ref):
    segment = tok_ref.shape[1]
    out_ref[...] = tok_ref[...] + act_ref[...].astype(F32)[:, :segment]
    grad_ref[...] = cot_ref[...] + dlt_ref[...].astype(F32)[:, :segment]


def finish(tokens, cotangent, act, dlt):
    clips, segment, width = tokens.shape
    wide = pl.BlockSpec((2, segment, width), lambda i: (i, 0, 0))
    low = pl.BlockSpec((2,) + act.shape[1:], lambda i: (i, 0, 0))
    shape = jax.ShapeDtypeStruct(tokens.shape, F32)
    return pl.pallas_call(
        finish_kernel, grid=(clips // 2,), in_specs=[wide, wide, low, low], out_specs=[wide, wide],
        out_shape=[shape, shape],
        compiler_params=pltpu.CompilerParams(dimension_semantics=("arbitrary",), vmem_limit_bytes=LIMIT),
        name="finish")(tokens, cotangent, act, dlt)


RATES = (MATRIX_RATE, MATRIX_RATE, MATRIX_RATE, MATRIX_RATE, VECTOR_RATE)
DECAYS = (MATRIX_DECAY, MATRIX_DECAY, MATRIX_DECAY, MATRIX_DECAY, 0.0)


def adamw_kernel(norm_ref, *refs):
    weights, firsts, seconds, shares = refs[:5], refs[5:10], refs[10:15], refs[15:20]
    outs = refs[20:]
    factor = CLIP_LIMIT / jnp.maximum(jnp.sqrt(norm_ref[0:1, 0:1]), CLIP_LIMIT)
    for index in range(5):
        clipped = shares[index][...] * factor
        weight = weights[index][...]
        momentum = BETA_ONE * firsts[index][...] + (1.0 - BETA_ONE) * clipped
        variance = BETA_TWO * seconds[index][...] + (1.0 - BETA_TWO) * clipped * clipped
        mean_hat = momentum / (1.0 - BETA_ONE**STEP)
        var_hat = variance / (1.0 - BETA_TWO**STEP)
        updated = weight - RATES[index] * (
            mean_hat / (jnp.sqrt(var_hat) + ADAM_EPS) + DECAYS[index] * weight)
        for kind, value in enumerate((clipped, momentum, variance, updated)):
            outs[5 * kind + index][...] = value


def adamw(norm, weights, firsts, seconds, shares):
    inside = pl.BlockSpec(memory_space=pltpu.VMEM)
    return pl.pallas_call(
        adamw_kernel, in_specs=[inside] * 21, out_specs=[inside] * 20,
        out_shape=[jax.ShapeDtypeStruct(w.shape, F32) for w in weights] * 4,
        compiler_params=pltpu.CompilerParams(vmem_limit_bytes=LIMIT),
        name="adamw")(norm, *weights, *firsts, *seconds, *shares)


def shards(
    tokens, kept_time, kept_bands, cotangent,
    weight_merged, weight_output, weight_expand, weight_shrink, vectors,
    first_merged, first_output, first_expand, first_shrink, first_vectors,
    second_merged, second_output, second_expand, second_shrink, second_vectors,
):
    clip_count, segment, width = tokens.shape
    dp, blk = lax.axis_size("dp"), lax.axis_size("blk")
    own = lax.axis_index("blk")
    clips = clip_count // blk
    padded = -(-segment // 16) * 16
    total = clips * blk * padded
    rows = weight_merged.shape[0]
    ff = weight_expand.shape[1]
    cube = (2,) * (bits_of(dp) + bits_of(blk))

    columns = jnp.pad(vectors.T, ((0, 0), (0, LANES - vectors.shape[0])))
    merged_low = jnp.concatenate([weight_merged, columns], 1).astype(BF16)
    wide_low = jnp.concatenate([weight_output, weight_expand], 1).astype(BF16)
    xc_home, cot_home = prepare(tokens, cotangent, padded)
    half = (merged_low.shape[1] // LANES + 1) // 2 * LANES
    half_wide = wide_low.shape[1] // 2
    merged, wide, shrink, xc, cot = comm_in(
        [merged_low, wide_low, weight_shrink.astype(BF16)], [xc_home, cot_home], dp, blk,
        [(0, 0, half, "XbYa"), (0, half, merged_low.shape[1] - half, "XabY"),
         (1, 0, half_wide, "abXY"), (1, half_wide, half_wide, "XYab"), (2, 0, width, "bXYa")], 0)
    merged = merged.reshape(width, merged_low.shape[1])
    wide = wide.reshape(width, wide_low.shape[1])
    shrink = shrink.reshape(ff, width)
    xc, cot = xc.reshape(total, width), cot.reshape(total, width)
    vec = merged[:, 3 * width:3 * width + vectors.shape[0]].T.astype(F32)
    dead = key_columns(kept_time, kept_bands, blk, own, segment, padded)
    n1, qa, kv, mix, mid = attn_fwd(xc, dead, merged, wide, vec, clips, HEADS)
    act, dmid, grad_expand, grad_shrink, early = ffn(mid, xc, cot, wide, shrink, vec, blk * padded)
    dlt, grad_merged, grad_output = attn_bwd(
        xc, cot, dmid, dead, n1, qa, kv, mix, merged, wide, vec, early, clips, HEADS)
    grads = [g.reshape(cube + (g.shape[0] // (dp * blk), g.shape[1]))
             for g in (grad_merged, grad_output, grad_expand, grad_shrink)]
    sent = (clips, blk, padded, width)
    *shares, norm, act_home, dlt_home = comm_out(
        grads, [act.reshape(sent), dlt.reshape(sent)], dp, blk,
        [(0, 0, merged_low.shape[1], "YXba"), (1, 0, width, "aYXb"), (2, 0, ff // 2, "YbaX"),
         (2, ff // 2, ff // 2, "YXab"), (3, 0, width, "aYXb")], 1)
    activations, token_grads = finish(tokens, cotangent, act_home, dlt_home)
    shares.append(shares[0][:, 3 * width:3 * width + vectors.shape[0]].T)
    shares[0] = shares[0][:, :3 * width]
    steps_out = adamw(
        norm, (weight_merged, weight_output, weight_expand, weight_shrink, vectors),
        (first_merged, first_output, first_expand, first_shrink, first_vectors),
        (second_merged, second_output, second_expand, second_shrink, second_vectors), shares)
    return (activations, token_grads, jnp.sqrt(norm[0, 0]), *steps_out)


def solution(mesh):
    return jax.shard_map(
        shards,
        mesh=mesh,
        in_specs=(
            P("dp", "blk", None),
            P("dp", None),
            P("dp", None),
            P("dp", "blk", None),
            P(("dp", "blk"), None),
            P(("dp", "blk"), None),
            P(("dp", "blk"), None),
            P(("dp", "blk"), None),
            P(None, ("dp", "blk")),
            P(("dp", "blk"), None),
            P(("dp", "blk"), None),
            P(("dp", "blk"), None),
            P(("dp", "blk"), None),
            P(None, ("dp", "blk")),
            P(("dp", "blk"), None),
            P(("dp", "blk"), None),
            P(("dp", "blk"), None),
            P(("dp", "blk"), None),
            P(None, ("dp", "blk")),
        ),
        out_specs=(
            P("dp", "blk", None),
            P("dp", "blk", None),
            P(),
            P(("dp", "blk"), None),
            P(("dp", "blk"), None),
            P(("dp", "blk"), None),
            P(("dp", "blk"), None),
            P(None, ("dp", "blk")),
            P(("dp", "blk"), None),
            P(("dp", "blk"), None),
            P(("dp", "blk"), None),
            P(("dp", "blk"), None),
            P(None, ("dp", "blk")),
            P(("dp", "blk"), None),
            P(("dp", "blk"), None),
            P(("dp", "blk"), None),
            P(("dp", "blk"), None),
            P(None, ("dp", "blk")),
            P(("dp", "blk"), None),
            P(("dp", "blk"), None),
            P(("dp", "blk"), None),
            P(("dp", "blk"), None),
            P(None, ("dp", "blk")),
        ),
        check_vma=False,
    )
```

```python
import functools
import jax
import jax.numpy as jnp
from jax import lax
from jax.experimental import pallas as pl
from jax.experimental.pallas import tpu as pltpu
from jax.sharding import PartitionSpec as P

HEADS = 12
STEP = 5
CLIP_LIMIT = 1.0
BETA_ONE = 0.5
BETA_TWO = 0.5
ADAM_EPS = 1e-08
MATRIX_RATE = 0.1
VECTOR_RATE = 0.3
MATRIX_DECAY = 0.05

F32, BF16 = jnp.float32, jnp.bfloat16
EPS = 1e-06
HALF = 64
LANES = 128
LIMIT = 62 * 1024 * 1024
MESH = pl.DeviceIdType.MESH

FWD_PLAN = {1: [0, 2], 2: [1, 4], 4: [-1, 3], 5: [2], 6: [0, 1], 7: [-2], 10: [3, 4], 12: [0, 1], 14: [3], 15: [2],
            16: [4], -1: [-3, 1, 0, 3, 2, 4, 1, 0, 3, 2, 4]}
BWD_PLAN = {0: [-1], 1: [0, 1], 2: [2], 3: [3, -2], 4: [4], 6: [1], 8: [-3, 0, 2], 9: [3], 10: [4], 12: [0, 1, 4],
            15: [0, 3], 16: [2, 1], 17: [0], -1: [4, 3, 2, 1, 4, 3, 2]}


def nn(a, b):
    return lax.dot_general(a, b, (((1,), (0,)), ((), ())), preferred_element_type=F32)


def nt(a, b):
    return lax.dot_general(a, b, (((1,), (1,)), ((), ())), preferred_element_type=F32)


def tn(a, b):
    return lax.dot_general(a, b, (((0,), (0,)), ((), ())), preferred_element_type=F32)


def norm_stats(v):
    centre = jnp.mean(v, -1, keepdims=True)
    c = v - centre
    spread = jnp.mean(c * c, -1, keepdims=True)
    r = lax.rsqrt(spread + EPS)
    return c * r, r


def norm_back(xhat, r, dy, gain):
    dx = dy * gain
    m1 = jnp.mean(dx, -1, keepdims=True)
    m2 = jnp.mean(dx * xhat, -1, keepdims=True)
    return (dx - m1 - xhat * m2) * r


def gelu_pair(x):
    z = jnp.abs(x)
    t = 1.0 / (1.0 + 0.3275911 * 0.7071067811865476 * z)
    e = jnp.exp(-0.5 * x * x)
    poly = t * (0.127414796 + t * (-0.142248368 + t * (0.7107068705 + t * (-0.7265760135 + t * 0.5307027145))))
    tail = poly * e
    phi = jnp.where(x >= 0, 1.0 - tail, tail)
    return x * phi, phi + (0.3989422804014327 * x) * e


def ffn_kernel(mix_ref, xc_ref, cot_ref, prj_ref, exp_ref, shr_ref, vec_ref,
               act_ref, dmid_ref, ge_ref, gs_ref, sums_ref,
               mid_s, n2_s, y_s, dn_s, ae_s, as_s):
    f, i = pl.program_id(0), pl.program_id(1)
    nf, ni = pl.num_programs(0), pl.num_programs(1)
    rows = mix_ref.shape[0]
    here = pl.ds(pl.multiple_of(i * rows, rows), rows)

    @pl.when((f == 0) & (i == 0))
    def _():
        sums_ref[...] = jnp.zeros_like(sums_ref)

    @pl.when(f == 0)
    def _():
        mid = xc_ref[...].astype(F32) + nn(mix_ref[...], prj_ref[...]) + vec_ref[4:5, :]
        mid_s[here, :] = mid
        xhat, _ = norm_stats(mid)
        n2_s[here, :] = (xhat * vec_ref[5:6, :] + vec_ref[6:7, :]).astype(BF16)

    n2 = n2_s[here, :]
    d2 = cot_ref[...]
    h = nn(n2, exp_ref[...]) + vec_ref[pl.ds(8 + f, 1), :]
    dg = nt(d2, shr_ref[...])
    g, gp = gelu_pair(h)
    g = g.astype(BF16)
    dh32 = gp * dg
    dh = dh32.astype(BF16)
    sums_ref[pl.ds(8 + f, 1), :] += jnp.sum(dh32, 0, keepdims=True)
    y = nn(g, shr_ref[...])
    dn = nt(dh, exp_ref[...])
    ge = tn(n2, dh)
    gs = tn(g, d2)

    @pl.when(f == 0)
    def _():
        y_s[here, :] = y
        dn_s[here, :] = dn

    @pl.when(f > 0)
    def _():
        y_s[here, :] += y
        dn_s[here, :] += dn

    @pl.when(i == 0)
    def _():
        ae_s[...] = ge
        as_s[...] = gs

    @pl.when((i > 0) & (i < ni - 1))
    def _():
        ae_s[...] += ge
        as_s[...] += gs

    @pl.when(i == ni - 1)
    def _():
        ge_ref[...] = (ae_s[...] + ge).astype(ge_ref.dtype)
        gs_ref[...] = (as_s[...] + gs).astype(gs_ref.dtype)

    @pl.when(f == nf - 1)
    def _():
        mid = mid_s[here, :]
        cot = d2.astype(F32)
        xhat, r = norm_stats(mid)
        dy = dn_s[here, :]
        act_ref[...] = ((mid - xc_ref[...].astype(F32)) + (y_s[here, :] + vec_ref[7:8, :])).astype(BF16)
        dmid_ref[...] = cot + norm_back(xhat, r, dy, vec_ref[5:6, :])
        sums_ref[5:6, :] += jnp.sum(dy * xhat, 0, keepdims=True)
        sums_ref[6:7, :] += jnp.sum(dy, 0, keepdims=True)
        sums_ref[7:8, :] += jnp.sum(cot, 0, keepdims=True)


def ffn(mix, xc, cot, expand, shrink, vec, rows):
    total, width = xc.shape
    ff = expand.shape[1] - width
    nf, ni = ff // width, total // rows
    first = lambda f, i: (jnp.where((f == 0) | (f == nf - 1), i, ni - 1), 0)
    last = lambda f, i: (jnp.where(f == nf - 1, i, 0), 0)
    return pl.pallas_call(
        ffn_kernel,
        grid=(nf, ni),
        in_specs=[
            pl.BlockSpec((rows, width), lambda f, i: (jnp.where(f == 0, i, ni - 1), 0)),
            pl.BlockSpec((rows, width), first),
            pl.BlockSpec((rows, width), lambda f, i: (i, 0)),
            pl.BlockSpec((width, width), lambda f, i: (0, 0)),
            pl.BlockSpec((width, width), lambda f, i: (0, f + 1)),
            pl.BlockSpec((width, width), lambda f, i: (f, 0)),
            pl.BlockSpec(vec.shape, lambda f, i: (0, 0)),
        ],
        out_specs=[
            pl.BlockSpec((rows, width), last),
            pl.BlockSpec((rows, width), last),
            pl.BlockSpec((width, width), lambda f, i: (0, f)),
            pl.BlockSpec((width, width), lambda f, i: (f, 0)),
            pl.BlockSpec((16, width), lambda f, i: (0, 0)),
        ],
        out_shape=[
            jax.ShapeDtypeStruct((total, width), BF16),
            jax.ShapeDtypeStruct((total, width), F32),
            jax.ShapeDtypeStruct((width, ff), BF16),
            jax.ShapeDtypeStruct((ff, width), BF16),
            jax.ShapeDtypeStruct((16, width), F32),
        ],
        scratch_shapes=[
            pltpu.VMEM((total, width), F32),
            pltpu.VMEM((total, width), BF16),
            pltpu.VMEM((total, width), F32),
            pltpu.VMEM((total, width), F32),
            pltpu.VMEM((width, width), F32),
            pltpu.VMEM((width, width), F32),
        ],
        compiler_params=pltpu.CompilerParams(
            dimension_semantics=("arbitrary", "arbitrary"), vmem_limit_bytes=LIMIT),
        name="ffn",
    )(mix, xc, cot, expand, expand, shrink, vec)


def attn_fwd_kernel(cube, parts, plan, heads, xc_ref, dead_ref, mrg_ref, vec_ref, wide_in, shrink_in, cot_in,
                    n1_ref, qa_ref, kv_ref, mix_ref, wide_out, shrink_out, cot_out,
                    pk_s, send, recv, local, t_send, t_recv, t_local):
    width = xc_ref.shape[1]
    seq = xc_ref.shape[0]
    pairs = heads // 2
    cube.bind()
    clip = pl.program_id(0)
    own = [pltpu.make_async_copy(wide_in, wide_out.at[tuple(cube.mine)], local.at[0]),
           pltpu.make_async_copy(shrink_in, shrink_out.at[tuple(cube.mine)], local.at[1])]
    gathers = [Gather(cube, (wide_in, shrink_in)[a], (wide_out, shrink_out)[a], pl.ds(first, size), letters,
                      send.at[n], recv.at[n]) for n, (a, first, size, letters) in enumerate(parts)]
    exchange = Exchange(cube, cot_in, cot_out, False, t_send, t_recv, t_local)
    points = Points(plan, gathers, exchange)

    @pl.when(clip == 0)
    def _():
        cube.barrier()
        for gather in gathers:
            gather.start()
        for copy in own:
            copy.start()
        for copy in own:
            copy.wait()

    xc = xc_ref[...].astype(F32)
    xhat, _ = norm_stats(xc)
    n1 = (xhat * vec_ref[0:1, :] + vec_ref[1:2, :]).astype(BF16)
    n1_ref[...] = n1
    for third in range(3):
        cols = pl.ds(third * width, width)
        part = nn(n1, mrg_ref[:, cols])
        if third != 1:
            part = part + vec_ref[2 + third // 2:3 + third // 2, :]
        part = part.astype(BF16)
        pk_s[:, cols] = part
        if third:
            kv_ref[:, pl.ds((third - 1) * width, width)] = part
    lane = lax.broadcasted_iota(jnp.int32, (seq, LANES), 1)
    low = lane < HALF
    in_half = lane % HALF
    dead = dead_ref[...]
    ones = jnp.ones((seq, LANES), BF16)

    def pair(p, _):
        points.visit(clip * pairs + p, False)
        qcols = pl.ds(pl.multiple_of(p * LANES, LANES), LANES)
        kcols = pl.ds(pl.multiple_of(width + p * LANES, LANES), LANES)
        vcols = pl.ds(pl.multiple_of(2 * width + p * LANES, LANES), LANES)
        q = pk_s[:, qcols] * jnp.array(0.125, BF16)
        k = pk_s[:, kcols]
        v = pk_s[:, vcols]
        outs = []
        for side in range(2):
            mine = low if side == 0 else ~low
            qs = jnp.where(mine, q, jnp.where(in_half == 0, 1.0, 0.0).astype(BF16))
            ks = jnp.where(mine, k, dead)
            vs = jnp.where(mine, v, ones)
            s = nt(qs, ks)
            top = jnp.max(s, -1, keepdims=True)
            e = jnp.exp(s - top).astype(BF16)
            o = nn(e, vs)
            swapped = pltpu.roll(o, HALF, 1)
            outs.append(o / swapped)
            lse = top + jnp.log(jnp.where(mine, swapped, o))
            hi = (-lse).astype(BF16)
            rest = -lse - hi.astype(F32)
            mid_part = rest.astype(BF16)
            lo = (rest - mid_part.astype(F32)).astype(BF16)
            extra = jnp.where(in_half == 0, 1.0, 0.0).astype(BF16)
            extra = jnp.where(in_half == 1, hi, extra)
            extra = jnp.where(in_half == 2, mid_part, extra)
            extra = jnp.where(in_half == 3, lo, extra)
            qa_ref[2 * p + side] = jnp.where(mine, q, extra)
        mix_ref[:, qcols] = jnp.where(low, outs[0], outs[1]).astype(BF16)
        return 0

    lax.fori_loop(0, pairs, pair, 0)

    @pl.when(clip == pl.num_programs(0) - 1)
    def _():
        points.finish()
        for part in range(exchange.clips):
            exchange.wait(part)


class Points:
    def __init__(self, plan, movers, exchange):
        self.plan, self.movers, self.exchange = plan, movers, exchange

    def act(self, which):
        if which < 0:
            self.exchange.start(-1 - which)
        else:
            self.movers[which].advance()

    def visit(self, now, last):
        for point in sorted(p for p in self.plan if p >= 0):
            @pl.when(now == point)
            def _():
                for which in self.plan[point]:
                    self.act(which)

    def finish(self):
        for which in self.plan[-1]:
            self.act(which)


def attn_fwd(xc, dead, merged, vec, wide, shrink, cot, clips, heads, dp, blk, cid):
    total, width = xc.shape
    seq = total // clips
    cube = Cube(dp, blk)
    whole = lambda c: (0, 0)
    row = lambda c: (c, 0)
    anywhere = pl.BlockSpec(memory_space=pl.ANY)
    third, half = wide.shape[1] // 3, shrink.shape[1] // 2
    parts = [(0, 0, third, "XbYa"), (0, third, third, "baXY"), (0, 2 * third, third, "YXba"),
             (1, 0, half, "baYX"), (1, half, half, "XbaY")]
    return pl.pallas_call(
        functools.partial(attn_fwd_kernel, cube, parts, FWD_PLAN, heads),
        grid=(clips,),
        in_specs=[
            pl.BlockSpec((seq, width), row),
            pl.BlockSpec((seq, LANES), row),
            pl.BlockSpec(merged.shape, whole),
            pl.BlockSpec(vec.shape, whole),
            pl.BlockSpec(wide.shape, whole),
            pl.BlockSpec(shrink.shape, whole),
            anywhere,
        ],
        out_specs=[
            pl.BlockSpec((seq, width), row),
            pl.BlockSpec((heads, seq, LANES), lambda c: (0, c, 0)),
            pl.BlockSpec((seq, 2 * width), row),
            pl.BlockSpec((seq, width), row),
            anywhere, anywhere, anywhere,
        ],
        out_shape=[
            jax.ShapeDtypeStruct((total, width), BF16),
            jax.ShapeDtypeStruct((heads, total, LANES), BF16),
            jax.ShapeDtypeStruct((total, 2 * width), BF16),
            jax.ShapeDtypeStruct((total, width), BF16),
            jax.ShapeDtypeStruct((2,) * cube.count + wide.shape, BF16),
            jax.ShapeDtypeStruct((2,) * cube.count + shrink.shape, BF16),
            jax.ShapeDtypeStruct((clips, blk) + cot.shape[1:], BF16),
        ],
        scratch_shapes=[
            pltpu.VMEM((seq, 3 * width), BF16),
            pltpu.SemaphoreType.DMA((len(parts), cube.count)),
            pltpu.SemaphoreType.DMA((len(parts), cube.count)),
            pltpu.SemaphoreType.DMA((2,)),
        ] + exchange_semaphores(clips, blk),
        compiler_params=pltpu.CompilerParams(
            dimension_semantics=("arbitrary",), vmem_limit_bytes=LIMIT, collective_id=cid, has_side_effects=True),
        name="attn_fwd",
    )(xc, dead, merged, vec, wide, shrink, cot)


def attn_bwd_kernel(cube, parts, plan, heads, xc_ref, cot_ref, dmid_ref, dead_ref, n1_ref, qa_ref, kv_ref, mix_ref,
                    mrg_ref, out_ref, vec_ref, early_ref,
                    ge_in, gs_in, act_in,
                    dlt_ref, gm_ref, go_ref, ge_out, gs_out, act_out,
                    dm_s, dp_s, am_s, ao_s, sums_ref, *refs):
    c = pl.program_id(0)
    n = pl.num_programs(0)
    seq, width = xc_ref.shape
    pairs = heads // 2
    cube.bind()
    n_p = len(parts)
    held = refs[:n_p]
    landed = [refs[n_p + k * cube.count:n_p + (k + 1) * cube.count] for k in range(n_p)]
    send, recv, local, t_send, t_recv, t_local = refs[n_p * (1 + cube.count):]
    reduces = [Reduce(cube, (ge_in, gs_in)[a], pl.ds(first, size), letters, held[k], landed[k], (ge_out, gs_out)[a],
                      send.at[k], recv.at[k], local.at[k])
               for k, (a, first, size, letters) in enumerate(parts)]
    exchange = Exchange(cube, act_in, act_out, True, t_send, t_recv, t_local)
    points = Points(plan, reduces, exchange)

    @pl.when(c == 0)
    def _():
        cube.barrier()
        for reduce in reduces:
            reduce.start()
        sums_ref[...] = early_ref[...]
        am_s[...] = jnp.zeros_like(am_s)
        ao_s[...] = jnp.zeros_like(ao_s)

    d_one = dmid_ref[...].astype(BF16)
    dm_s[...] = nt(d_one, out_ref[...]).astype(BF16)
    ao_s[...] += tn(mix_ref[...], d_one)
    sums_ref[4:5, :] += jnp.sum(d_one.astype(F32), 0, keepdims=True)

    lane = lax.broadcasted_iota(jnp.int32, (seq, LANES), 1)
    low = lane < HALF
    in_half = lane % HALF
    dead = dead_ref[...]
    vone = jnp.where(in_half < 2, 1.0, 0.0).astype(BF16)

    def pair(p, _):
        points.visit(c * pairs + p, False)
        qcols = pl.ds(pl.multiple_of(p * LANES, LANES), LANES)
        kcols = pl.ds(pl.multiple_of(width + p * LANES, LANES), LANES)
        vcols = pl.ds(pl.multiple_of(2 * width + p * LANES, LANES), LANES)
        k = kv_ref[:, qcols]
        v = kv_ref[:, kcols]
        dm = dm_s[:, qcols]
        prod = dm.astype(F32) * mix_ref[:, qcols].astype(F32)
        k_t = jnp.transpose(k)
        dks, dvs, dqs = [], [], []
        for side in range(2):
            mine = low if side == 0 else ~low
            qa = qa_ref[2 * p + side]
            ka = jnp.where(mine, k, dead)
            va = jnp.where(mine, v, vone)
            dd = -jnp.sum(jnp.where(mine, prod, 0.0), -1, keepdims=True)
            hi = dd.astype(BF16)
            lo = (dd - hi.astype(F32)).astype(BF16)
            da = jnp.where(mine, dm, jnp.where(in_half == 0, hi, lo))
            p_t = jnp.exp(nt(ka, qa))
            ds_t = (p_t * nt(va, da)).astype(BF16)
            dvs.append(nn(p_t.astype(BF16), da))
            dks.append(nn(ds_t, qa))
            dqs.append(nn(k_t[side * HALF:(side + 1) * HALF, :], ds_t))
        dq = jnp.transpose(jnp.concatenate(dqs, 0)) * 0.125
        dk = jnp.where(low, dks[0], dks[1])
        dv = jnp.where(low, dvs[0], dvs[1])
        sums_ref[2:3, qcols] += jnp.sum(dq, 0, keepdims=True)
        sums_ref[3:4, qcols] += jnp.sum(dv, 0, keepdims=True)
        dp_s[:, qcols] = dq.astype(BF16)
        dp_s[:, kcols] = dk.astype(BF16)
        dp_s[:, vcols] = dv.astype(BF16)
        return 0

    lax.fori_loop(0, pairs, pair, 0)
    dp = dp_s[...]
    am_s[...] += tn(n1_ref[...], dp)
    dy = nt(dp, mrg_ref[:, :3 * width])
    xhat, r = norm_stats(xc_ref[...].astype(F32))
    sums_ref[0:1, :] += jnp.sum(dy * xhat, 0, keepdims=True)
    sums_ref[1:2, :] += jnp.sum(dy, 0, keepdims=True)
    dlt_ref[...] = ((dmid_ref[...] - cot_ref[...].astype(F32))
                    + norm_back(xhat, r, dy, vec_ref[0:1, :])).astype(BF16)

    @pl.when(c == n - 1)
    def _():
        gm_ref[:, :3 * width] = am_s[...].astype(gm_ref.dtype)
        columns = jnp.transpose(sums_ref[...])
        gm_ref[:, 3 * width:] = jnp.concatenate(
            [columns, jnp.zeros((width, LANES - columns.shape[1]), F32)], 1).astype(gm_ref.dtype)
        go_ref[...] = ao_s[...].astype(go_ref.dtype)
        points.finish()
        for part in range(exchange.clips):
            exchange.wait(part)


def attn_bwd(xc, cot, dmid, dead, n1, qa, kv, mix, merged, output, vec, early,
             grad_expand, grad_shrink, act, clips, heads, dp, blk, cid):
    total, width = xc.shape
    seq = total // clips
    cube = Cube(dp, blk)
    whole = lambda c: (0, 0)
    row = lambda c: (c, 0)
    once = pl.Buffered(1)
    anywhere = pl.BlockSpec(memory_space=pl.ANY)
    shards = [grad_expand.shape[-2:], grad_shrink.shape[-2:]]
    third, half = shards[0][1] // 3, shards[1][1] // 2
    parts = [(0, 0, third, "bYaX"), (0, third, third, "YaXb"), (0, 2 * third, third, "YXab"),
             (1, 0, half, "XbYa"), (1, half, half, "aYbX")]
    return pl.pallas_call(
        functools.partial(attn_bwd_kernel, cube, parts, BWD_PLAN, heads),
        grid=(clips,),
        in_specs=[
            pl.BlockSpec((seq, width), row),
            pl.BlockSpec((seq, width), row),
            pl.BlockSpec((seq, width), row),
            pl.BlockSpec((seq, LANES), row),
            pl.BlockSpec((seq, width), row),
            pl.BlockSpec((heads, seq, LANES), lambda c: (0, c, 0)),
            pl.BlockSpec((seq, 2 * width), row),
            pl.BlockSpec((seq, width), row),
            pl.BlockSpec(merged.shape, whole, pipeline_mode=once),
            pl.BlockSpec((width, width), whole, pipeline_mode=once),
            pl.BlockSpec(vec.shape, whole),
            pl.BlockSpec(early.shape, whole),
            anywhere, anywhere, anywhere,
        ],
        out_specs=[
            pl.BlockSpec((seq, width), row),
            pl.BlockSpec(merged.shape, whole, pipeline_mode=once),
            pl.BlockSpec((width, width), whole, pipeline_mode=once),
            pl.BlockSpec(shards[0], whole, pipeline_mode=once),
            pl.BlockSpec(shards[1], whole, pipeline_mode=once),
            anywhere,
        ],
        out_shape=[
            jax.ShapeDtypeStruct((total, width), BF16),
            jax.ShapeDtypeStruct(merged.shape, BF16),
            jax.ShapeDtypeStruct((width, width), BF16),
            jax.ShapeDtypeStruct(shards[0], F32),
            jax.ShapeDtypeStruct(shards[1], F32),
            jax.ShapeDtypeStruct((clips * blk,) + act.shape[2:], BF16),
        ],
        scratch_shapes=[
            pltpu.VMEM((seq, width), BF16),
            pltpu.VMEM((seq, 3 * width), BF16),
            pltpu.VMEM((width, 3 * width), F32),
            pltpu.VMEM((width, width), F32),
            pltpu.VMEM((16, width), F32),
        ] + reduce_scratch(cube, [(shards[a][0], size) for a, _, size, _ in parts])
        + exchange_semaphores(clips, blk),
        compiler_params=pltpu.CompilerParams(
            dimension_semantics=("arbitrary",), vmem_limit_bytes=LIMIT, collective_id=cid, has_side_effects=True),
        name="attn_bwd",
    )(xc, cot, dmid, dead, n1, qa, kv, mix, merged, output, vec, early, grad_expand, grad_shrink, act)


def bits_of(size):
    return size.bit_length() - 1


class Cube:
    def __init__(self, dp, blk):
        self.sizes = (dp, blk)
        self.n_dp, self.n_blk = bits_of(dp), bits_of(blk)
        self.count = self.n_dp + self.n_blk
        far = list(range(self.n_dp - 1))
        self.letters = {"X": list(range(self.n_dp, self.count - 1)), "Y": [self.n_dp - 1],
                        "a": far[-1:], "b": far[:-1], "C": [self.count - 1]}

    def bind(self):
        self.at_dp, self.at_blk = lax.axis_index("dp"), lax.axis_index("blk")
        self.mine = [lax.rem(self.at_dp // (1 << (self.n_dp - 1 - k)), 2) for k in range(self.n_dp)]
        self.mine += [lax.rem(self.at_blk // (1 << (self.n_blk - 1 - k)), 2) for k in range(self.n_blk)]
        return self

    def partner(self, bit):
        if bit < self.n_dp:
            step = 1 << (self.n_dp - 1 - bit)
            return (self.at_dp + step - 2 * step * self.mine[bit], self.at_blk)
        step = 1 << (self.count - 1 - bit)
        return (self.at_dp, self.at_blk + step - 2 * step * self.mine[bit])

    def row_peer(self, offset):
        return (self.at_dp, lax.rem(self.at_blk + offset, self.sizes[1]))

    def column_peer(self, offset):
        return (lax.rem(self.at_dp + offset, self.sizes[0]), self.at_blk)

    def barrier(self):
        sem = pltpu.get_barrier_semaphore()
        others = [self.row_peer(k) for k in range(1, self.sizes[1])]
        others += [self.column_peer(k) for k in range(1, self.sizes[0])]
        for other in others:
            pl.semaphore_signal(sem, inc=1, device_id=other, device_id_type=MESH)
        pl.semaphore_wait(sem, len(others))


def remote(src, dst, send, recv, device):
    return pltpu.make_async_remote_copy(
        src_ref=src, dst_ref=dst, send_sem=send, recv_sem=recv, device_id=device, device_id_type=MESH)


class Gather:
    def __init__(self, cube, src, dst, cols, letters, send, recv):
        self.cube, self.src, self.dst, self.cols = cube, src, dst, cols
        self.steps = [cube.letters[letter] for letter in letters + "C"]
        self.order = sum(self.steps, [])
        self.send, self.recv, self.step = send, recv, 0

    def copy(self, s):
        cube = self.cube
        sel = tuple(slice(None) if bit in self.order[:s] else cube.mine[bit] for bit in range(cube.count))
        there = self.dst.at[sel + (slice(None), self.cols)]
        here = self.src.at[:, self.cols] if s == 0 else there
        return remote(here, there, self.send.at[s], self.recv.at[s], cube.partner(self.order[s]))

    def start(self):
        self.done = 0
        self.copy(0).start()

    def advance(self):
        for _ in self.steps[self.step]:
            self.copy(self.done).wait()
            self.done += 1
            if self.done < len(self.order):
                self.copy(self.done).start()
        self.step += 1


class Reduce:
    def __init__(self, cube, src, cols, letters, held, landed, out, send, recv, local):
        self.cube, self.src, self.cols, self.held, self.landed = cube, src, cols, held, landed
        self.steps = [cube.letters[letter] for letter in "C" + letters]
        self.order = sum(self.steps, [])
        self.out = out
        self.send, self.recv, self.local, self.step = send, recv, local, 0

    def part(self, s, kept):
        cube = self.cube
        sel = []
        for bit in range(cube.count):
            if bit in self.order[:s]:
                pick = cube.mine[bit]
            elif bit == self.order[s]:
                pick = cube.mine[bit] if kept else 1 - cube.mine[bit]
            else:
                pick = slice(None)
            sel.append(pick)
        return tuple(sel)

    def own(self):
        return pltpu.make_async_copy(
            self.src.at[self.part(0, True) + (slice(None), self.cols)], self.held, self.local)

    def copy(self, s):
        if s == 0:
            here = self.src.at[self.part(0, False) + (slice(None), self.cols)]
        else:
            here = self.held.at[self.part(s, False)[:-1]]
        return remote(here, self.landed[s], self.send.at[s], self.recv.at[s], self.cube.partner(self.order[s]))

    def start(self):
        self.done = 0
        self.own().start()
        self.copy(0).start()

    def add(self, s):
        keep = self.part(s, True)[:-1]
        width = self.held.shape[-1]
        if s + 1 == len(self.order):
            self.out[:, self.cols] = self.held[keep].astype(F32) + self.landed[s][...].astype(F32)
            return
        wide = (slice(None),) * (len(self.landed[s].shape) - 1)
        tile = LANES * max(k for k in (1, 2, 3) if width % (LANES * k) == 0)

        def some(j, _):
            cols = (pl.ds(pl.multiple_of(j * tile, tile), tile),)
            at = keep + (slice(None),) + cols
            self.held[at] = self.held[at] + self.landed[s][wide + cols]
            return 0

        lax.fori_loop(0, width // tile, some, 0)

    def advance(self):
        for _ in self.steps[self.step]:
            s = self.done
            self.copy(s).wait()
            if s == 0:
                self.own().wait()
            self.add(s)
            self.done += 1
            if self.done < len(self.order):
                self.copy(self.done).start()
        self.step += 1


class Exchange:
    def __init__(self, cube, src, dst, back, send, recv, local):
        self.cube, self.src, self.dst, self.back = cube, src, dst, back
        self.clips = (src if back else dst).shape[0]
        self.send, self.recv, self.local = send, recv, local

    def ends(self, to, clip):
        if self.back:
            return self.src.at[clip, to], self.dst.at[self.cube.at_blk * self.clips + clip]
        return self.src.at[to * self.clips + clip], self.dst.at[clip, self.cube.at_blk]

    def copies(self, clip):
        found = [pltpu.make_async_copy(*self.ends(self.cube.at_blk, clip), self.local.at[clip])]
        for k in range(1, self.cube.sizes[1]):
            other = self.cube.row_peer(k)
            found.append(remote(*self.ends(other[1], clip), self.send.at[clip, k - 1], self.recv.at[clip, k - 1], other))
        return found

    def start(self, clip):
        for copy in self.copies(clip):
            copy.start()

    def wait(self, clip):
        for copy in self.copies(clip):
            copy.wait()


def exchange_semaphores(clips, blk):
    return [pltpu.SemaphoreType.DMA((clips, blk)), pltpu.SemaphoreType.DMA((clips, blk)),
            pltpu.SemaphoreType.DMA((clips,))]


def front_kernel(cube, parts, plan, *refs):
    merged_in, xc_in, merged_out, xc_out, send, recv, local, t_send, t_recv, t_local = refs
    cube.bind().barrier()
    gathers = [Gather(cube, merged_in, merged_out, pl.ds(first, size), letters, send.at[k], recv.at[k])
               for k, (first, size, letters) in enumerate(parts)]
    for gather in gathers:
        gather.start()
    own = pltpu.make_async_copy(merged_in, merged_out.at[tuple(cube.mine)], local)
    own.start()
    exchange = Exchange(cube, xc_in, xc_out, False, t_send, t_recv, t_local)
    own.wait()
    for which in plan:
        if which < 0:
            exchange.start(-1 - which)
        else:
            gathers[which].advance()
    for clip in range(exchange.clips):
        exchange.wait(clip)


def front(merged, xc, dp, blk, cid):
    cube = Cube(dp, blk)
    clips = xc.shape[0] // blk
    anywhere = pl.BlockSpec(memory_space=pl.ANY)
    half = (merged.shape[1] // LANES + 1) // 2 * LANES
    parts = [(0, half, "XbYa"), (half, merged.shape[1] - half, "XabY")]
    plan = [0, 1] + [-1 - clip for clip in range(clips)] + [0, 1] * 4
    return pl.pallas_call(
        functools.partial(front_kernel, cube, parts, plan),
        in_specs=[pl.BlockSpec(memory_space=pltpu.VMEM), anywhere],
        out_specs=[anywhere] * 2,
        out_shape=[jax.ShapeDtypeStruct((2,) * cube.count + merged.shape, BF16),
                   jax.ShapeDtypeStruct((clips, blk) + xc.shape[1:], BF16)],
        scratch_shapes=[pltpu.SemaphoreType.DMA((len(parts), cube.count)),
                        pltpu.SemaphoreType.DMA((len(parts), cube.count)),
                        pltpu.SemaphoreType.DMA] + exchange_semaphores(clips, blk),
        compiler_params=pltpu.CompilerParams(collective_id=cid, has_side_effects=True, vmem_limit_bytes=LIMIT),
        name="front",
    )(merged, xc)


def back_kernel(cube, parts, plan, *refs):
    grads, early, toks = refs[:2], refs[2:4], refs[4]
    outs, norm, home = refs[5:7], refs[7], refs[8]
    refs = refs[9:]
    n_p = len(parts)
    held = refs[:n_p]
    landed = [refs[n_p + k * cube.count:n_p + (k + 1) * cube.count] for k in range(n_p)]
    send, recv, local, t_send, t_recv, t_local, sums, s_send, s_recv = refs[n_p * (1 + cube.count):]
    dp, blk = cube.sizes
    cube.bind().barrier()
    reduces = [Reduce(cube, grads[a], pl.ds(first, size), letters, held[k], landed[k], outs[a],
                      send.at[k], recv.at[k], local.at[k])
               for k, (a, first, size, letters) in enumerate(parts)]
    for reduce in reduces:
        reduce.start()
    exchange = Exchange(cube, toks, home, True, t_send, t_recv, t_local)
    total = jnp.sum(early[0][...] * early[0][...]) + jnp.sum(early[1][...] * early[1][...])
    for which in plan:
        if which < 0:
            exchange.start(-1 - which)
        else:
            reduces[which].advance()
    for out in outs:
        total = total + jnp.sum(out[...] * out[...])
    for axis, (size, peer, at) in enumerate(((dp, cube.column_peer, cube.at_dp), (blk, cube.row_peer, cube.at_blk))):
        box = sums[axis]
        box[at] = jnp.full(box.shape[1:], total, F32)
        copies = [remote(box.at[at], box.at[at], s_send[axis].at[k - 1], s_recv[axis].at[k - 1], peer(k))
                  for k in range(1, size)]
        for copy in copies:
            copy.start()
        for copy in copies:
            copy.wait()
        whole = box[0]
        for k in range(1, size):
            whole = whole + box[k]
        total = whole[0, 0]
    norm[...] = whole
    for clip in range(exchange.clips):
        exchange.wait(clip)


def reduce_scratch(cube, shapes):
    held = [pltpu.VMEM((2,) * (cube.count - 1) + s, BF16) for s in shapes]
    landed = [pltpu.VMEM((2,) * (cube.count - 1 - k) + s, BF16) for s in shapes for k in range(cube.count)]
    return held + landed + [pltpu.SemaphoreType.DMA((len(shapes), cube.count)),
                            pltpu.SemaphoreType.DMA((len(shapes), cube.count)),
                            pltpu.SemaphoreType.DMA((len(shapes),))]


def back(merged, output, expand_share, shrink_share, dlt, dp, blk, cid):
    cube = Cube(dp, blk)
    clips = dlt.shape[0]
    anywhere = pl.BlockSpec(memory_space=pl.ANY)
    inside = pl.BlockSpec(memory_space=pltpu.VMEM)
    shards = [merged.shape[-2:], output.shape[-2:]]
    third = shards[0][1] // LANES // 3 * LANES
    parts = [(0, 0, shards[0][1] - 2 * third, "YbXa"), (0, shards[0][1] - 2 * third, third, "aYXb"),
             (0, shards[0][1] - third, third, "aYXb"), (1, 0, shards[1][1], "YabX")]
    plan = [0, 1, 2, 3] + [-1 - clip for clip in range(clips)] + [0, 1, 2, 3] * 4
    return pl.pallas_call(
        functools.partial(back_kernel, cube, parts, plan),
        in_specs=[anywhere] * 2 + [inside] * 2 + [anywhere],
        out_specs=[inside] * 3 + [anywhere],
        out_shape=[jax.ShapeDtypeStruct(s, F32) for s in shards] + [
            jax.ShapeDtypeStruct((8, LANES), F32),
            jax.ShapeDtypeStruct((clips * blk,) + dlt.shape[2:], BF16)],
        scratch_shapes=reduce_scratch(cube, [(shards[a][0], size) for a, _, size, _ in parts])
        + exchange_semaphores(clips, blk) + [
            [pltpu.VMEM((dp, 8, LANES), F32), pltpu.VMEM((blk, 8, LANES), F32)],
            [pltpu.SemaphoreType.DMA((dp,)), pltpu.SemaphoreType.DMA((blk,))],
            [pltpu.SemaphoreType.DMA((dp,)), pltpu.SemaphoreType.DMA((blk,))],
        ],
        compiler_params=pltpu.CompilerParams(collective_id=cid, has_side_effects=True, vmem_limit_bytes=LIMIT),
        name="back",
    )(merged, output, expand_share, shrink_share, dlt)


def key_columns(kept_time, kept_bands, blocks, own, segment, padded):
    clips = kept_time.shape[0] // blocks
    kept_time = lax.dynamic_slice_in_dim(kept_time, own * clips, clips)
    kept_bands = lax.dynamic_slice_in_dim(kept_bands, own * clips, clips)
    columns = kept_time.shape[1] // blocks
    patches = kept_time.reshape(clips, blocks, columns, 1) * kept_bands[:, None, None, :]
    patches = patches.reshape(clips, blocks, columns * kept_bands.shape[1])
    leading = (jnp.arange(blocks, dtype=jnp.int32) == 0).astype(jnp.int32)
    special = jnp.broadcast_to(leading[None, :, None], (clips, blocks, segment - patches.shape[2]))
    live = jnp.concatenate([special, patches, jnp.zeros((clips, blocks, padded - segment), jnp.int32)], 2)
    bias = jnp.where(live > 0, 0.0, -1e30).reshape(-1, 1)
    lane = jnp.arange(LANES, dtype=jnp.int32)[None, :] % HALF
    return jnp.where(lane == 0, bias, jnp.where(lane < 4, 1.0, 0.0)).astype(BF16)


def prepare_kernel(tok_ref, cot_ref, xc_ref, low_ref):
    segment, extra = tok_ref.shape[1], xc_ref.shape[1] - tok_ref.shape[1]
    values = tok_ref[...]
    centred = (values - jnp.mean(values, -1, keepdims=True)).astype(BF16)
    blank = jnp.zeros((values.shape[0], extra, values.shape[2]), BF16)
    xc_ref[...] = jnp.concatenate([centred, blank], 1)
    low_ref[...] = jnp.concatenate([cot_ref[...].astype(BF16), blank], 1)


def prepare(tokens, cotangent, padded):
    clips, segment, width = tokens.shape
    wide = pl.BlockSpec((2, segment, width), lambda i: (i, 0, 0))
    out = pl.BlockSpec((2, padded, width), lambda i: (i, 0, 0))
    shape = jax.ShapeDtypeStruct((clips, padded, width), BF16)
    return pl.pallas_call(
        prepare_kernel, grid=(clips // 2,), in_specs=[wide, wide], out_specs=[out, out], out_shape=[shape, shape],
        compiler_params=pltpu.CompilerParams(dimension_semantics=("arbitrary",), vmem_limit_bytes=LIMIT),
        name="prepare")(tokens, cotangent)


def finish_kernel(tok_ref, cot_ref, act_ref, dlt_ref, out_ref, grad_ref):
    segment = tok_ref.shape[1]
    out_ref[...] = tok_ref[...] + act_ref[...].astype(F32)[:, :segment]
    grad_ref[...] = cot_ref[...] + dlt_ref[...].astype(F32)[:, :segment]


def finish(tokens, cotangent, act, dlt):
    clips, segment, width = tokens.shape
    wide = pl.BlockSpec((2, segment, width), lambda i: (i, 0, 0))
    low = pl.BlockSpec((2,) + act.shape[1:], lambda i: (i, 0, 0))
    shape = jax.ShapeDtypeStruct(tokens.shape, F32)
    return pl.pallas_call(
        finish_kernel, grid=(clips // 2,), in_specs=[wide, wide, low, low], out_specs=[wide, wide],
        out_shape=[shape, shape],
        compiler_params=pltpu.CompilerParams(dimension_semantics=("arbitrary",), vmem_limit_bytes=LIMIT),
        name="finish")(tokens, cotangent, act, dlt)


RATES = (MATRIX_RATE, MATRIX_RATE, MATRIX_RATE, MATRIX_RATE, VECTOR_RATE)
DECAYS = (MATRIX_DECAY, MATRIX_DECAY, MATRIX_DECAY, MATRIX_DECAY, 0.0)


def adamw_kernel(norm_ref, *refs):
    weights, firsts, seconds, shares = refs[:5], refs[5:10], refs[10:15], refs[15:20]
    outs = refs[20:]
    factor = CLIP_LIMIT / jnp.maximum(jnp.sqrt(norm_ref[0:1, 0:1]), CLIP_LIMIT)
    for index in range(5):
        clipped = shares[index][...] * factor
        weight = weights[index][...]
        momentum = BETA_ONE * firsts[index][...] + (1.0 - BETA_ONE) * clipped
        variance = BETA_TWO * seconds[index][...] + (1.0 - BETA_TWO) * clipped * clipped
        mean_hat = momentum / (1.0 - BETA_ONE**STEP)
        var_hat = variance / (1.0 - BETA_TWO**STEP)
        updated = weight - RATES[index] * (
            mean_hat / (jnp.sqrt(var_hat) + ADAM_EPS) + DECAYS[index] * weight)
        for kind, value in enumerate((clipped, momentum, variance, updated)):
            outs[5 * kind + index][...] = value


def adamw(norm, weights, firsts, seconds, shares):
    inside = pl.BlockSpec(memory_space=pltpu.VMEM)
    return pl.pallas_call(
        adamw_kernel, in_specs=[inside] * 21, out_specs=[inside] * 20,
        out_shape=[jax.ShapeDtypeStruct(w.shape, F32) for w in weights] * 4,
        compiler_params=pltpu.CompilerParams(vmem_limit_bytes=LIMIT),
        name="adamw")(norm, *weights, *firsts, *seconds, *shares)


def shards(
    tokens, kept_time, kept_bands, cotangent,
    weight_merged, weight_output, weight_expand, weight_shrink, vectors,
    first_merged, first_output, first_expand, first_shrink, first_vectors,
    second_merged, second_output, second_expand, second_shrink, second_vectors,
):
    clip_count, segment, width = tokens.shape
    dp, blk = lax.axis_size("dp"), lax.axis_size("blk")
    own = lax.axis_index("blk")
    clips = clip_count // blk
    padded = -(-segment // 16) * 16
    total = clips * blk * padded
    rows = weight_merged.shape[0]
    ff = weight_expand.shape[1]
    cube = (2,) * (bits_of(dp) + bits_of(blk))

    columns = jnp.pad(vectors.T, ((0, 0), (0, LANES - vectors.shape[0])))
    merged_low = jnp.concatenate([weight_merged, columns], 1).astype(BF16)
    wide_low = jnp.concatenate([weight_output, weight_expand], 1).astype(BF16)
    xc_home, cot_home = prepare(tokens, cotangent, padded)
    shrink_low = weight_shrink.astype(BF16)
    merged, xc = front(merged_low, xc_home, dp, blk, 0)
    merged = merged.reshape(width, merged_low.shape[1])
    xc = xc.reshape(total, width)
    vec = merged[:, 3 * width:3 * width + vectors.shape[0]].T.astype(F32)
    dead = key_columns(kept_time, kept_bands, blk, own, segment, padded)
    n1, qa, kv, mix, wide, shrink, cot = attn_fwd(
        xc, dead, merged, vec, wide_low, shrink_low, cot_home, clips, HEADS, dp, blk, 1)
    wide = wide.reshape(width, wide_low.shape[1])
    shrink = shrink.reshape(ff, width)
    cot = cot.reshape(total, width)
    act, dmid, grad_expand, grad_shrink, early = ffn(mix, xc, cot, wide, shrink, vec, blk * padded)

    def by_device(grad):
        return grad.reshape(cube + (grad.shape[0] // (dp * blk), grad.shape[1]))

    sent = (clips, blk, padded, width)
    dlt, grad_merged, grad_output, expand_share, shrink_share, act_home = attn_bwd(
        xc, cot, dmid, dead, n1, qa, kv, mix, merged, wide, vec, early,
        by_device(grad_expand), by_device(grad_shrink), act.reshape(sent), clips, HEADS, dp, blk, 2)
    merged_share, output_share, norm, dlt_home = back(
        by_device(grad_merged), by_device(grad_output), expand_share, shrink_share, dlt.reshape(sent), dp, blk, 3)
    shares = [merged_share, output_share, expand_share, shrink_share]
    activations, token_grads = finish(tokens, cotangent, act_home, dlt_home)
    shares.append(shares[0][:, 3 * width:3 * width + vectors.shape[0]].T)
    shares[0] = shares[0][:, :3 * width]
    steps_out = adamw(
        norm, (weight_merged, weight_output, weight_expand, weight_shrink, vectors),
        (first_merged, first_output, first_expand, first_shrink, first_vectors),
        (second_merged, second_output, second_expand, second_shrink, second_vectors), shares)
    return (activations, token_grads, jnp.sqrt(norm[0, 0]), *steps_out)


def solution(mesh):
    return jax.shard_map(
        shards,
        mesh=mesh,
        in_specs=(
            P("dp", "blk", None),
            P("dp", None),
            P("dp", None),
            P("dp", "blk", None),
            P(("dp", "blk"), None),
            P(("dp", "blk"), None),
            P(("dp", "blk"), None),
            P(("dp", "blk"), None),
            P(None, ("dp", "blk")),
            P(("dp", "blk"), None),
            P(("dp", "blk"), None),
            P(("dp", "blk"), None),
            P(("dp", "blk"), None),
            P(None, ("dp", "blk")),
            P(("dp", "blk"), None),
            P(("dp", "blk"), None),
            P(("dp", "blk"), None),
            P(("dp", "blk"), None),
            P(None, ("dp", "blk")),
        ),
        out_specs=(
            P("dp", "blk", None),
            P("dp", "blk", None),
            P(),
            P(("dp", "blk"), None),
            P(("dp", "blk"), None),
            P(("dp", "blk"), None),
            P(("dp", "blk"), None),
            P(None, ("dp", "blk")),
            P(("dp", "blk"), None),
            P(("dp", "blk"), None),
            P(("dp", "blk"), None),
            P(("dp", "blk"), None),
            P(None, ("dp", "blk")),
            P(("dp", "blk"), None),
            P(("dp", "blk"), None),
            P(("dp", "blk"), None),
            P(("dp", "blk"), None),
            P(None, ("dp", "blk")),
            P(("dp", "blk"), None),
            P(("dp", "blk"), None),
            P(("dp", "blk"), None),
            P(("dp", "blk"), None),
            P(None, ("dp", "blk")),
        ),
        check_vma=False,
    )
```

```python
import functools
import jax
import jax.numpy as jnp
from jax import lax
from jax.experimental import pallas as pl
from jax.experimental.pallas import tpu as pltpu
from jax.sharding import PartitionSpec as P

HEADS = 12
STEP = 5
CLIP_LIMIT = 1.0
BETA_ONE = 0.5
BETA_TWO = 0.5
ADAM_EPS = 1e-08
MATRIX_RATE = 0.1
VECTOR_RATE = 0.3
MATRIX_DECAY = 0.05

F32, BF16 = jnp.float32, jnp.bfloat16
EPS = 1e-06
HALF = 64
LANES = 128
LIMIT = 127 * 512 * 1024
MESH = pl.DeviceIdType.MESH

FWD_PLAN = {1: [0, 2], 2: [1, 4], 4: [-1, 3], 5: [2], 6: [0, 1], 7: [-2], 10: [3, 4], 12: [0, 1], 14: [3], 15: [2],
            16: [4], -1: [-3, 1, 0, 3, 2, 4, 1, 0, 3, 2, 4]}
FF_CHUNKS = 4
FFN_LETTERS = ["aXYb", "aYXb"]
FFN_ROOTS = ["XY", "XY"]
FFN_PLAN = {8: [0, 2], 11: [0, 2], 13: [0, 2], 14: [1, 3], 15: [0], 17: [2, 3], 18: [1], 19: [0, 3], 20: [1], 22: [1],
            23: [3], -1: [1]}
BWD_LETTERS = ["YbaX", "bYaX", "aYbX"]
BWD_ROOTS = ["YX", "XY"]
BWD_PLAN = {0: [-1], 2: [0, 1, 2, 3, 4], 5: [-2], 6: [0, 4], 7: [1, 2, 3], 9: [4, -3], 11: [0, 1], 12: [2],
            13: [4, 0, 3], 14: [1], 15: [2], -1: [3, 0, 1, 2]}


def nn(a, b):
    return lax.dot_general(a, b, (((1,), (0,)), ((), ())), preferred_element_type=F32)


def nt(a, b):
    return lax.dot_general(a, b, (((1,), (1,)), ((), ())), preferred_element_type=F32)


def tn(a, b):
    return lax.dot_general(a, b, (((0,), (0,)), ((), ())), preferred_element_type=F32)


def norm_stats(v):
    centre = jnp.mean(v, -1, keepdims=True)
    c = v - centre
    spread = jnp.mean(c * c, -1, keepdims=True)
    r = lax.rsqrt(spread + EPS)
    return c * r, r


def norm_back(xhat, r, dy, gain):
    dx = dy * gain
    m1 = jnp.mean(dx, -1, keepdims=True)
    m2 = jnp.mean(dx * xhat, -1, keepdims=True)
    return (dx - m1 - xhat * m2) * r


def gelu_pair(x):
    z = jnp.abs(x)
    t = 1.0 / (1.0 + 0.3275911 * 0.7071067811865476 * z)
    e = jnp.exp(-0.5 * x * x)
    poly = t * (0.127414796 + t * (-0.142248368 + t * (0.7107068705 + t * (-0.7265760135 + t * 0.5307027145))))
    tail = poly * e
    phi = jnp.where(x >= 0, 1.0 - tail, tail)
    return x * phi, phi + (0.3989422804014327 * x) * e


def ffn_kernel(cube, letters, plan, mix_ref, xc_ref, cot_ref, prj_ref, exp_ref, shr_ref, vec_ref,
               act_ref, dmid_ref, ge_ref, gs_ref, go_ref, sums_ref, share_ref, shrink_ref,
               n2_s, y_s, dn_s, ae_s, as_s, ao_s, *refs):
    f, i = pl.program_id(0), pl.program_id(1)
    nf, ni = pl.num_programs(0), pl.num_programs(1)
    rows, width = mix_ref.shape
    here = pl.ds(pl.multiple_of(i * rows, rows), rows)
    cube.bind()
    n_p = len(letters)
    ready, held = refs[:n_p], refs[n_p:2 * n_p]
    landed = [refs[2 * n_p + k * cube.count:2 * n_p + (k + 1) * cube.count] for k in range(n_p)]
    refs = refs[n_p * (2 + cube.count):]
    send, recv, local = refs[:3]
    gs_ready, refs = refs[3:3 + n_p], refs[3 + n_p:]
    reduces = [Reduce(cube, ready[k], slice(None), letters[k], held[k], landed[k],
                      share_ref.at[:, pl.ds(k * width, width)], send.at[k], recv.at[k], local.at[k])
               for k in range(n_p)]
    reduces += root_reduces(cube, gs_ready, range(n_p), FF_CHUNKS, FFN_ROOTS, shrink_ref, refs)
    points = Points(plan, reduces, None)

    @pl.when((f == 0) & (i == 0))
    def _():
        cube.barrier()
        shrink_ref[...] = jnp.zeros_like(shrink_ref)
        sums_ref[...] = jnp.zeros_like(sums_ref)

    @pl.when(f == 0)
    def _():
        mid = xc_ref[...].astype(F32) + nn(mix_ref[...], prj_ref[...]) + vec_ref[4:5, :]
        xhat, _ = norm_stats(mid)
        n2_s[here, :] = (xhat * vec_ref[5:6, :] + vec_ref[6:7, :]).astype(BF16)

    points.visit(2 * (f * ni + i), 0)
    n2 = n2_s[here, :]
    d2 = cot_ref[...]
    h = nn(n2, exp_ref[...]) + vec_ref[pl.ds(8 + f, 1), :]
    dg = nt(d2, shr_ref[...])
    g, gp = gelu_pair(h)
    g = g.astype(BF16)
    dh32 = gp * dg
    dh = dh32.astype(BF16)
    sums_ref[pl.ds(8 + f, 1), :] += jnp.sum(dh32, 0, keepdims=True)
    y = nn(g, shr_ref[...])
    dn = nt(dh, exp_ref[...])

    @pl.when(f == 0)
    def _():
        y_s[here, :] = y
        dn_s[here, :] = dn

    @pl.when(f > 0)
    def _():
        y_s[here, :] += y
        dn_s[here, :] += dn

    points.visit(2 * (f * ni + i) + 1, 1)
    ge = tn(n2, dh)
    gs = tn(g, d2)

    @pl.when(i == 0)
    def _():
        ae_s[...] = ge
        as_s[...] = gs

    @pl.when((i > 0) & (i < ni - 1))
    def _():
        ae_s[...] += ge
        as_s[...] += gs

    @pl.when(i == ni - 1)
    def _():
        full_s = (as_s[...] + gs).astype(BF16)
        full = (ae_s[...] + ge).astype(BF16)
        for chunk in range(n_p):
            @pl.when(f == chunk)
            def _():
                ready[chunk][...] = full.reshape(ready[chunk].shape)
                reduces[chunk].start()
                gs_ready[chunk][...] = full_s.reshape(gs_ready[chunk].shape)
                reduces[n_p + chunk].start()

        @pl.when(f >= n_p)
        def _():
            ge_ref[...] = full
            gs_ref[...] = full_s

    @pl.when(f == nf - 1)
    def _():
        mix = mix_ref[...]
        delta = nn(mix, prj_ref[...]) + vec_ref[4:5, :]
        mid = xc_ref[...].astype(F32) + delta
        cot = d2.astype(F32)
        xhat, r = norm_stats(mid)
        dy = dn_s[here, :]
        act_ref[...] = (delta + (y_s[here, :] + vec_ref[7:8, :])).astype(BF16)
        dmid = cot + norm_back(xhat, r, dy, vec_ref[5:6, :])
        dmid_ref[...] = dmid
        d_one = dmid.astype(BF16)
        sums_ref[4:5, :] += jnp.sum(d_one.astype(F32), 0, keepdims=True)
        go = tn(mix, d_one)

        @pl.when(i == 0)
        def _():
            ao_s[...] = go

        @pl.when(i > 0)
        def _():
            ao_s[...] += go

        @pl.when(i == ni - 1)
        def _():
            go_ref[...] = ao_s[...].astype(BF16)

        sums_ref[5:6, :] += jnp.sum(dy * xhat, 0, keepdims=True)
        sums_ref[6:7, :] += jnp.sum(dy, 0, keepdims=True)
        sums_ref[7:8, :] += jnp.sum(cot, 0, keepdims=True)

    @pl.when((f == nf - 1) & (i == ni - 1))
    def _():
        points.finish()


def ffn(mix, xc, cot, expand, shrink, vec, rows, dp, blk, cid):
    total, width = xc.shape
    cube = Cube(dp, blk)
    ff = expand.shape[1] - width
    nf, ni = ff // width, total // rows
    letters = FFN_LETTERS
    early = len(letters)
    chunk = (width // (dp * blk), width)
    own = (ff // (dp * blk), width)
    first = lambda f, i: (jnp.where((f == 0) | (f == nf - 1), i, ni - 1), 0)
    last = lambda f, i: (jnp.where(f == nf - 1, i, 0), 0)
    once = pl.Buffered(1)
    whole = lambda f, i: (0, 0)
    return pl.pallas_call(
        functools.partial(ffn_kernel, cube, letters, FFN_PLAN),
        grid=(nf, ni),
        in_specs=[
            pl.BlockSpec((rows, width), first),
            pl.BlockSpec((rows, width), first),
            pl.BlockSpec((rows, width), lambda f, i: (i, 0)),
            pl.BlockSpec((width, width), whole, pipeline_mode=once),
            pl.BlockSpec((width, width), lambda f, i: (0, f + 1)),
            pl.BlockSpec((width, width), lambda f, i: (f, 0)),
            pl.BlockSpec(vec.shape, whole),
        ],
        out_specs=[
            pl.BlockSpec((rows, width), last),
            pl.BlockSpec((rows, width), last),
            pl.BlockSpec((width, width), lambda f, i: (0, jnp.maximum(f - early, 0)), pipeline_mode=once),
            pl.BlockSpec((width, width), lambda f, i: (jnp.maximum(f - early, 0), 0), pipeline_mode=once),
            pl.BlockSpec((width, width), whole, pipeline_mode=once),
            pl.BlockSpec((16, width), whole),
            pl.BlockSpec((chunk[0], width * early), whole, pipeline_mode=once),
            pl.BlockSpec(own, whole, pipeline_mode=once),
        ],
        out_shape=[
            jax.ShapeDtypeStruct((total, width), BF16),
            jax.ShapeDtypeStruct((total, width), F32),
            jax.ShapeDtypeStruct((width, ff - early * width), BF16),
            jax.ShapeDtypeStruct((ff - early * width, width), BF16),
            jax.ShapeDtypeStruct((width, width), BF16),
            jax.ShapeDtypeStruct((16, width), F32),
            jax.ShapeDtypeStruct((chunk[0], width * early), F32),
            jax.ShapeDtypeStruct(own, F32),
        ],
        scratch_shapes=[
            pltpu.VMEM((total, width), BF16),
            pltpu.VMEM((total, width), F32),
            pltpu.VMEM((total, width), F32),
            pltpu.VMEM((width, width), F32),
            pltpu.VMEM((width, width), F32),
            pltpu.VMEM((width, width), F32),
        ] + [pltpu.VMEM((2,) * cube.count + chunk, BF16) for _ in letters]
        + reduce_scratch(cube, [chunk] * early)
        + [pltpu.VMEM((2,) * (cube.count - bits_of(FF_CHUNKS)) + own, BF16) for _ in letters]
        + root_scratch(cube, early, FF_CHUNKS, own),
        compiler_params=pltpu.CompilerParams(
            dimension_semantics=("arbitrary", "arbitrary"), vmem_limit_bytes=LIMIT, collective_id=cid,
            has_side_effects=True),
        name="ffn",
    )(mix, xc, cot, expand, expand, shrink, vec)


def attn_fwd_kernel(cube, parts, plan, heads, xc_ref, dead_ref, mrg_ref, vec_ref, wide_in, shrink_in, cot_in,
                    n1_ref, qa_ref, kv_ref, mix_ref, wide_out, shrink_out, cot_out,
                    pk_s, send, recv, local, t_send, t_recv, t_local):
    width = xc_ref.shape[1]
    seq = xc_ref.shape[0]
    pairs = heads // 2
    cube.bind()
    clip = pl.program_id(0)
    own = [pltpu.make_async_copy(wide_in, wide_out.at[tuple(cube.mine)], local.at[0]),
           pltpu.make_async_copy(shrink_in, shrink_out.at[tuple(cube.mine)], local.at[1])]
    gathers = [Gather(cube, (wide_in, shrink_in)[a], (wide_out, shrink_out)[a], pl.ds(first, size), letters,
                      send.at[n], recv.at[n]) for n, (a, first, size, letters) in enumerate(parts)]
    exchange = Exchange(cube, cot_in, cot_out, False, t_send, t_recv, t_local)
    points = Points(plan, gathers, exchange)

    @pl.when(clip == 0)
    def _():
        cube.barrier()
        for gather in gathers:
            gather.start()
        for copy in own:
            copy.start()
        for copy in own:
            copy.wait()

    xc = xc_ref[...].astype(F32)
    xhat, _ = norm_stats(xc)
    n1 = (xhat * vec_ref[0:1, :] + vec_ref[1:2, :]).astype(BF16)
    n1_ref[...] = n1
    for third in range(3):
        cols = pl.ds(third * width, width)
        part = nn(n1, mrg_ref[:, cols])
        if third != 1:
            part = part + vec_ref[2 + third // 2:3 + third // 2, :]
        part = part.astype(BF16)
        pk_s[:, cols] = part
        if third:
            kv_ref[:, pl.ds((third - 1) * width, width)] = part
    lane = lax.broadcasted_iota(jnp.int32, (seq, LANES), 1)
    low = lane < HALF
    in_half = lane % HALF
    dead = dead_ref[...]
    ones = jnp.ones((seq, LANES), BF16)

    def pair(p, _):
        points.visit(clip * pairs + p)
        qcols = pl.ds(pl.multiple_of(p * LANES, LANES), LANES)
        kcols = pl.ds(pl.multiple_of(width + p * LANES, LANES), LANES)
        vcols = pl.ds(pl.multiple_of(2 * width + p * LANES, LANES), LANES)
        q = pk_s[:, qcols] * jnp.array(0.125, BF16)
        k = pk_s[:, kcols]
        v = pk_s[:, vcols]
        outs = []
        for side in range(2):
            mine = low if side == 0 else ~low
            qs = jnp.where(mine, q, jnp.where(in_half == 0, 1.0, 0.0).astype(BF16))
            ks = jnp.where(mine, k, dead)
            vs = jnp.where(mine, v, ones)
            s = nt(qs, ks)
            top = jnp.max(s, -1, keepdims=True)
            e = jnp.exp(s - top).astype(BF16)
            o = nn(e, vs)
            swapped = pltpu.roll(o, HALF, 1)
            outs.append(o / swapped)
            lse = top + jnp.log(jnp.where(mine, swapped, o))
            hi = (-lse).astype(BF16)
            rest = -lse - hi.astype(F32)
            mid_part = rest.astype(BF16)
            lo = (rest - mid_part.astype(F32)).astype(BF16)
            extra = jnp.where(in_half == 0, 1.0, 0.0).astype(BF16)
            extra = jnp.where(in_half == 1, hi, extra)
            extra = jnp.where(in_half == 2, mid_part, extra)
            extra = jnp.where(in_half == 3, lo, extra)
            qa_ref[2 * p + side] = jnp.where(mine, q, extra)
        mix_ref[:, qcols] = jnp.where(low, outs[0], outs[1]).astype(BF16)
        return 0

    lax.fori_loop(0, pairs, pair, 0)

    @pl.when(clip == pl.num_programs(0) - 1)
    def _():
        points.finish()
        for part in range(exchange.clips):
            exchange.wait(part)


class Points:
    def __init__(self, plan, movers, exchange):
        self.movers, self.exchange = movers, exchange
        self.plan, taken = {}, {}
        for point in sorted(plan, key=lambda p: p if p >= 0 else 1 << 20):
            self.plan[point] = []
            for which in plan[point]:
                self.plan[point].append((which, taken.get(which, 0)))
                taken[which] = taken.get(which, 0) + 1

    def act(self, point):
        for which, step in self.plan[point]:
            if which < 0:
                self.exchange.start(-1 - which)
            else:
                self.movers[which].advance(step)

    def visit(self, now, parity=None):
        for point in self.plan:
            if point < 0 or (parity is not None and point % 2 != parity):
                continue

            @pl.when(now == point)
            def _():
                self.act(point)

    def finish(self):
        self.act(-1)


def attn_fwd(xc, dead, merged, vec, wide, shrink, cot, clips, heads, dp, blk, cid):
    total, width = xc.shape
    seq = total // clips
    cube = Cube(dp, blk)
    whole = lambda c: (0, 0)
    row = lambda c: (c, 0)
    anywhere = pl.BlockSpec(memory_space=pl.ANY)
    third, half = wide.shape[1] // 3, shrink.shape[1] // 2
    parts = [(0, 0, third, "XbYa"), (0, third, third, "baXY"), (0, 2 * third, third, "YXba"),
             (1, 0, half, "baYX"), (1, half, half, "XbaY")]
    return pl.pallas_call(
        functools.partial(attn_fwd_kernel, cube, parts, FWD_PLAN, heads),
        grid=(clips,),
        in_specs=[
            pl.BlockSpec((seq, width), row),
            pl.BlockSpec((seq, LANES), row),
            pl.BlockSpec(merged.shape, whole),
            pl.BlockSpec(vec.shape, whole),
            pl.BlockSpec(wide.shape, whole),
            pl.BlockSpec(shrink.shape, whole),
            anywhere,
        ],
        out_specs=[
            pl.BlockSpec((seq, width), row),
            pl.BlockSpec((heads, seq, LANES), lambda c: (0, c, 0)),
            pl.BlockSpec((seq, 2 * width), row),
            pl.BlockSpec((seq, width), row),
            anywhere, anywhere, anywhere,
        ],
        out_shape=[
            jax.ShapeDtypeStruct((total, width), BF16),
            jax.ShapeDtypeStruct((heads, total, LANES), BF16),
            jax.ShapeDtypeStruct((total, 2 * width), BF16),
            jax.ShapeDtypeStruct((total, width), BF16),
            jax.ShapeDtypeStruct((2,) * cube.count + wide.shape, BF16),
            jax.ShapeDtypeStruct((2,) * cube.count + shrink.shape, BF16),
            jax.ShapeDtypeStruct((clips, blk) + cot.shape[1:], BF16),
        ],
        scratch_shapes=[
            pltpu.VMEM((seq, 3 * width), BF16),
            pltpu.SemaphoreType.DMA((len(parts), cube.count)),
            pltpu.SemaphoreType.DMA((len(parts), cube.count)),
            pltpu.SemaphoreType.DMA((2,)),
        ] + exchange_semaphores(clips, blk),
        compiler_params=pltpu.CompilerParams(
            dimension_semantics=("arbitrary",), vmem_limit_bytes=LIMIT, collective_id=cid, has_side_effects=True),
        name="attn_fwd",
    )(xc, dead, merged, vec, wide, shrink, cot)


def attn_bwd_kernel(cube, late, tail, plan, heads, xc_ref, cot_ref, dmid_ref, dead_ref, n1_ref, qa_ref, kv_ref, mix_ref,
                    mrg_ref, out_ref, vec_ref, early_ref, ge_early, gs_early,
                    ge_in, gs_in, go_in, act_in,
                    gm_out, gv_out, go_out, ge_out, gs_out, norm_ref, act_out, dlt_out,
                    dm_s, dp_s, am_s, gm_s, gl_s, gw_s, gx_s, dlt_s, sums_ref, *refs):
    c = pl.program_id(0)
    n = pl.num_programs(0)
    seq, width = xc_ref.shape
    pairs = heads // 2
    cube.bind()

    def take(count):
        nonlocal refs
        taken, refs = refs[:count], refs[count:]
        return taken

    def sums_of(parts, sources, outs):
        count = len(parts)
        held = take(count)
        landed = [take(cube.count) for _ in parts]
        send, recv, local = take(3)
        return [Reduce(cube, sources[a], pl.ds(first, size), letters, held[m], landed[m], outs[a],
                       send.at[m], recv.at[m], local.at[m]) for m, (a, first, size, letters) in enumerate(parts)]

    reduces = sums_of(late, (ge_in, go_in), (gx_s, go_out))
    roots = FF_CHUNKS - gs_in.shape[0]
    count = gs_in.shape[0]
    reduces += root_reduces(cube, [gs_in.at[m] for m in range(count)], range(roots, FF_CHUNKS), FF_CHUNKS, BWD_ROOTS,
                            gl_s, take(4 * count + count * (cube.count - bits_of(FF_CHUNKS)) - count + 3))
    ends = sums_of(tail, (gm_s,), (gw_s,))
    exchange = Exchange(cube, act_in, act_out, True, *take(3))
    homeward = Exchange(cube, dlt_s, dlt_out, True, *take(3))
    sums, s_send, s_recv = refs
    points = Points(plan, reduces, exchange)

    @pl.when(c == 0)
    def _():
        cube.barrier()
        for reduce in reduces:
            reduce.start()
        gl_s[...] = jnp.zeros_like(gl_s)
        sums_ref[...] = early_ref[...]
        am_s[...] = jnp.zeros_like(am_s)

    d_one = dmid_ref[...].astype(BF16)
    dm_s[...] = nt(d_one, out_ref[...]).astype(BF16)

    lane = lax.broadcasted_iota(jnp.int32, (seq, LANES), 1)
    low = lane < HALF
    in_half = lane % HALF
    dead = dead_ref[...]
    vone = jnp.where(in_half < 2, 1.0, 0.0).astype(BF16)

    def pair(p, _):
        points.visit(c * pairs + p)
        qcols = pl.ds(pl.multiple_of(p * LANES, LANES), LANES)
        kcols = pl.ds(pl.multiple_of(width + p * LANES, LANES), LANES)
        vcols = pl.ds(pl.multiple_of(2 * width + p * LANES, LANES), LANES)
        k = kv_ref[:, qcols]
        v = kv_ref[:, kcols]
        dm = dm_s[:, qcols]
        prod = dm.astype(F32) * mix_ref[:, qcols].astype(F32)
        k_t = jnp.transpose(k)
        dks, dvs, dqs = [], [], []
        for side in range(2):
            mine = low if side == 0 else ~low
            qa = qa_ref[2 * p + side]
            ka = jnp.where(mine, k, dead)
            va = jnp.where(mine, v, vone)
            dd = -jnp.sum(jnp.where(mine, prod, 0.0), -1, keepdims=True)
            hi = dd.astype(BF16)
            lo = (dd - hi.astype(F32)).astype(BF16)
            da = jnp.where(mine, dm, jnp.where(in_half == 0, hi, lo))
            p_t = jnp.exp(nt(ka, qa))
            ds_t = (p_t * nt(va, da)).astype(BF16)
            dvs.append(nn(p_t.astype(BF16), da))
            dks.append(nn(ds_t, qa))
            dqs.append(nn(k_t[side * HALF:(side + 1) * HALF, :], ds_t))
        dq = jnp.transpose(jnp.concatenate(dqs, 0)) * 0.125
        dk = jnp.where(low, dks[0], dks[1])
        dv = jnp.where(low, dvs[0], dvs[1])
        sums_ref[2:3, qcols] += jnp.sum(dq, 0, keepdims=True)
        sums_ref[3:4, qcols] += jnp.sum(dv, 0, keepdims=True)
        dp_s[:, qcols] = dq.astype(BF16)
        dp_s[:, kcols] = dk.astype(BF16)
        dp_s[:, vcols] = dv.astype(BF16)
        return 0

    lax.fori_loop(0, pairs, pair, 0)
    dp = dp_s[...]
    am_s[...] += tn(n1_ref[...], dp)

    def by_device(values):
        return values.astype(BF16).reshape((2,) * cube.count + (width // (1 << cube.count), values.shape[1]))

    def hand_over(first, size):
        def some(m, _):
            cols = pl.ds(pl.multiple_of(first + m * LANES, LANES), LANES)
            gm_s[(slice(None),) * (cube.count + 1) + (cols,)] = by_device(am_s[:, cols])
            return 0

        lax.fori_loop(0, size // LANES, some, 0)

    @pl.when(c == n - 1)
    def _():
        for m, (_, first, size, _) in enumerate(tail[:-1]):
            hand_over(first, size)
            ends[m].start()

    dy = nt(dp, mrg_ref[:, :3 * width])
    xhat, r = norm_stats(xc_ref[...].astype(F32))
    sums_ref[0:1, :] += jnp.sum(dy * xhat, 0, keepdims=True)
    sums_ref[1:2, :] += jnp.sum(dy, 0, keepdims=True)
    delta = ((dmid_ref[...] - cot_ref[...].astype(F32)) + norm_back(xhat, r, dy, vec_ref[0:1, :])).astype(BF16)
    dlt_s[c] = delta.reshape(dlt_s.shape[1:])
    for clip in range(homeward.clips):
        @pl.when(c == clip)
        def _():
            homeward.start(clip)

    @pl.when(c == n - 1)
    def _():
        _, first, size, _ = tail[-1]
        hand_over(first, 3 * width - first)
        columns = jnp.transpose(sums_ref[...])
        blank = jnp.zeros((width, LANES - columns.shape[1]), F32)
        gm_s[(slice(None),) * (cube.count + 1) + (pl.ds(3 * width, LANES),)] = by_device(
            jnp.concatenate([columns, blank], 1))
        ends[-1].start()
        points.finish()
        shrink = gs_early[...] + gl_s[...]
        gs_out[...] = shrink
        part = ge_early.shape[1]
        ge_out[:, :part] = ge_early[...]
        ge_out[:, part:] = gx_s[...]
        total = jnp.sum(shrink * shrink) + jnp.sum(go_out[...] * go_out[...])
        total = total + jnp.sum(ge_early[...] * ge_early[...]) + jnp.sum(gx_s[...] * gx_s[...])
        for step in range(len(ends[0].steps)):
            for end in ends:
                end.advance(step)
        gm_out[...] = gw_s[:, :3 * width]
        gv_out[...] = gw_s[:, 3 * width:]
        total = total + jnp.sum(gw_s[...] * gw_s[...])
        norm_ref[...] = sum_everywhere(cube, total, sums, s_send, s_recv)
        for clip in range(homeward.clips):
            exchange.wait(clip)
            homeward.wait(clip)


def attn_bwd(xc, cot, dmid, dead, n1, qa, kv, mix, merged, output, vec, early, expand_early, shrink_early,
             grad_expand, grad_shrink, grad_output, act, clips, heads, dp, blk, cid):
    total, width = xc.shape
    seq = total // clips
    cube = Cube(dp, blk)
    whole = lambda c: (0, 0)
    row = lambda c: (c, 0)
    once = pl.Buffered(1)
    anywhere = pl.BlockSpec(memory_space=pl.ANY)
    rows, own = grad_expand.shape[-2], grad_shrink.shape[-2:]
    half = grad_expand.shape[-1] // 2
    third = merged.shape[1] // LANES // 3 * LANES
    late = [(0, 0, half, BWD_LETTERS[0]), (0, half, half, BWD_LETTERS[1]), (1, 0, width, BWD_LETTERS[2])]
    tail = [(0, 0, merged.shape[1] - 2 * third, "aYbX"), (0, merged.shape[1] - 2 * third, third, "XaYb"),
            (0, merged.shape[1] - third, third, "YbaX")]
    fixed = [(rows, 3 * width), (rows, merged.shape[1] - 3 * width), (rows, width),
             (rows, expand_early.shape[1] + 2 * half), own, (8, LANES)]
    home = (clips * blk,) + act.shape[2:]
    return pl.pallas_call(
        functools.partial(attn_bwd_kernel, cube, late, tail, BWD_PLAN, heads),
        grid=(clips,),
        in_specs=[
            pl.BlockSpec((seq, width), row),
            pl.BlockSpec((seq, width), row),
            pl.BlockSpec((seq, width), row),
            pl.BlockSpec((seq, LANES), row),
            pl.BlockSpec((seq, width), row),
            pl.BlockSpec((heads, seq, LANES), lambda c: (0, c, 0)),
            pl.BlockSpec((seq, 2 * width), row),
            pl.BlockSpec((seq, width), row),
            pl.BlockSpec(merged.shape, whole, pipeline_mode=once),
            pl.BlockSpec((width, width), whole, pipeline_mode=once),
            pl.BlockSpec(vec.shape, whole),
            pl.BlockSpec(early.shape, whole),
            pl.BlockSpec(expand_early.shape, whole, pipeline_mode=once),
            pl.BlockSpec(shrink_early.shape, whole, pipeline_mode=once),
            anywhere, anywhere, anywhere, anywhere,
        ],
        out_specs=[pl.BlockSpec(s, whole, pipeline_mode=once) for s in fixed] + [anywhere, anywhere],
        out_shape=[jax.ShapeDtypeStruct(s, F32) for s in fixed] + [jax.ShapeDtypeStruct(home, BF16)] * 2,
        scratch_shapes=[
            pltpu.VMEM((seq, width), BF16),
            pltpu.VMEM((seq, 3 * width), BF16),
            pltpu.VMEM((width, 3 * width), F32),
            pltpu.VMEM((2,) * cube.count + (rows, merged.shape[1]), BF16),
            pltpu.VMEM(own, F32),
            pltpu.VMEM((rows, merged.shape[1]), F32),
            pltpu.VMEM((rows, 2 * half), F32),
            pltpu.VMEM(act.shape, BF16),
            pltpu.VMEM((16, width), F32),
        ] + reduce_scratch(cube, [(rows, size) for _, _, size, _ in late])
        + root_scratch(cube, grad_shrink.shape[0], FF_CHUNKS, own)
        + reduce_scratch(cube, [(rows, size) for _, _, size, _ in tail])
        + exchange_semaphores(clips, blk) + exchange_semaphores(clips, blk) + sum_scratch(dp, blk),
        compiler_params=pltpu.CompilerParams(
            dimension_semantics=("arbitrary",), vmem_limit_bytes=LIMIT, collective_id=cid, has_side_effects=True),
        name="attn_bwd",
    )(xc, cot, dmid, dead, n1, qa, kv, mix, merged, output, vec, early, expand_early, shrink_early,
      grad_expand, grad_shrink, grad_output, act)


def bits_of(size):
    return size.bit_length() - 1


class Cube:
    def __init__(self, dp, blk):
        self.sizes = (dp, blk)
        self.n_dp, self.n_blk = bits_of(dp), bits_of(blk)
        self.count = self.n_dp + self.n_blk
        far = list(range(self.n_dp - 1))
        self.letters = {"X": list(range(self.n_dp, self.count - 1)), "Y": [self.n_dp - 1],
                        "a": far[-1:], "b": far[:-1], "C": [self.count - 1]}

    def bind(self):
        self.at_dp, self.at_blk = lax.axis_index("dp"), lax.axis_index("blk")
        self.mine = [lax.rem(self.at_dp // (1 << (self.n_dp - 1 - k)), 2) for k in range(self.n_dp)]
        self.mine += [lax.rem(self.at_blk // (1 << (self.n_blk - 1 - k)), 2) for k in range(self.n_blk)]
        return self

    def partner(self, bit):
        if bit < self.n_dp:
            step = 1 << (self.n_dp - 1 - bit)
            return (self.at_dp + step - 2 * step * self.mine[bit], self.at_blk)
        step = 1 << (self.count - 1 - bit)
        return (self.at_dp, self.at_blk + step - 2 * step * self.mine[bit])

    def row_peer(self, offset):
        return (self.at_dp, lax.rem(self.at_blk + offset, self.sizes[1]))

    def column_peer(self, offset):
        return (lax.rem(self.at_dp + offset, self.sizes[0]), self.at_blk)

    def barrier(self):
        sem = pltpu.get_barrier_semaphore()
        others = [self.row_peer(k) for k in range(1, self.sizes[1])]
        others += [self.column_peer(k) for k in range(1, self.sizes[0])]
        for other in others:
            pl.semaphore_signal(sem, inc=1, device_id=other, device_id_type=MESH)
        pl.semaphore_wait(sem, len(others))


def remote(src, dst, send, recv, device):
    return pltpu.make_async_remote_copy(
        src_ref=src, dst_ref=dst, send_sem=send, recv_sem=recv, device_id=device, device_id_type=MESH)


class Gather:
    def __init__(self, cube, src, dst, cols, letters, send, recv):
        self.cube, self.src, self.dst, self.cols = cube, src, dst, cols
        self.steps = [cube.letters[letter] for letter in letters + "C"]
        self.order = sum(self.steps, [])
        self.send, self.recv = send, recv

    def copy(self, s):
        cube = self.cube
        sel = tuple(slice(None) if bit in self.order[:s] else cube.mine[bit] for bit in range(cube.count))
        there = self.dst.at[sel + (slice(None), self.cols)]
        here = self.src.at[:, self.cols] if s == 0 else there
        return remote(here, there, self.send.at[s], self.recv.at[s], cube.partner(self.order[s]))

    def start(self):
        self.copy(0).start()

    def advance(self, step):
        first = sum(len(bits) for bits in self.steps[:step])
        for s in range(first, first + len(self.steps[step])):
            self.copy(s).wait()
            if s + 1 < len(self.order):
                self.copy(s + 1).start()


class Reduce:
    def __init__(self, cube, src, cols, letters, held, landed, out, send, recv, local):
        self.cube, self.src, self.cols, self.held, self.landed = cube, src, cols, held, landed
        self.dims = range(cube.count)
        self.steps = [cube.letters[letter] for letter in "C" + letters]
        self.order = sum(self.steps, [])
        self.out = out
        self.send, self.recv, self.local = send, recv, local

    def part(self, s, kept):
        cube = self.cube
        sel = []
        for bit in self.dims:
            if bit in self.order[:s]:
                pick = cube.mine[bit]
            elif bit == self.order[s]:
                pick = cube.mine[bit] if kept else 1 - cube.mine[bit]
            else:
                pick = slice(None)
            sel.append(pick)
        return tuple(sel)

    def own(self):
        return pltpu.make_async_copy(
            self.src.at[self.part(0, True) + (slice(None), self.cols)], self.held, self.local)

    def copy(self, s):
        if s == 0:
            here = self.src.at[self.part(0, False) + (slice(None), self.cols)]
        else:
            here = self.held.at[self.part(s, False)[:-1]]
        return remote(here, self.landed[s], self.send.at[s], self.recv.at[s], self.cube.partner(self.order[s]))

    def start(self):
        self.own().start()
        self.copy(0).start()

    def add(self, s):
        keep = self.part(s, True)[:-1]
        width = self.held.shape[-1]
        if s + 1 == len(self.order):
            self.last(self.held[keep].astype(F32) + self.landed[s][...].astype(F32))
            return
        wide = (slice(None),) * (len(self.landed[s].shape) - 1)
        tile = LANES * max(k for k in (1, 2, 3) if width % (LANES * k) == 0)

        def some(j, _):
            cols = (pl.ds(pl.multiple_of(j * tile, tile), tile),)
            at = keep + (slice(None),) + cols
            self.held[at] = self.held[at] + self.landed[s][wide + cols]
            return 0

        lax.fori_loop(0, width // tile, some, 0)

    def last(self, total):
        self.out[:, self.cols] = total

    def advance(self, step):
        first = sum(len(bits) for bits in self.steps[:step])
        for s in range(first, first + len(self.steps[step])):
            self.copy(s).wait()
            if s == 0:
                self.own().wait()
            self.add(s)
            if s + 1 < len(self.order):
                self.copy(s + 1).start()


class RootReduce(Reduce):
    def __init__(self, cube, chunk, chunks, src, letters, held, landed, partial, arrived, out, send, recv, local):
        lead = bits_of(chunks)
        super().__init__(cube, src, slice(None), letters, held, landed, out, send, recv, local)
        self.dims = range(lead, cube.count)
        near = {"X": cube.letters["X"], "Y": [b for b in cube.letters["b"] + cube.letters["a"] if b >= lead] + cube.letters["Y"]}
        self.steps = [cube.letters["C"]] + [near[letter] for letter in letters]
        self.order = sum(self.steps, [])
        self.chunk, self.chunks, self.partial, self.arrived = chunk, chunks, partial, arrived
        self.group = cube.at_dp // (cube.sizes[0] // chunks)

    def owner(self):
        cube, size = self.cube, self.cube.sizes[0] // self.chunks
        slot = lax.rem(self.group + 2 * self.chunks - self.chunk - 1, self.chunks)
        base = len(self.order)
        return remote(self.partial, self.arrived.at[slot], self.send.at[base], self.recv.at[base + slot],
                      (cube.at_dp + (self.chunk - self.group) * size, cube.at_blk))

    def last(self, total):
        @pl.when(self.group == self.chunk)
        def _():
            self.out[...] = total

        @pl.when(self.group != self.chunk)
        def _():
            self.partial[...] = total.astype(BF16)
            self.owner().start()

    def advance(self, step):
        if step < len(self.steps):
            super().advance(step)
            return

        @pl.when(self.group == self.chunk)
        def _():
            base = len(self.order)
            total = self.out[...]
            for slot in range(self.chunks - 1):
                remote(self.partial, self.arrived.at[slot], self.send.at[base], self.recv.at[base + slot],
                       (self.cube.at_dp, self.cube.at_blk)).wait_recv()
                total = total + self.arrived[slot].astype(F32)
            self.out[...] = total

        @pl.when(self.group != self.chunk)
        def _():
            self.owner().wait_send()


def root_scratch(cube, count, chunks, tail):
    rest = cube.count - bits_of(chunks)
    kinds = []
    for _ in range(count):
        kinds.append(pltpu.VMEM((2,) * (rest - 1) + tail, BF16))
    for _ in range(count):
        kinds += [pltpu.VMEM((2,) * (rest - 1 - s) + tail, BF16) for s in range(rest)]
    for _ in range(count):
        kinds += [pltpu.VMEM(tail, BF16), pltpu.VMEM((chunks - 1,) + tail, BF16)]
    sems = rest + chunks
    return kinds + [pltpu.SemaphoreType.DMA((count, sems)), pltpu.SemaphoreType.DMA((count, sems)),
                    pltpu.SemaphoreType.DMA((count,))]


def root_reduces(cube, sources, names, chunks, letters, out, refs):
    count, rest = len(names), cube.count - bits_of(chunks)
    held = refs[:count]
    landed = [refs[count + n * rest:count + (n + 1) * rest] for n in range(count)]
    refs = refs[count * (1 + rest):]
    send, recv, local = refs[2 * count:2 * count + 3]
    return [RootReduce(cube, names[n], chunks, sources[n], letters[n], held[n], landed[n], refs[2 * n], refs[2 * n + 1],
                       out, send.at[n], recv.at[n], local.at[n]) for n in range(count)]


class Exchange:
    def __init__(self, cube, src, dst, back, send, recv, local):
        self.cube, self.src, self.dst, self.back = cube, src, dst, back
        self.clips = (src if back else dst).shape[0]
        self.send, self.recv, self.local = send, recv, local

    def ends(self, to, clip):
        if self.back:
            return self.src.at[clip, to], self.dst.at[self.cube.at_blk * self.clips + clip]
        return self.src.at[to * self.clips + clip], self.dst.at[clip, self.cube.at_blk]

    def copies(self, clip):
        found = [pltpu.make_async_copy(*self.ends(self.cube.at_blk, clip), self.local.at[clip])]
        for k in range(1, self.cube.sizes[1]):
            other = self.cube.row_peer(k)
            found.append(remote(*self.ends(other[1], clip), self.send.at[clip, k - 1], self.recv.at[clip, k - 1], other))
        return found

    def start(self, clip):
        for copy in self.copies(clip):
            copy.start()

    def wait(self, clip):
        for copy in self.copies(clip):
            copy.wait()


def exchange_semaphores(clips, blk):
    return [pltpu.SemaphoreType.DMA((clips, blk)), pltpu.SemaphoreType.DMA((clips, blk)),
            pltpu.SemaphoreType.DMA((clips,))]


def front_kernel(cube, parts, plan, *refs):
    merged_in, xc_in, merged_out, xc_out, send, recv, local, t_send, t_recv, t_local = refs
    cube.bind().barrier()
    gathers = [Gather(cube, merged_in, merged_out, pl.ds(first, size), letters, send.at[k], recv.at[k])
               for k, (first, size, letters) in enumerate(parts)]
    for gather in gathers:
        gather.start()
    own = pltpu.make_async_copy(merged_in, merged_out.at[tuple(cube.mine)], local)
    own.start()
    exchange = Exchange(cube, xc_in, xc_out, False, t_send, t_recv, t_local)
    own.wait()
    points = Points({-1: plan}, gathers, exchange)
    points.finish()
    for clip in range(exchange.clips):
        exchange.wait(clip)


def front(merged, xc, dp, blk, cid):
    cube = Cube(dp, blk)
    clips = xc.shape[0] // blk
    anywhere = pl.BlockSpec(memory_space=pl.ANY)
    half = (merged.shape[1] // LANES + 1) // 2 * LANES
    parts = [(0, half, "XbYa"), (half, merged.shape[1] - half, "XabY")]
    plan = [0, 1] + [-1 - clip for clip in range(clips)] + [0, 1] * 4
    return pl.pallas_call(
        functools.partial(front_kernel, cube, parts, plan),
        in_specs=[pl.BlockSpec(memory_space=pltpu.VMEM), anywhere],
        out_specs=[anywhere] * 2,
        out_shape=[jax.ShapeDtypeStruct((2,) * cube.count + merged.shape, BF16),
                   jax.ShapeDtypeStruct((clips, blk) + xc.shape[1:], BF16)],
        scratch_shapes=[pltpu.SemaphoreType.DMA((len(parts), cube.count)),
                        pltpu.SemaphoreType.DMA((len(parts), cube.count)),
                        pltpu.SemaphoreType.DMA] + exchange_semaphores(clips, blk),
        compiler_params=pltpu.CompilerParams(collective_id=cid, has_side_effects=True, vmem_limit_bytes=LIMIT),
        name="front",
    )(merged, xc)


def sum_everywhere(cube, total, sums, send, recv):
    dp, blk = cube.sizes
    for axis, (size, peer, at) in enumerate(((dp, cube.column_peer, cube.at_dp), (blk, cube.row_peer, cube.at_blk))):
        box = sums[axis]
        box[at] = jnp.full(box.shape[1:], total, F32)
        copies = [remote(box.at[at], box.at[at], send[axis].at[k - 1], recv[axis].at[k - 1], peer(k))
                  for k in range(1, size)]
        for copy in copies:
            copy.start()
        for copy in copies:
            copy.wait()
        whole = box[0]
        for k in range(1, size):
            whole = whole + box[k]
        total = whole[0, 0]
    return whole


def sum_scratch(dp, blk):
    return [[pltpu.VMEM((dp, 8, LANES), F32), pltpu.VMEM((blk, 8, LANES), F32)],
            [pltpu.SemaphoreType.DMA((dp,)), pltpu.SemaphoreType.DMA((blk,))],
            [pltpu.SemaphoreType.DMA((dp,)), pltpu.SemaphoreType.DMA((blk,))]]


def reduce_scratch(cube, shapes):
    held = [pltpu.VMEM((2,) * (cube.count - 1) + s, BF16) for s in shapes]
    landed = [pltpu.VMEM((2,) * (cube.count - 1 - k) + s, BF16) for s in shapes for k in range(cube.count)]
    return held + landed + [pltpu.SemaphoreType.DMA((len(shapes), cube.count)),
                            pltpu.SemaphoreType.DMA((len(shapes), cube.count)),
                            pltpu.SemaphoreType.DMA((len(shapes),))]


def key_columns(kept_time, kept_bands, blocks, own, segment, padded):
    clips = kept_time.shape[0] // blocks
    kept_time = lax.dynamic_slice_in_dim(kept_time, own * clips, clips)
    kept_bands = lax.dynamic_slice_in_dim(kept_bands, own * clips, clips)
    columns = kept_time.shape[1] // blocks
    patches = kept_time.reshape(clips, blocks, columns, 1) * kept_bands[:, None, None, :]
    patches = patches.reshape(clips, blocks, columns * kept_bands.shape[1])
    leading = (jnp.arange(blocks, dtype=jnp.int32) == 0).astype(jnp.int32)
    special = jnp.broadcast_to(leading[None, :, None], (clips, blocks, segment - patches.shape[2]))
    live = jnp.concatenate([special, patches, jnp.zeros((clips, blocks, padded - segment), jnp.int32)], 2)
    bias = jnp.where(live > 0, 0.0, -1e30).reshape(-1, 1)
    lane = jnp.arange(LANES, dtype=jnp.int32)[None, :] % HALF
    return jnp.where(lane == 0, bias, jnp.where(lane < 4, 1.0, 0.0)).astype(BF16)


def prepare_kernel(tok_ref, cot_ref, xc_ref, low_ref):
    segment, extra = tok_ref.shape[1], xc_ref.shape[1] - tok_ref.shape[1]
    values = tok_ref[...]
    centred = (values - jnp.mean(values, -1, keepdims=True)).astype(BF16)
    blank = jnp.zeros((values.shape[0], extra, values.shape[2]), BF16)
    xc_ref[...] = jnp.concatenate([centred, blank], 1)
    low_ref[...] = jnp.concatenate([cot_ref[...].astype(BF16), blank], 1)


def prepare(tokens, cotangent, padded):
    clips, segment, width = tokens.shape
    wide = pl.BlockSpec((2, segment, width), lambda i: (i, 0, 0))
    out = pl.BlockSpec((2, padded, width), lambda i: (i, 0, 0))
    shape = jax.ShapeDtypeStruct((clips, padded, width), BF16)
    return pl.pallas_call(
        prepare_kernel, grid=(clips // 2,), in_specs=[wide, wide], out_specs=[out, out], out_shape=[shape, shape],
        compiler_params=pltpu.CompilerParams(dimension_semantics=("arbitrary",), vmem_limit_bytes=LIMIT),
        name="prepare")(tokens, cotangent)


def finish_kernel(tok_ref, cot_ref, act_ref, dlt_ref, out_ref, grad_ref):
    segment = tok_ref.shape[1]
    out_ref[...] = tok_ref[...] + act_ref[...].astype(F32)[:, :segment]
    grad_ref[...] = cot_ref[...] + dlt_ref[...].astype(F32)[:, :segment]


def finish(tokens, cotangent, act, dlt):
    clips, segment, width = tokens.shape
    wide = pl.BlockSpec((2, segment, width), lambda i: (i, 0, 0))
    low = pl.BlockSpec((2,) + act.shape[1:], lambda i: (i, 0, 0))
    shape = jax.ShapeDtypeStruct(tokens.shape, F32)
    return pl.pallas_call(
        finish_kernel, grid=(clips // 2,), in_specs=[wide, wide, low, low], out_specs=[wide, wide],
        out_shape=[shape, shape],
        compiler_params=pltpu.CompilerParams(dimension_semantics=("arbitrary",), vmem_limit_bytes=LIMIT),
        name="finish")(tokens, cotangent, act, dlt)


RATES = (MATRIX_RATE, MATRIX_RATE, MATRIX_RATE, MATRIX_RATE, VECTOR_RATE)
DECAYS = (MATRIX_DECAY, MATRIX_DECAY, MATRIX_DECAY, MATRIX_DECAY, 0.0)


def adamw_kernel(norm_ref, *refs):
    weights, firsts, seconds, shares = refs[:5], refs[5:10], refs[10:15], refs[15:20]
    outs = refs[20:]
    factor = CLIP_LIMIT / jnp.maximum(jnp.sqrt(norm_ref[0:1, 0:1]), CLIP_LIMIT)
    for index in range(5):
        clipped = shares[index][...] * factor
        weight = weights[index][...]
        momentum = BETA_ONE * firsts[index][...] + (1.0 - BETA_ONE) * clipped
        variance = BETA_TWO * seconds[index][...] + (1.0 - BETA_TWO) * clipped * clipped
        mean_hat = momentum / (1.0 - BETA_ONE**STEP)
        var_hat = variance / (1.0 - BETA_TWO**STEP)
        updated = weight - RATES[index] * (
            mean_hat / (jnp.sqrt(var_hat) + ADAM_EPS) + DECAYS[index] * weight)
        for kind, value in enumerate((clipped, momentum, variance, updated)):
            outs[5 * kind + index][...] = value


def adamw(norm, weights, firsts, seconds, shares):
    inside = pl.BlockSpec(memory_space=pltpu.VMEM)
    return pl.pallas_call(
        adamw_kernel, in_specs=[inside] * 21, out_specs=[inside] * 20,
        out_shape=[jax.ShapeDtypeStruct(w.shape, F32) for w in weights] * 4,
        compiler_params=pltpu.CompilerParams(vmem_limit_bytes=LIMIT),
        name="adamw")(norm, *weights, *firsts, *seconds, *shares)


def shards(
    tokens, kept_time, kept_bands, cotangent,
    weight_merged, weight_output, weight_expand, weight_shrink, vectors,
    first_merged, first_output, first_expand, first_shrink, first_vectors,
    second_merged, second_output, second_expand, second_shrink, second_vectors,
):
    clip_count, segment, width = tokens.shape
    dp, blk = lax.axis_size("dp"), lax.axis_size("blk")
    own = lax.axis_index("blk")
    clips = clip_count // blk
    padded = -(-segment // 16) * 16
    total = clips * blk * padded
    rows = weight_merged.shape[0]
    ff = weight_expand.shape[1]
    cube = (2,) * (bits_of(dp) + bits_of(blk))

    columns = jnp.pad(vectors.T, ((0, 0), (0, LANES - vectors.shape[0])))
    merged_low = jnp.concatenate([weight_merged, columns], 1).astype(BF16)
    wide_low = jnp.concatenate([weight_output, weight_expand], 1).astype(BF16)
    xc_home, cot_home = prepare(tokens, cotangent, padded)
    shrink_low = weight_shrink.astype(BF16)
    merged, xc = front(merged_low, xc_home, dp, blk, 0)
    merged = merged.reshape(width, merged_low.shape[1])
    xc = xc.reshape(total, width)
    vec = merged[:, 3 * width:3 * width + vectors.shape[0]].T.astype(F32)
    dead = key_columns(kept_time, kept_bands, blk, own, segment, padded)
    n1, qa, kv, mix, wide, shrink, cot = attn_fwd(
        xc, dead, merged, vec, wide_low, shrink_low, cot_home, clips, HEADS, dp, blk, 1)
    wide = wide.reshape(width, wide_low.shape[1])
    shrink = shrink.reshape(ff, width)
    cot = cot.reshape(total, width)
    act, dmid, grad_expand, grad_shrink, grad_output, early, expand_early, shrink_early = ffn(
        mix, xc, cot, wide, shrink, vec, blk * padded, dp, blk, 2)

    def by_device(grad):
        return grad.reshape(cube + (grad.shape[0] // (dp * blk), grad.shape[1]))

    sent = (clips, blk, padded, width)
    owners = (2,) * (len(cube) - bits_of(FF_CHUNKS))
    merged_share, vector_share, output_share, expand_share, shrink_share, norm, act_home, dlt_home = attn_bwd(
        xc, cot, dmid, dead, n1, qa, kv, mix, merged, wide, vec, early, expand_early, shrink_early,
        by_device(grad_expand), grad_shrink.reshape((-1,) + owners + weight_shrink.shape), by_device(grad_output),
        act.reshape(sent), clips, HEADS, dp, blk, 3)
    shares = [merged_share, output_share, expand_share, shrink_share, vector_share[:, :vectors.shape[0]].T]
    activations, token_grads = finish(tokens, cotangent, act_home, dlt_home)
    steps_out = adamw(
        norm, (weight_merged, weight_output, weight_expand, weight_shrink, vectors),
        (first_merged, first_output, first_expand, first_shrink, first_vectors),
        (second_merged, second_output, second_expand, second_shrink, second_vectors), shares)
    return (activations, token_grads, jnp.sqrt(norm[0, 0]), *steps_out)


def solution(mesh):
    return jax.shard_map(
        shards,
        mesh=mesh,
        in_specs=(
            P("dp", "blk", None),
            P("dp", None),
            P("dp", None),
            P("dp", "blk", None),
            P(("dp", "blk"), None),
            P(("dp", "blk"), None),
            P(("dp", "blk"), None),
            P(("dp", "blk"), None),
            P(None, ("dp", "blk")),
            P(("dp", "blk"), None),
            P(("dp", "blk"), None),
            P(("dp", "blk"), None),
            P(("dp", "blk"), None),
            P(None, ("dp", "blk")),
            P(("dp", "blk"), None),
            P(("dp", "blk"), None),
            P(("dp", "blk"), None),
            P(("dp", "blk"), None),
            P(None, ("dp", "blk")),
        ),
        out_specs=(
            P("dp", "blk", None),
            P("dp", "blk", None),
            P(),
            P(("dp", "blk"), None),
            P(("dp", "blk"), None),
            P(("dp", "blk"), None),
            P(("dp", "blk"), None),
            P(None, ("dp", "blk")),
            P(("dp", "blk"), None),
            P(("dp", "blk"), None),
            P(("dp", "blk"), None),
            P(("dp", "blk"), None),
            P(None, ("dp", "blk")),
            P(("dp", "blk"), None),
            P(("dp", "blk"), None),
            P(("dp", "blk"), None),
            P(("dp", "blk"), None),
            P(None, ("dp", "blk")),
            P(("dp", "blk"), None),
            P(("dp", "blk"), None),
            P(("dp", "blk"), None),
            P(("dp", "blk"), None),
            P(None, ("dp", "blk")),
        ),
        check_vma=False,
    )
```

```python
import functools
import jax
import jax.numpy as jnp
from jax import lax
from jax.experimental import pallas as pl
from jax.experimental.pallas import tpu as pltpu
from jax.sharding import PartitionSpec as P

HEADS = 12
STEP = 5
CLIP_LIMIT = 1.0
BETA_ONE = 0.5
BETA_TWO = 0.5
ADAM_EPS = 1e-08
MATRIX_RATE = 0.1
VECTOR_RATE = 0.3
MATRIX_DECAY = 0.05

F32, BF16 = jnp.float32, jnp.bfloat16
EPS = 1e-06
HALF = 64
LANES = 128
LIMIT = 127 * 512 * 1024
MESH = pl.DeviceIdType.MESH

FWD_PLAN = {1: [0, 2], 2: [1, 4], 4: [-1, 3], 5: [2], 6: [0, 1], 7: [-2], 10: [3, 4], 12: [0, 1], 14: [3], 15: [2],
            16: [4], -1: [-3, 1, 0, 3, 2, 4, 1, 0, 3, 2, 4]}
FF_CHUNKS = 4
FFN_LETTERS = ["aXYb", "aYXb"]
FFN_ROOTS = ["XY", "XY"]
FFN_PLAN = {8: [0, 2], 11: [0, 2], 13: [0, 2], 14: [1, 3], 15: [0], 17: [2, 3], 18: [1], 19: [0, 3], 20: [1], 22: [1],
            23: [3], -1: [1]}
BWD_LETTERS = ["YbaX", "bYaX", "aYbX"]
BWD_ROOTS = ["YX", "XY"]
BWD_PLAN = {0: [-1], 2: [0, 1, 2, 3, 4], 5: [-2], 6: [0, 4], 7: [1, 2, 3], 9: [4, -3], 11: [0, 1], 12: [2],
            13: [4, 0, 3], 14: [1], 15: [2], -1: [3, 0, 1, 2]}
END_LETTERS = ["abYX", "XYab", "YbaX", "XYba", "XaYb"]
END_PLAN = {4: [0], 6: [1], 7: [0, 2, 3, 4], -1: [1, 2, 3, 4, 0, 1, 3, 4, 2, 0, 1, 4, 2, 3, 0, 1, 4, 2, 3]}


def nn(a, b):
    return lax.dot_general(a, b, (((1,), (0,)), ((), ())), preferred_element_type=F32)


def nt(a, b):
    return lax.dot_general(a, b, (((1,), (1,)), ((), ())), preferred_element_type=F32)


def tn(a, b):
    return lax.dot_general(a, b, (((0,), (0,)), ((), ())), preferred_element_type=F32)


def norm_stats(v):
    centre = jnp.mean(v, -1, keepdims=True)
    c = v - centre
    spread = jnp.mean(c * c, -1, keepdims=True)
    r = lax.rsqrt(spread + EPS)
    return c * r, r


def norm_back(xhat, r, dy, gain):
    dx = dy * gain
    m1 = jnp.mean(dx, -1, keepdims=True)
    m2 = jnp.mean(dx * xhat, -1, keepdims=True)
    return (dx - m1 - xhat * m2) * r


def gelu_pair(x):
    z = jnp.abs(x)
    t = 1.0 / (1.0 + 0.3275911 * 0.7071067811865476 * z)
    e = jnp.exp(-0.5 * x * x)
    poly = t * (0.127414796 + t * (-0.142248368 + t * (0.7107068705 + t * (-0.7265760135 + t * 0.5307027145))))
    tail = poly * e
    phi = jnp.where(x >= 0, 1.0 - tail, tail)
    return x * phi, phi + (0.3989422804014327 * x) * e


def ffn_kernel(cube, letters, plan, mix_ref, xc_ref, cot_ref, prj_ref, exp_ref, shr_ref, vec_ref,
               act_ref, dmid_ref, ge_ref, gs_ref, go_ref, sums_ref, share_ref, shrink_ref,
               n2_s, y_s, dn_s, ae_s, as_s, ao_s, *refs):
    f, i = pl.program_id(0), pl.program_id(1)
    nf, ni = pl.num_programs(0), pl.num_programs(1)
    rows, width = mix_ref.shape
    here = pl.ds(pl.multiple_of(i * rows, rows), rows)
    cube.bind()
    n_p = len(letters)
    ready, held = refs[:n_p], refs[n_p:2 * n_p]
    landed = [refs[2 * n_p + k * cube.count:2 * n_p + (k + 1) * cube.count] for k in range(n_p)]
    refs = refs[n_p * (2 + cube.count):]
    send, recv, local = refs[:3]
    gs_ready, refs = refs[3:3 + n_p], refs[3 + n_p:]
    reduces = [Reduce(cube, ready[k], slice(None), letters[k], held[k], landed[k],
                      share_ref.at[:, pl.ds(k * width, width)], send.at[k], recv.at[k], local.at[k])
               for k in range(n_p)]
    reduces += root_reduces(cube, gs_ready, range(n_p), FF_CHUNKS, FFN_ROOTS, shrink_ref, refs)
    points = Points(plan, reduces, None)

    @pl.when((f == 0) & (i == 0))
    def _():
        cube.barrier()
        shrink_ref[...] = jnp.zeros_like(shrink_ref)
        sums_ref[...] = jnp.zeros_like(sums_ref)

    @pl.when(f == 0)
    def _():
        mid = xc_ref[...].astype(F32) + nn(mix_ref[...], prj_ref[...]) + vec_ref[4:5, :]
        xhat, _ = norm_stats(mid)
        n2_s[here, :] = (xhat * vec_ref[5:6, :] + vec_ref[6:7, :]).astype(BF16)

    points.visit(2 * (f * ni + i), 0)
    n2 = n2_s[here, :]
    d2 = cot_ref[...]
    h = nn(n2, exp_ref[...]) + vec_ref[pl.ds(8 + f, 1), :]
    dg = nt(d2, shr_ref[...])
    g, gp = gelu_pair(h)
    g = g.astype(BF16)
    dh32 = gp * dg
    dh = dh32.astype(BF16)
    sums_ref[pl.ds(8 + f, 1), :] += jnp.sum(dh32, 0, keepdims=True)
    y = nn(g, shr_ref[...])
    dn = nt(dh, exp_ref[...])

    @pl.when(f == 0)
    def _():
        y_s[here, :] = y
        dn_s[here, :] = dn

    @pl.when(f > 0)
    def _():
        y_s[here, :] += y
        dn_s[here, :] += dn

    points.visit(2 * (f * ni + i) + 1, 1)
    ge = tn(n2, dh)
    gs = tn(g, d2)

    @pl.when(i == 0)
    def _():
        ae_s[...] = ge
        as_s[...] = gs

    @pl.when((i > 0) & (i < ni - 1))
    def _():
        ae_s[...] += ge
        as_s[...] += gs

    @pl.when(i == ni - 1)
    def _():
        full_s = (as_s[...] + gs).astype(BF16)
        full = (ae_s[...] + ge).astype(BF16)
        for chunk in range(n_p):
            @pl.when(f == chunk)
            def _():
                ready[chunk][...] = full.reshape(ready[chunk].shape)
                reduces[chunk].start()
                gs_ready[chunk][...] = full_s.reshape(gs_ready[chunk].shape)
                reduces[n_p + chunk].start()

        @pl.when(f >= n_p)
        def _():
            ge_ref[...] = full
            gs_ref[...] = full_s

    @pl.when(f == nf - 1)
    def _():
        mix = mix_ref[...]
        delta = nn(mix, prj_ref[...]) + vec_ref[4:5, :]
        mid = xc_ref[...].astype(F32) + delta
        cot = d2.astype(F32)
        xhat, r = norm_stats(mid)
        dy = dn_s[here, :]
        act_ref[...] = (delta + (y_s[here, :] + vec_ref[7:8, :])).astype(BF16)
        dmid = cot + norm_back(xhat, r, dy, vec_ref[5:6, :])
        dmid_ref[...] = dmid
        d_one = dmid.astype(BF16)
        sums_ref[4:5, :] += jnp.sum(d_one.astype(F32), 0, keepdims=True)
        go = tn(mix, d_one)

        @pl.when(i == 0)
        def _():
            ao_s[...] = go

        @pl.when(i > 0)
        def _():
            ao_s[...] += go

        @pl.when(i == ni - 1)
        def _():
            go_ref[...] = ao_s[...].astype(BF16)

        sums_ref[5:6, :] += jnp.sum(dy * xhat, 0, keepdims=True)
        sums_ref[6:7, :] += jnp.sum(dy, 0, keepdims=True)
        sums_ref[7:8, :] += jnp.sum(cot, 0, keepdims=True)

    @pl.when((f == nf - 1) & (i == ni - 1))
    def _():
        points.finish()


def ffn(mix, xc, cot, expand, shrink, vec, rows, dp, blk, cid):
    total, width = xc.shape
    cube = Cube(dp, blk)
    ff = expand.shape[1] - width
    nf, ni = ff // width, total // rows
    letters = FFN_LETTERS
    early = len(letters)
    chunk = (width // (dp * blk), width)
    own = (ff // (dp * blk), width)
    first = lambda f, i: (jnp.where((f == 0) | (f == nf - 1), i, ni - 1), 0)
    last = lambda f, i: (jnp.where(f == nf - 1, i, 0), 0)
    once = pl.Buffered(1)
    whole = lambda f, i: (0, 0)
    return pl.pallas_call(
        functools.partial(ffn_kernel, cube, letters, FFN_PLAN),
        grid=(nf, ni),
        in_specs=[
            pl.BlockSpec((rows, width), first),
            pl.BlockSpec((rows, width), first),
            pl.BlockSpec((rows, width), lambda f, i: (i, 0)),
            pl.BlockSpec((width, width), whole, pipeline_mode=once),
            pl.BlockSpec((width, width), lambda f, i: (0, f + 1)),
            pl.BlockSpec((width, width), lambda f, i: (f, 0)),
            pl.BlockSpec(vec.shape, whole),
        ],
        out_specs=[
            pl.BlockSpec((rows, width), last),
            pl.BlockSpec((rows, width), last),
            pl.BlockSpec((width, width), lambda f, i: (0, jnp.maximum(f - early, 0)), pipeline_mode=once),
            pl.BlockSpec((width, width), lambda f, i: (jnp.maximum(f - early, 0), 0), pipeline_mode=once),
            pl.BlockSpec((width, width), whole, pipeline_mode=once),
            pl.BlockSpec((16, width), whole),
            pl.BlockSpec((chunk[0], width * early), whole, pipeline_mode=once),
            pl.BlockSpec(own, whole, pipeline_mode=once),
        ],
        out_shape=[
            jax.ShapeDtypeStruct((total, width), BF16),
            jax.ShapeDtypeStruct((total, width), F32),
            jax.ShapeDtypeStruct((width, ff - early * width), BF16),
            jax.ShapeDtypeStruct((ff - early * width, width), BF16),
            jax.ShapeDtypeStruct((width, width), BF16),
            jax.ShapeDtypeStruct((16, width), F32),
            jax.ShapeDtypeStruct((chunk[0], width * early), F32),
            jax.ShapeDtypeStruct(own, F32),
        ],
        scratch_shapes=[
            pltpu.VMEM((total, width), BF16),
            pltpu.VMEM((total, width), F32),
            pltpu.VMEM((total, width), F32),
            pltpu.VMEM((width, width), F32),
            pltpu.VMEM((width, width), F32),
            pltpu.VMEM((width, width), F32),
        ] + [pltpu.VMEM((2,) * cube.count + chunk, BF16) for _ in letters]
        + reduce_scratch(cube, [chunk] * early)
        + [pltpu.VMEM((2,) * (cube.count - bits_of(FF_CHUNKS)) + own, BF16) for _ in letters]
        + root_scratch(cube, early, FF_CHUNKS, own),
        compiler_params=pltpu.CompilerParams(
            dimension_semantics=("arbitrary", "arbitrary"), vmem_limit_bytes=LIMIT, collective_id=cid,
            has_side_effects=True),
        name="ffn",
    )(mix, xc, cot, expand, expand, shrink, vec)


def attn_fwd_kernel(cube, parts, plan, heads, xc_ref, dead_ref, mrg_ref, vec_ref, wide_in, shrink_in, cot_in,
                    n1_ref, qa_ref, kv_ref, mix_ref, wide_out, shrink_out, cot_out,
                    pk_s, send, recv, local, t_send, t_recv, t_local):
    width = xc_ref.shape[1]
    seq = xc_ref.shape[0]
    pairs = heads // 2
    cube.bind()
    clip = pl.program_id(0)
    own = [pltpu.make_async_copy(wide_in, wide_out.at[tuple(cube.mine)], local.at[0]),
           pltpu.make_async_copy(shrink_in, shrink_out.at[tuple(cube.mine)], local.at[1])]
    gathers = [Gather(cube, (wide_in, shrink_in)[a], (wide_out, shrink_out)[a], pl.ds(first, size), letters,
                      send.at[n], recv.at[n]) for n, (a, first, size, letters) in enumerate(parts)]
    exchange = Exchange(cube, cot_in, cot_out, False, t_send, t_recv, t_local)
    points = Points(plan, gathers, exchange)

    @pl.when(clip == 0)
    def _():
        cube.barrier()
        for gather in gathers:
            gather.start()
        for copy in own:
            copy.start()
        for copy in own:
            copy.wait()

    xc = xc_ref[...].astype(F32)
    xhat, _ = norm_stats(xc)
    n1 = (xhat * vec_ref[0:1, :] + vec_ref[1:2, :]).astype(BF16)
    n1_ref[...] = n1
    for third in range(3):
        cols = pl.ds(third * width, width)
        part = nn(n1, mrg_ref[:, cols])
        if third != 1:
            part = part + vec_ref[2 + third // 2:3 + third // 2, :]
        part = part.astype(BF16)
        pk_s[:, cols] = part
        if third:
            kv_ref[:, pl.ds((third - 1) * width, width)] = part
    lane = lax.broadcasted_iota(jnp.int32, (seq, LANES), 1)
    low = lane < HALF
    in_half = lane % HALF
    dead = dead_ref[...]
    ones = jnp.ones((seq, LANES), BF16)

    def pair(p, _):
        points.visit(clip * pairs + p)
        qcols = pl.ds(pl.multiple_of(p * LANES, LANES), LANES)
        kcols = pl.ds(pl.multiple_of(width + p * LANES, LANES), LANES)
        vcols = pl.ds(pl.multiple_of(2 * width + p * LANES, LANES), LANES)
        q = pk_s[:, qcols] * jnp.array(0.125, BF16)
        k = pk_s[:, kcols]
        v = pk_s[:, vcols]
        outs = []
        for side in range(2):
            mine = low if side == 0 else ~low
            qs = jnp.where(mine, q, jnp.where(in_half == 0, 1.0, 0.0).astype(BF16))
            ks = jnp.where(mine, k, dead)
            vs = jnp.where(mine, v, ones)
            s = nt(qs, ks)
            top = jnp.max(s, -1, keepdims=True)
            e = jnp.exp(s - top).astype(BF16)
            o = nn(e, vs)
            swapped = pltpu.roll(o, HALF, 1)
            outs.append(o / swapped)
            lse = top + jnp.log(jnp.where(mine, swapped, o))
            hi = (-lse).astype(BF16)
            rest = -lse - hi.astype(F32)
            mid_part = rest.astype(BF16)
            lo = (rest - mid_part.astype(F32)).astype(BF16)
            extra = jnp.where(in_half == 0, 1.0, 0.0).astype(BF16)
            extra = jnp.where(in_half == 1, hi, extra)
            extra = jnp.where(in_half == 2, mid_part, extra)
            extra = jnp.where(in_half == 3, lo, extra)
            qa_ref[2 * p + side] = jnp.where(mine, q, extra)
        mix_ref[:, qcols] = jnp.where(low, outs[0], outs[1]).astype(BF16)
        return 0

    lax.fori_loop(0, pairs, pair, 0)

    @pl.when(clip == pl.num_programs(0) - 1)
    def _():
        points.finish()
        for part in range(exchange.clips):
            exchange.wait(part)


class Points:
    def __init__(self, plan, movers, exchange):
        self.movers, self.exchange = movers, exchange
        self.plan, taken = {}, {}
        for point in sorted(plan, key=lambda p: p if p >= 0 else 1 << 20):
            self.plan[point] = []
            for which in plan[point]:
                self.plan[point].append((which, taken.get(which, 0)))
                taken[which] = taken.get(which, 0) + 1

    def act(self, point):
        for which, step in self.plan[point]:
            if which < 0:
                self.exchange.start(-1 - which)
            else:
                self.movers[which].advance(step)

    def visit(self, now, at=None, period=2, limit=1 << 20):
        for point in self.plan:
            if point < 0 or point >= limit or (at is not None and point % period != at):
                continue

            @pl.when(now == point)
            def _():
                self.act(point)

    def finish(self):
        self.act(-1)


def attn_fwd(xc, dead, merged, vec, wide, shrink, cot, clips, heads, dp, blk, cid):
    total, width = xc.shape
    seq = total // clips
    cube = Cube(dp, blk)
    whole = lambda c: (0, 0)
    row = lambda c: (c, 0)
    anywhere = pl.BlockSpec(memory_space=pl.ANY)
    third, half = wide.shape[1] // 3, shrink.shape[1] // 2
    parts = [(0, 0, third, "XbYa"), (0, third, third, "baXY"), (0, 2 * third, third, "YXba"),
             (1, 0, half, "baYX"), (1, half, half, "XbaY")]
    return pl.pallas_call(
        functools.partial(attn_fwd_kernel, cube, parts, FWD_PLAN, heads),
        grid=(clips,),
        in_specs=[
            pl.BlockSpec((seq, width), row),
            pl.BlockSpec((seq, LANES), row),
            pl.BlockSpec(merged.shape, whole),
            pl.BlockSpec(vec.shape, whole),
            pl.BlockSpec(wide.shape, whole),
            pl.BlockSpec(shrink.shape, whole),
            anywhere,
        ],
        out_specs=[
            pl.BlockSpec((seq, width), row),
            pl.BlockSpec((heads, seq, LANES), lambda c: (0, c, 0)),
            pl.BlockSpec((seq, 2 * width), row),
            pl.BlockSpec((seq, width), row),
            anywhere, anywhere, anywhere,
        ],
        out_shape=[
            jax.ShapeDtypeStruct((total, width), BF16),
            jax.ShapeDtypeStruct((heads, total, LANES), BF16),
            jax.ShapeDtypeStruct((total, 2 * width), BF16),
            jax.ShapeDtypeStruct((total, width), BF16),
            jax.ShapeDtypeStruct((2,) * cube.count + wide.shape, BF16),
            jax.ShapeDtypeStruct((2,) * cube.count + shrink.shape, BF16),
            jax.ShapeDtypeStruct((clips, blk) + cot.shape[1:], BF16),
        ],
        scratch_shapes=[
            pltpu.VMEM((seq, 3 * width), BF16),
            pltpu.SemaphoreType.DMA((len(parts), cube.count)),
            pltpu.SemaphoreType.DMA((len(parts), cube.count)),
            pltpu.SemaphoreType.DMA((2,)),
        ] + exchange_semaphores(clips, blk),
        compiler_params=pltpu.CompilerParams(
            dimension_semantics=("arbitrary",), vmem_limit_bytes=LIMIT, collective_id=cid, has_side_effects=True),
        name="attn_fwd",
    )(xc, dead, merged, vec, wide, shrink, cot)


def attn_bwd_kernel(cube, late, tail, plan, heads, xc_ref, cot_ref, dmid_ref, dead_ref, n1_ref, qa_ref, kv_ref, mix_ref,
                    mrg_ref, out_ref, vec_ref, early_ref, ge_early, gs_early,
                    ge_in, gs_in, go_in, act_in,
                    gm_out, gv_out, go_out, ge_out, gs_out, norm_ref, act_out, dlt_out,
                    dm_s, dp_s, nt_s, am_s, gm_s, gl_s, gw_s, gx_s, dlt_s, sums_ref, *refs):
    c = pl.program_id(0)
    n = pl.num_programs(0)
    seq, width = xc_ref.shape
    pairs = heads // 2
    cube.bind()

    def take(count):
        nonlocal refs
        taken, refs = refs[:count], refs[count:]
        return taken

    def sums_of(parts, sources, outs):
        count = len(parts)
        held = take(count)
        landed = [take(cube.count) for _ in parts]
        send, recv, local = take(3)
        return [Reduce(cube, sources[a], pl.ds(first, size), letters, held[m], landed[m], outs[a],
                       send.at[m], recv.at[m], local.at[m]) for m, (a, first, size, letters) in enumerate(parts)]

    reduces = sums_of(late, (ge_in, go_in), (gx_s, go_out))
    roots = FF_CHUNKS - gs_in.shape[0]
    count = gs_in.shape[0]
    reduces += root_reduces(cube, [gs_in.at[m] for m in range(count)], range(roots, FF_CHUNKS), FF_CHUNKS, BWD_ROOTS,
                            gl_s, take(4 * count + count * (cube.count - bits_of(FF_CHUNKS)) - count + 3))
    ends = sums_of(tail, (gm_s,), (gw_s,))
    exchange = Exchange(cube, act_in, act_out, True, *take(3))
    homeward = Exchange(cube, dlt_s, dlt_out, True, *take(3))
    sums, s_send, s_recv = refs
    points = Points(plan, reduces, exchange)
    finale = Points(END_PLAN, ends, None)

    @pl.when(c == 0)
    def _():
        cube.barrier()
        for reduce in reduces:
            reduce.start()
        gl_s[...] = jnp.zeros_like(gl_s)
        sums_ref[...] = early_ref[...]
        am_s[...] = jnp.zeros_like(am_s)

    d_one = dmid_ref[...].astype(BF16)
    dm_s[...] = nt(d_one, out_ref[...]).astype(BF16)
    nt_s[...] = jnp.transpose(n1_ref[...])
    group = 3 * LANES

    def by_device(values):
        return values.astype(BF16).reshape((2,) * cube.count + (width // (1 << cube.count), values.shape[1]))

    lane = lax.broadcasted_iota(jnp.int32, (seq, LANES), 1)
    low = lane < HALF
    in_half = lane % HALF
    dead = dead_ref[...]
    vone = jnp.where(in_half < 2, 1.0, 0.0).astype(BF16)

    def pair(p, _):
        points.visit(c * pairs + p)
        finale.visit(jnp.where(c == n - 1, p, -1), limit=pairs)
        qcols = pl.ds(pl.multiple_of(p * LANES, LANES), LANES)
        kcols = pl.ds(pl.multiple_of(width + p * LANES, LANES), LANES)
        vcols = pl.ds(pl.multiple_of(2 * width + p * LANES, LANES), LANES)
        k = kv_ref[:, qcols]
        v = kv_ref[:, kcols]
        dm = dm_s[:, qcols]
        prod = dm.astype(F32) * mix_ref[:, qcols].astype(F32)
        k_t = jnp.transpose(k)
        dks, dvs, dqs = [], [], []
        for side in range(2):
            mine = low if side == 0 else ~low
            qa = qa_ref[2 * p + side]
            ka = jnp.where(mine, k, dead)
            va = jnp.where(mine, v, vone)
            dd = -jnp.sum(jnp.where(mine, prod, 0.0), -1, keepdims=True)
            hi = dd.astype(BF16)
            lo = (dd - hi.astype(F32)).astype(BF16)
            da = jnp.where(mine, dm, jnp.where(in_half == 0, hi, lo))
            p_t = jnp.exp(nt(ka, qa))
            ds_t = (p_t * nt(va, da)).astype(BF16)
            dvs.append(nn(p_t.astype(BF16), da))
            dks.append(nn(ds_t, qa))
            dqs.append(nn(k_t[side * HALF:(side + 1) * HALF, :], ds_t))
        dq = jnp.transpose(jnp.concatenate(dqs, 0)) * 0.125
        dk = jnp.where(low, dks[0], dks[1])
        dv = jnp.where(low, dvs[0], dvs[1])
        sums_ref[2:3, qcols] += jnp.sum(dq, 0, keepdims=True)
        sums_ref[3:4, qcols] += jnp.sum(dv, 0, keepdims=True)
        three = jnp.concatenate([dq, dk, dv], 1).astype(BF16)
        dp_s[:, qcols] = three[:, :LANES]
        dp_s[:, kcols] = three[:, LANES:2 * LANES]
        dp_s[:, vcols] = three[:, 2 * LANES:]
        mine = pl.ds(pl.multiple_of(p * group, group), group)
        grad = am_s[:, mine] + nn(nt_s[...], three)
        am_s[:, mine] = grad

        @pl.when(c == n - 1)
        def _():
            gm_s[(slice(None),) * (cube.count + 1) + (mine,)] = by_device(grad)
            for m, (_, first, size, _) in enumerate(tail[:-1]):
                @pl.when(first + size == (p + 1) * group)
                def _():
                    ends[m].start()

        return 0

    lax.fori_loop(0, pairs, pair, 0)
    dp = dp_s[...]

    @pl.when(c == n - 1)
    def _():
        finale.act(pairs)

    dy = nt(dp, mrg_ref[:, :3 * width])
    xhat, r = norm_stats(xc_ref[...].astype(F32))
    sums_ref[0:1, :] += jnp.sum(dy * xhat, 0, keepdims=True)
    sums_ref[1:2, :] += jnp.sum(dy, 0, keepdims=True)
    delta = ((dmid_ref[...] - cot_ref[...].astype(F32)) + norm_back(xhat, r, dy, vec_ref[0:1, :])).astype(BF16)
    dlt_s[c] = delta.reshape(dlt_s.shape[1:])
    for clip in range(homeward.clips - 1):
        @pl.when(c == clip)
        def _():
            homeward.start(clip)

    @pl.when(c == n - 1)
    def _():
        columns = jnp.transpose(sums_ref[...])
        blank = jnp.zeros((width, LANES - columns.shape[1]), F32)
        gm_s[(slice(None),) * (cube.count + 1) + (pl.ds(3 * width, LANES),)] = by_device(
            jnp.concatenate([columns, blank], 1))
        ends[-1].start()
        finale.act(pairs + 1)
        homeward.start(homeward.clips - 1)
        points.finish()
        finale.finish()
        shrink = gs_early[...] + gl_s[...]
        gs_out[...] = shrink
        part = ge_early.shape[1]
        ge_out[:, :part] = ge_early[...]
        ge_out[:, part:] = gx_s[...]
        total = jnp.sum(shrink * shrink) + jnp.sum(go_out[...] * go_out[...])
        total = total + jnp.sum(ge_early[...] * ge_early[...]) + jnp.sum(gx_s[...] * gx_s[...])
        for p in range(pairs):
            for third in range(3):
                gm_out[:, third * width + p * LANES:third * width + (p + 1) * LANES] = (
                    gw_s[:, p * group + third * LANES:p * group + (third + 1) * LANES])
        gv_out[...] = gw_s[:, 3 * width:]
        total = total + jnp.sum(gw_s[...] * gw_s[...])
        norm_ref[...] = sum_everywhere(cube, total, sums, s_send, s_recv)
        for clip in range(homeward.clips):
            exchange.wait(clip)
            homeward.wait(clip)


def attn_bwd(xc, cot, dmid, dead, n1, qa, kv, mix, merged, output, vec, early, expand_early, shrink_early,
             grad_expand, grad_shrink, grad_output, act, clips, heads, dp, blk, cid):
    total, width = xc.shape
    seq = total // clips
    cube = Cube(dp, blk)
    whole = lambda c: (0, 0)
    row = lambda c: (c, 0)
    once = pl.Buffered(1)
    anywhere = pl.BlockSpec(memory_space=pl.ANY)
    rows, own = grad_expand.shape[-2], grad_shrink.shape[-2:]
    half = grad_expand.shape[-1] // 2
    late = [(0, 0, half, BWD_LETTERS[0]), (0, half, half, BWD_LETTERS[1]), (1, 0, width, BWD_LETTERS[2])]
    sixth = width // 2
    cuts = [0, 2 * sixth, 4 * sixth, 5 * sixth, 6 * sixth, merged.shape[1]]
    tail = [(0, cuts[m], cuts[m + 1] - cuts[m], END_LETTERS[m]) for m in range(5)]
    fixed = [(rows, 3 * width), (rows, merged.shape[1] - 3 * width), (rows, width),
             (rows, expand_early.shape[1] + 2 * half), own, (8, LANES)]
    home = (clips * blk,) + act.shape[2:]
    return pl.pallas_call(
        functools.partial(attn_bwd_kernel, cube, late, tail, BWD_PLAN, heads),
        grid=(clips,),
        in_specs=[
            pl.BlockSpec((seq, width), row),
            pl.BlockSpec((seq, width), row),
            pl.BlockSpec((seq, width), row),
            pl.BlockSpec((seq, LANES), row),
            pl.BlockSpec((seq, width), row),
            pl.BlockSpec((heads, seq, LANES), lambda c: (0, c, 0)),
            pl.BlockSpec((seq, 2 * width), row),
            pl.BlockSpec((seq, width), row),
            pl.BlockSpec(merged.shape, whole, pipeline_mode=once),
            pl.BlockSpec((width, width), whole, pipeline_mode=once),
            pl.BlockSpec(vec.shape, whole),
            pl.BlockSpec(early.shape, whole),
            pl.BlockSpec(expand_early.shape, whole, pipeline_mode=once),
            pl.BlockSpec(shrink_early.shape, whole, pipeline_mode=once),
            anywhere, anywhere, anywhere, anywhere,
        ],
        out_specs=[pl.BlockSpec(s, whole, pipeline_mode=once) for s in fixed] + [anywhere, anywhere],
        out_shape=[jax.ShapeDtypeStruct(s, F32) for s in fixed] + [jax.ShapeDtypeStruct(home, BF16)] * 2,
        scratch_shapes=[
            pltpu.VMEM((seq, width), BF16),
            pltpu.VMEM((seq, 3 * width), BF16),
            pltpu.VMEM((width, seq), BF16),
            pltpu.VMEM((width, 3 * width), F32),
            pltpu.VMEM((2,) * cube.count + (rows, merged.shape[1]), BF16),
            pltpu.VMEM(own, F32),
            pltpu.VMEM((rows, merged.shape[1]), F32),
            pltpu.VMEM((rows, 2 * half), F32),
            pltpu.VMEM(act.shape, BF16),
            pltpu.VMEM((16, width), F32),
        ] + reduce_scratch(cube, [(rows, size) for _, _, size, _ in late])
        + root_scratch(cube, grad_shrink.shape[0], FF_CHUNKS, own)
        + reduce_scratch(cube, [(rows, size) for _, _, size, _ in tail])
        + exchange_semaphores(clips, blk) + exchange_semaphores(clips, blk) + sum_scratch(dp, blk),
        compiler_params=pltpu.CompilerParams(
            dimension_semantics=("arbitrary",), vmem_limit_bytes=LIMIT, collective_id=cid, has_side_effects=True),
        name="attn_bwd",
    )(xc, cot, dmid, dead, n1, qa, kv, mix, merged, output, vec, early, expand_early, shrink_early,
      grad_expand, grad_shrink, grad_output, act)


def bits_of(size):
    return size.bit_length() - 1


class Cube:
    def __init__(self, dp, blk):
        self.sizes = (dp, blk)
        self.n_dp, self.n_blk = bits_of(dp), bits_of(blk)
        self.count = self.n_dp + self.n_blk
        far = list(range(self.n_dp - 1))
        self.letters = {"X": list(range(self.n_dp, self.count - 1)), "Y": [self.n_dp - 1],
                        "a": far[-1:], "b": far[:-1], "C": [self.count - 1]}

    def bind(self):
        self.at_dp, self.at_blk = lax.axis_index("dp"), lax.axis_index("blk")
        self.mine = [lax.rem(self.at_dp // (1 << (self.n_dp - 1 - k)), 2) for k in range(self.n_dp)]
        self.mine += [lax.rem(self.at_blk // (1 << (self.n_blk - 1 - k)), 2) for k in range(self.n_blk)]
        return self

    def partner(self, bit):
        if bit < self.n_dp:
            step = 1 << (self.n_dp - 1 - bit)
            return (self.at_dp + step - 2 * step * self.mine[bit], self.at_blk)
        step = 1 << (self.count - 1 - bit)
        return (self.at_dp, self.at_blk + step - 2 * step * self.mine[bit])

    def row_peer(self, offset):
        return (self.at_dp, lax.rem(self.at_blk + offset, self.sizes[1]))

    def column_peer(self, offset):
        return (lax.rem(self.at_dp + offset, self.sizes[0]), self.at_blk)

    def barrier(self):
        sem = pltpu.get_barrier_semaphore()
        others = [self.row_peer(k) for k in range(1, self.sizes[1])]
        others += [self.column_peer(k) for k in range(1, self.sizes[0])]
        for other in others:
            pl.semaphore_signal(sem, inc=1, device_id=other, device_id_type=MESH)
        pl.semaphore_wait(sem, len(others))


def remote(src, dst, send, recv, device):
    return pltpu.make_async_remote_copy(
        src_ref=src, dst_ref=dst, send_sem=send, recv_sem=recv, device_id=device, device_id_type=MESH)


class Gather:
    def __init__(self, cube, src, dst, cols, letters, send, recv):
        self.cube, self.src, self.dst, self.cols = cube, src, dst, cols
        self.steps = [cube.letters[letter] for letter in letters + "C"]
        self.order = sum(self.steps, [])
        self.send, self.recv = send, recv

    def copy(self, s):
        cube = self.cube
        sel = tuple(slice(None) if bit in self.order[:s] else cube.mine[bit] for bit in range(cube.count))
        there = self.dst.at[sel + (slice(None), self.cols)]
        here = self.src.at[:, self.cols] if s == 0 else there
        return remote(here, there, self.send.at[s], self.recv.at[s], cube.partner(self.order[s]))

    def start(self):
        self.copy(0).start()

    def advance(self, step):
        first = sum(len(bits) for bits in self.steps[:step])
        for s in range(first, first + len(self.steps[step])):
            self.copy(s).wait()
            if s + 1 < len(self.order):
                self.copy(s + 1).start()


class Reduce:
    def __init__(self, cube, src, cols, letters, held, landed, out, send, recv, local):
        self.cube, self.src, self.cols, self.held, self.landed = cube, src, cols, held, landed
        self.dims = range(cube.count)
        self.steps = [cube.letters[letter] for letter in "C" + letters]
        self.order = sum(self.steps, [])
        self.out = out
        self.send, self.recv, self.local = send, recv, local

    def part(self, s, kept):
        cube = self.cube
        sel = []
        for bit in self.dims:
            if bit in self.order[:s]:
                pick = cube.mine[bit]
            elif bit == self.order[s]:
                pick = cube.mine[bit] if kept else 1 - cube.mine[bit]
            else:
                pick = slice(None)
            sel.append(pick)
        return tuple(sel)

    def own(self):
        return pltpu.make_async_copy(
            self.src.at[self.part(0, True) + (slice(None), self.cols)], self.held, self.local)

    def copy(self, s):
        if s == 0:
            here = self.src.at[self.part(0, False) + (slice(None), self.cols)]
        else:
            here = self.held.at[self.part(s, False)[:-1]]
        return remote(here, self.landed[s], self.send.at[s], self.recv.at[s], self.cube.partner(self.order[s]))

    def start(self):
        self.own().start()
        self.copy(0).start()

    def add(self, s):
        keep = self.part(s, True)[:-1]
        width = self.held.shape[-1]
        if s + 1 == len(self.order):
            self.last(self.held[keep].astype(F32) + self.landed[s][...].astype(F32))
            return
        wide = (slice(None),) * (len(self.landed[s].shape) - 1)
        tile = LANES * max(k for k in (1, 2, 3) if width % (LANES * k) == 0)

        def some(j, _):
            cols = (pl.ds(pl.multiple_of(j * tile, tile), tile),)
            at = keep + (slice(None),) + cols
            self.held[at] = self.held[at] + self.landed[s][wide + cols]
            return 0

        lax.fori_loop(0, width // tile, some, 0)

    def last(self, total):
        self.out[:, self.cols] = total

    def advance(self, step):
        first = sum(len(bits) for bits in self.steps[:step])
        for s in range(first, first + len(self.steps[step])):
            self.copy(s).wait()
            if s == 0:
                self.own().wait()
            self.add(s)
            if s + 1 < len(self.order):
                self.copy(s + 1).start()


class RootReduce(Reduce):
    def __init__(self, cube, chunk, chunks, src, letters, held, landed, partial, arrived, out, send, recv, local):
        lead = bits_of(chunks)
        super().__init__(cube, src, slice(None), letters, held, landed, out, send, recv, local)
        self.dims = range(lead, cube.count)
        near = {"X": cube.letters["X"], "Y": [b for b in cube.letters["b"] + cube.letters["a"] if b >= lead] + cube.letters["Y"]}
        self.steps = [cube.letters["C"]] + [near[letter] for letter in letters]
        self.order = sum(self.steps, [])
        self.chunk, self.chunks, self.partial, self.arrived = chunk, chunks, partial, arrived
        self.group = cube.at_dp // (cube.sizes[0] // chunks)

    def owner(self):
        cube, size = self.cube, self.cube.sizes[0] // self.chunks
        slot = lax.rem(self.group + 2 * self.chunks - self.chunk - 1, self.chunks)
        base = len(self.order)
        return remote(self.partial, self.arrived.at[slot], self.send.at[base], self.recv.at[base + slot],
                      (cube.at_dp + (self.chunk - self.group) * size, cube.at_blk))

    def last(self, total):
        @pl.when(self.group == self.chunk)
        def _():
            self.out[...] = total

        @pl.when(self.group != self.chunk)
        def _():
            self.partial[...] = total.astype(BF16)
            self.owner().start()

    def advance(self, step):
        if step < len(self.steps):
            super().advance(step)
            return

        @pl.when(self.group == self.chunk)
        def _():
            base = len(self.order)
            total = self.out[...]
            for slot in range(self.chunks - 1):
                remote(self.partial, self.arrived.at[slot], self.send.at[base], self.recv.at[base + slot],
                       (self.cube.at_dp, self.cube.at_blk)).wait_recv()
                total = total + self.arrived[slot].astype(F32)
            self.out[...] = total

        @pl.when(self.group != self.chunk)
        def _():
            self.owner().wait_send()


def root_scratch(cube, count, chunks, tail):
    rest = cube.count - bits_of(chunks)
    kinds = []
    for _ in range(count):
        kinds.append(pltpu.VMEM((2,) * (rest - 1) + tail, BF16))
    for _ in range(count):
        kinds += [pltpu.VMEM((2,) * (rest - 1 - s) + tail, BF16) for s in range(rest)]
    for _ in range(count):
        kinds += [pltpu.VMEM(tail, BF16), pltpu.VMEM((chunks - 1,) + tail, BF16)]
    sems = rest + chunks
    return kinds + [pltpu.SemaphoreType.DMA((count, sems)), pltpu.SemaphoreType.DMA((count, sems)),
                    pltpu.SemaphoreType.DMA((count,))]


def root_reduces(cube, sources, names, chunks, letters, out, refs):
    count, rest = len(names), cube.count - bits_of(chunks)
    held = refs[:count]
    landed = [refs[count + n * rest:count + (n + 1) * rest] for n in range(count)]
    refs = refs[count * (1 + rest):]
    send, recv, local = refs[2 * count:2 * count + 3]
    return [RootReduce(cube, names[n], chunks, sources[n], letters[n], held[n], landed[n], refs[2 * n], refs[2 * n + 1],
                       out, send.at[n], recv.at[n], local.at[n]) for n in range(count)]


class Exchange:
    def __init__(self, cube, src, dst, back, send, recv, local):
        self.cube, self.src, self.dst, self.back = cube, src, dst, back
        self.clips = (src if back else dst).shape[0]
        self.send, self.recv, self.local = send, recv, local

    def ends(self, to, clip):
        if self.back:
            return self.src.at[clip, to], self.dst.at[self.cube.at_blk * self.clips + clip]
        return self.src.at[to * self.clips + clip], self.dst.at[clip, self.cube.at_blk]

    def copies(self, clip):
        found = [pltpu.make_async_copy(*self.ends(self.cube.at_blk, clip), self.local.at[clip])]
        for k in range(1, self.cube.sizes[1]):
            other = self.cube.row_peer(k)
            found.append(remote(*self.ends(other[1], clip), self.send.at[clip, k - 1], self.recv.at[clip, k - 1], other))
        return found

    def start(self, clip):
        for copy in self.copies(clip):
            copy.start()

    def wait(self, clip):
        for copy in self.copies(clip):
            copy.wait()


def exchange_semaphores(clips, blk):
    return [pltpu.SemaphoreType.DMA((clips, blk)), pltpu.SemaphoreType.DMA((clips, blk)),
            pltpu.SemaphoreType.DMA((clips,))]


def front_kernel(cube, parts, plan, *refs):
    merged_in, xc_in, merged_out, xc_out, send, recv, local, t_send, t_recv, t_local = refs
    cube.bind().barrier()
    gathers = [Gather(cube, merged_in, merged_out, pl.ds(first, size), letters, send.at[k], recv.at[k])
               for k, (first, size, letters) in enumerate(parts)]
    for gather in gathers:
        gather.start()
    own = pltpu.make_async_copy(merged_in, merged_out.at[tuple(cube.mine)], local)
    own.start()
    exchange = Exchange(cube, xc_in, xc_out, False, t_send, t_recv, t_local)
    own.wait()
    points = Points({-1: plan}, gathers, exchange)
    points.finish()
    for clip in range(exchange.clips):
        exchange.wait(clip)


def front(merged, xc, dp, blk, cid):
    cube = Cube(dp, blk)
    clips = xc.shape[0] // blk
    anywhere = pl.BlockSpec(memory_space=pl.ANY)
    half = (merged.shape[1] // LANES + 1) // 2 * LANES
    parts = [(0, half, "XbYa"), (half, merged.shape[1] - half, "XabY")]
    plan = [0, 1] + [-1 - clip for clip in range(clips)] + [0, 1] * 4
    return pl.pallas_call(
        functools.partial(front_kernel, cube, parts, plan),
        in_specs=[pl.BlockSpec(memory_space=pltpu.VMEM), anywhere],
        out_specs=[anywhere] * 2,
        out_shape=[jax.ShapeDtypeStruct((2,) * cube.count + merged.shape, BF16),
                   jax.ShapeDtypeStruct((clips, blk) + xc.shape[1:], BF16)],
        scratch_shapes=[pltpu.SemaphoreType.DMA((len(parts), cube.count)),
                        pltpu.SemaphoreType.DMA((len(parts), cube.count)),
                        pltpu.SemaphoreType.DMA] + exchange_semaphores(clips, blk),
        compiler_params=pltpu.CompilerParams(collective_id=cid, has_side_effects=True, vmem_limit_bytes=LIMIT),
        name="front",
    )(merged, xc)


def sum_everywhere(cube, total, sums, send, recv):
    dp, blk = cube.sizes
    for axis, (size, peer, at) in enumerate(((dp, cube.column_peer, cube.at_dp), (blk, cube.row_peer, cube.at_blk))):
        box = sums[axis]
        box[at] = jnp.full(box.shape[1:], total, F32)
        copies = [remote(box.at[at], box.at[at], send[axis].at[k - 1], recv[axis].at[k - 1], peer(k))
                  for k in range(1, size)]
        for copy in copies:
            copy.start()
        for copy in copies:
            copy.wait()
        whole = box[0]
        for k in range(1, size):
            whole = whole + box[k]
        total = whole[0, 0]
    return whole


def sum_scratch(dp, blk):
    return [[pltpu.VMEM((dp, 8, LANES), F32), pltpu.VMEM((blk, 8, LANES), F32)],
            [pltpu.SemaphoreType.DMA((dp,)), pltpu.SemaphoreType.DMA((blk,))],
            [pltpu.SemaphoreType.DMA((dp,)), pltpu.SemaphoreType.DMA((blk,))]]


def reduce_scratch(cube, shapes):
    held = [pltpu.VMEM((2,) * (cube.count - 1) + s, BF16) for s in shapes]
    landed = [pltpu.VMEM((2,) * (cube.count - 1 - k) + s, BF16) for s in shapes for k in range(cube.count)]
    return held + landed + [pltpu.SemaphoreType.DMA((len(shapes), cube.count)),
                            pltpu.SemaphoreType.DMA((len(shapes), cube.count)),
                            pltpu.SemaphoreType.DMA((len(shapes),))]


def key_columns(kept_time, kept_bands, blocks, own, segment, padded):
    clips = kept_time.shape[0] // blocks
    kept_time = lax.dynamic_slice_in_dim(kept_time, own * clips, clips)
    kept_bands = lax.dynamic_slice_in_dim(kept_bands, own * clips, clips)
    columns = kept_time.shape[1] // blocks
    patches = kept_time.reshape(clips, blocks, columns, 1) * kept_bands[:, None, None, :]
    patches = patches.reshape(clips, blocks, columns * kept_bands.shape[1])
    leading = (jnp.arange(blocks, dtype=jnp.int32) == 0).astype(jnp.int32)
    special = jnp.broadcast_to(leading[None, :, None], (clips, blocks, segment - patches.shape[2]))
    live = jnp.concatenate([special, patches, jnp.zeros((clips, blocks, padded - segment), jnp.int32)], 2)
    bias = jnp.where(live > 0, 0.0, -1e30).reshape(-1, 1)
    lane = jnp.arange(LANES, dtype=jnp.int32)[None, :] % HALF
    return jnp.where(lane == 0, bias, jnp.where(lane < 4, 1.0, 0.0)).astype(BF16)


def prepare_kernel(tok_ref, cot_ref, mrg_ref, col_ref, out_ref, exp_ref, shr_ref,
                   xc_ref, low_ref, merged_ref, wide_ref, shrink_ref):
    extra = xc_ref.shape[1] - tok_ref.shape[1]
    values = tok_ref[...]
    centred = (values - jnp.mean(values, -1, keepdims=True)).astype(BF16)
    blank = jnp.zeros((values.shape[0], extra, values.shape[2]), BF16)
    xc_ref[...] = jnp.concatenate([centred, blank], 1)
    low_ref[...] = jnp.concatenate([cot_ref[...].astype(BF16), blank], 1)

    @pl.when(pl.program_id(0) == 0)
    def _():
        first = mrg_ref.shape[1]
        merged_ref[:, :first] = mrg_ref[...].astype(BF16)
        merged_ref[:, first:] = col_ref[...].astype(BF16)
        first = out_ref.shape[1]
        wide_ref[:, :first] = out_ref[...].astype(BF16)
        wide_ref[:, first:] = exp_ref[...].astype(BF16)
        shrink_ref[...] = shr_ref[...].astype(BF16)


def prepare(tokens, cotangent, merged, columns, output, expand, shrink, padded):
    clips, segment, width = tokens.shape
    some = 3 if clips % 3 == 0 else 1
    wide = pl.BlockSpec((some, segment, width), lambda i: (i, 0, 0))
    out = pl.BlockSpec((some, padded, width), lambda i: (i, 0, 0))
    shape = jax.ShapeDtypeStruct((clips, padded, width), BF16)
    shards = [(merged.shape[0], merged.shape[1] + columns.shape[1]),
              (output.shape[0], output.shape[1] + expand.shape[1]), shrink.shape]
    return pl.pallas_call(
        prepare_kernel, grid=(clips // some,),
        in_specs=[wide, wide] + [pl.BlockSpec(w.shape, lambda i: (0, 0)) for w in (merged, columns, output, expand, shrink)],
        out_specs=[out, out] + [pl.BlockSpec(s, lambda i: (0, 0)) for s in shards],
        out_shape=[shape, shape] + [jax.ShapeDtypeStruct(s, BF16) for s in shards],
        compiler_params=pltpu.CompilerParams(dimension_semantics=("arbitrary",), vmem_limit_bytes=LIMIT),
        name="prepare")(tokens, cotangent, merged, columns, output, expand, shrink)


RATES = (MATRIX_RATE, MATRIX_RATE, MATRIX_RATE, MATRIX_RATE, VECTOR_RATE)
DECAYS = (MATRIX_DECAY, MATRIX_DECAY, MATRIX_DECAY, MATRIX_DECAY, 0.0)


def finish_kernel(tok_ref, cot_ref, act_ref, dlt_ref, norm_ref, *refs):
    refs, out_ref, grad_ref = refs[:-2], refs[-2], refs[-1]
    segment = tok_ref.shape[1]
    out_ref[...] = tok_ref[...] + act_ref[...].astype(F32)[:, :segment]
    grad_ref[...] = cot_ref[...] + dlt_ref[...].astype(F32)[:, :segment]

    @pl.when(pl.program_id(0) == 0)
    def _():
        adamw_step(norm_ref, *refs)


def adamw_step(norm_ref, *refs):
    weights, firsts, seconds, shares = refs[:5], refs[5:10], refs[10:15], refs[15:20]
    outs = refs[20:]
    factor = CLIP_LIMIT / jnp.maximum(jnp.sqrt(norm_ref[0:1, 0:1]), CLIP_LIMIT)
    for index in range(5):
        clipped = shares[index][...] * factor
        weight = weights[index][...]
        momentum = BETA_ONE * firsts[index][...] + (1.0 - BETA_ONE) * clipped
        variance = BETA_TWO * seconds[index][...] + (1.0 - BETA_TWO) * clipped * clipped
        mean_hat = momentum / (1.0 - BETA_ONE**STEP)
        var_hat = variance / (1.0 - BETA_TWO**STEP)
        updated = weight - RATES[index] * (
            mean_hat / (jnp.sqrt(var_hat) + ADAM_EPS) + DECAYS[index] * weight)
        for kind, value in enumerate((clipped, momentum, variance, updated)):
            outs[5 * kind + index][...] = value


def finish(tokens, cotangent, act, dlt, norm, weights, firsts, seconds, shares):
    clips, segment, width = tokens.shape
    some = 3 if clips % 3 == 0 else 1
    wide = pl.BlockSpec((some, segment, width), lambda i: (i, 0, 0))
    low = pl.BlockSpec((some,) + act.shape[1:], lambda i: (i, 0, 0))
    fixed = [pl.BlockSpec(a.shape, lambda i: (0, 0))
             for a in (norm, *weights, *firsts, *seconds, *shares)]
    outs = [jax.ShapeDtypeStruct(w.shape, F32) for w in weights] * 4 + [jax.ShapeDtypeStruct(tokens.shape, F32)] * 2
    return pl.pallas_call(
        finish_kernel, grid=(clips // some,), in_specs=[wide, wide, low, low] + fixed,
        out_specs=[pl.BlockSpec(w.shape, lambda i: (0, 0)) for w in weights] * 4 + [wide, wide], out_shape=outs,
        compiler_params=pltpu.CompilerParams(dimension_semantics=("arbitrary",), vmem_limit_bytes=LIMIT),
        name="finish")(tokens, cotangent, act, dlt, norm, *weights, *firsts, *seconds, *shares)


def shards(
    tokens, kept_time, kept_bands, cotangent,
    weight_merged, weight_output, weight_expand, weight_shrink, vectors,
    first_merged, first_output, first_expand, first_shrink, first_vectors,
    second_merged, second_output, second_expand, second_shrink, second_vectors,
):
    clip_count, segment, width = tokens.shape
    dp, blk = lax.axis_size("dp"), lax.axis_size("blk")
    own = lax.axis_index("blk")
    clips = clip_count // blk
    padded = -(-segment // 16) * 16
    total = clips * blk * padded
    rows = weight_merged.shape[0]
    ff = weight_expand.shape[1]
    cube = (2,) * (bits_of(dp) + bits_of(blk))

    columns = jnp.pad(vectors.T, ((0, 0), (0, LANES - vectors.shape[0])))
    xc_home, cot_home, merged_low, wide_low, shrink_low = prepare(
        tokens, cotangent, weight_merged, columns, weight_output, weight_expand, weight_shrink, padded)
    merged, xc = front(merged_low, xc_home, dp, blk, 0)
    merged = merged.reshape(width, merged_low.shape[1])
    xc = xc.reshape(total, width)
    vec = merged[:, 3 * width:3 * width + vectors.shape[0]].T.astype(F32)
    dead = key_columns(kept_time, kept_bands, blk, own, segment, padded)
    n1, qa, kv, mix, wide, shrink, cot = attn_fwd(
        xc, dead, merged, vec, wide_low, shrink_low, cot_home, clips, HEADS, dp, blk, 1)
    wide = wide.reshape(width, wide_low.shape[1])
    shrink = shrink.reshape(ff, width)
    cot = cot.reshape(total, width)
    act, dmid, grad_expand, grad_shrink, grad_output, early, expand_early, shrink_early = ffn(
        mix, xc, cot, wide, shrink, vec, blk * padded, dp, blk, 2)

    def by_device(grad):
        return grad.reshape(cube + (grad.shape[0] // (dp * blk), grad.shape[1]))

    sent = (clips, blk, padded, width)
    owners = (2,) * (len(cube) - bits_of(FF_CHUNKS))
    merged_share, vector_share, output_share, expand_share, shrink_share, norm, act_home, dlt_home = attn_bwd(
        xc, cot, dmid, dead, n1, qa, kv, mix, merged, wide, vec, early, expand_early, shrink_early,
        by_device(grad_expand), grad_shrink.reshape((-1,) + owners + weight_shrink.shape), by_device(grad_output),
        act.reshape(sent), clips, HEADS, dp, blk, 3)
    shares = [merged_share, output_share, expand_share, shrink_share, vector_share[:, :vectors.shape[0]].T]
    *steps_out, activations, token_grads = finish(
        tokens, cotangent, act_home, dlt_home, norm, (weight_merged, weight_output, weight_expand, weight_shrink, vectors),
        (first_merged, first_output, first_expand, first_shrink, first_vectors),
        (second_merged, second_output, second_expand, second_shrink, second_vectors), shares)
    return (activations, token_grads, jnp.sqrt(norm[0, 0]), *steps_out)


def solution(mesh):
    return jax.shard_map(
        shards,
        mesh=mesh,
        in_specs=(
            P("dp", "blk", None),
            P("dp", None),
            P("dp", None),
            P("dp", "blk", None),
            P(("dp", "blk"), None),
            P(("dp", "blk"), None),
            P(("dp", "blk"), None),
            P(("dp", "blk"), None),
            P(None, ("dp", "blk")),
            P(("dp", "blk"), None),
            P(("dp", "blk"), None),
            P(("dp", "blk"), None),
            P(("dp", "blk"), None),
            P(None, ("dp", "blk")),
            P(("dp", "blk"), None),
            P(("dp", "blk"), None),
            P(("dp", "blk"), None),
            P(("dp", "blk"), None),
            P(None, ("dp", "blk")),
        ),
        out_specs=(
            P("dp", "blk", None),
            P("dp", "blk", None),
            P(),
            P(("dp", "blk"), None),
            P(("dp", "blk"), None),
            P(("dp", "blk"), None),
            P(("dp", "blk"), None),
            P(None, ("dp", "blk")),
            P(("dp", "blk"), None),
            P(("dp", "blk"), None),
            P(("dp", "blk"), None),
            P(("dp", "blk"), None),
            P(None, ("dp", "blk")),
            P(("dp", "blk"), None),
            P(("dp", "blk"), None),
            P(("dp", "blk"), None),
            P(("dp", "blk"), None),
            P(None, ("dp", "blk")),
            P(("dp", "blk"), None),
            P(("dp", "blk"), None),
            P(("dp", "blk"), None),
            P(("dp", "blk"), None),
            P(None, ("dp", "blk")),
        ),
        check_vma=False,
    )
```

```python
import functools
import jax
import jax.numpy as jnp
from jax import lax
from jax.experimental import pallas as pl
from jax.experimental.pallas import tpu as pltpu
from jax.sharding import PartitionSpec as P

HEADS = 12
STEP = 5
CLIP_LIMIT = 1.0
BETA_ONE = 0.5
BETA_TWO = 0.5
ADAM_EPS = 1e-08
MATRIX_RATE = 0.1
VECTOR_RATE = 0.3
MATRIX_DECAY = 0.05

F32, BF16 = jnp.float32, jnp.bfloat16
EPS = 1e-06
HALF = 64
LANES = 128
LIMIT = 127 * 512 * 1024
MESH = pl.DeviceIdType.MESH

FWD_LETTERS = ["XaYb", "baXY", "abYX", "abXY", "bXYa", "aYbX", "XbaY", "bXYa"]
FWD_PLAN = {1: [-1], 3: [0], 4: [2, 1, 6, 3], 5: [4, 5], 6: [7, 0], 7: [5, 1, 2], 9: [4, -2], 10: [7, 6], 11: [0],
            12: [1, 3, 2], 13: [4], 16: [7, 5, 6], 17: [-3],
            -1: [3, 1, 2, 1, 2, 0, 4, 6, 0, 4, 5, 6, 3, 7, 5, 3, 7]}
FF_CHUNKS = 4
FFN_LETTERS = ["aXYb", "aYXb"]
FFN_ROOTS = ["XY", "XY"]
FFN_PLAN = {8: [0, 2], 11: [0, 2], 13: [0, 2], 14: [1, 3], 15: [0], 17: [2, 3], 18: [1], 19: [0, 3], 20: [1], 22: [1],
            23: [3], -1: [1]}
BWD_LETTERS = ["YbaX", "bYaX", "aYbX"]
BWD_ROOTS = ["YX", "XY"]
BWD_PLAN = {0: [-1], 2: [0, 1, 2, 3, 4], 5: [-2], 6: [0, 4], 7: [1, 2, 3], 9: [4, -3], 11: [0, 1], 12: [2],
            13: [4, 0, 3], 14: [1], 15: [2], -1: [3, 0, 1, 2]}
END_LETTERS = ["abYX", "XYab", "YbaX", "XYba", "XaYb"]
END_PLAN = {4: [0], 6: [1], 7: [0, 2, 3, 4], -1: [1, 2, 3, 4, 0, 1, 3, 4, 2, 0, 1, 4, 2, 3, 0, 1, 4, 2, 3]}


def nn(a, b):
    return lax.dot_general(a, b, (((1,), (0,)), ((), ())), preferred_element_type=F32)


def nt(a, b):
    return lax.dot_general(a, b, (((1,), (1,)), ((), ())), preferred_element_type=F32)


def tn(a, b):
    return lax.dot_general(a, b, (((0,), (0,)), ((), ())), preferred_element_type=F32)


def norm_stats(v):
    centre = jnp.mean(v, -1, keepdims=True)
    c = v - centre
    spread = jnp.mean(c * c, -1, keepdims=True)
    r = lax.rsqrt(spread + EPS)
    return c * r, r


def norm_back(xhat, r, dy, gain):
    dx = dy * gain
    m1 = jnp.mean(dx, -1, keepdims=True)
    m2 = jnp.mean(dx * xhat, -1, keepdims=True)
    return (dx - m1 - xhat * m2) * r


def gelu_pair(x):
    z = jnp.abs(x)
    t = 1.0 / (1.0 + 0.3275911 * 0.7071067811865476 * z)
    e = jnp.exp(-0.5 * x * x)
    poly = t * (0.127414796 + t * (-0.142248368 + t * (0.7107068705 + t * (-0.7265760135 + t * 0.5307027145))))
    tail = poly * e
    phi = jnp.where(x >= 0, 1.0 - tail, tail)
    return x * phi, phi + (0.3989422804014327 * x) * e


def ffn_kernel(cube, letters, plan, mix_ref, xc_ref, cot_ref, prj_ref, exp_ref, shr_ref, vec_ref,
               act_ref, dmid_ref, ge_ref, gs_ref, go_ref, sums_ref, share_ref, shrink_ref,
               n2_s, y_s, dn_s, ae_s, as_s, ao_s, *refs):
    f, i = pl.program_id(0), pl.program_id(1)
    nf, ni = pl.num_programs(0), pl.num_programs(1)
    rows, width = mix_ref.shape
    here = pl.ds(pl.multiple_of(i * rows, rows), rows)
    cube.bind()
    n_p = len(letters)
    ready, held = refs[:n_p], refs[n_p:2 * n_p]
    landed = [refs[2 * n_p + k * cube.count:2 * n_p + (k + 1) * cube.count] for k in range(n_p)]
    refs = refs[n_p * (2 + cube.count):]
    send, recv, local = refs[:3]
    gs_ready, refs = refs[3:3 + n_p], refs[3 + n_p:]
    reduces = [Reduce(cube, ready[k], slice(None), letters[k], held[k], landed[k],
                      share_ref.at[:, pl.ds(k * width, width)], send.at[k], recv.at[k], local.at[k])
               for k in range(n_p)]
    reduces += root_reduces(cube, gs_ready, range(n_p), FF_CHUNKS, FFN_ROOTS, shrink_ref, refs)
    points = Points(plan, reduces, None)

    @pl.when((f == 0) & (i == 0))
    def _():
        cube.barrier()
        shrink_ref[...] = jnp.zeros_like(shrink_ref)
        sums_ref[...] = jnp.zeros_like(sums_ref)

    @pl.when(f == 0)
    def _():
        mid = xc_ref[...].astype(F32) + nn(mix_ref[...], prj_ref[...]) + vec_ref[4:5, :]
        xhat, _ = norm_stats(mid)
        n2_s[here, :] = (xhat * vec_ref[5:6, :] + vec_ref[6:7, :]).astype(BF16)

    points.visit(2 * (f * ni + i), 0)
    n2 = n2_s[here, :]
    d2 = cot_ref[...]
    h = nn(n2, exp_ref[...]) + vec_ref[pl.ds(8 + f, 1), :]
    dg = nt(d2, shr_ref[...])
    g, gp = gelu_pair(h)
    g = g.astype(BF16)
    dh32 = gp * dg
    dh = dh32.astype(BF16)
    sums_ref[pl.ds(8 + f, 1), :] += jnp.sum(dh32, 0, keepdims=True)
    y = nn(g, shr_ref[...])
    dn = nt(dh, exp_ref[...])

    @pl.when(f == 0)
    def _():
        y_s[here, :] = y
        dn_s[here, :] = dn

    @pl.when(f > 0)
    def _():
        y_s[here, :] += y
        dn_s[here, :] += dn

    points.visit(2 * (f * ni + i) + 1, 1)
    ge = tn(n2, dh)
    gs = tn(g, d2)

    @pl.when(i == 0)
    def _():
        ae_s[...] = ge
        as_s[...] = gs

    @pl.when((i > 0) & (i < ni - 1))
    def _():
        ae_s[...] += ge
        as_s[...] += gs

    @pl.when(i == ni - 1)
    def _():
        full_s = (as_s[...] + gs).astype(BF16)
        full = (ae_s[...] + ge).astype(BF16)
        for chunk in range(n_p):
            @pl.when(f == chunk)
            def _():
                ready[chunk][...] = full.reshape(ready[chunk].shape)
                reduces[chunk].start()
                gs_ready[chunk][...] = full_s.reshape(gs_ready[chunk].shape)
                reduces[n_p + chunk].start()

        @pl.when(f >= n_p)
        def _():
            ge_ref[...] = full
            gs_ref[...] = full_s

    @pl.when(f == nf - 1)
    def _():
        mix = mix_ref[...]
        delta = nn(mix, prj_ref[...]) + vec_ref[4:5, :]
        mid = xc_ref[...].astype(F32) + delta
        cot = d2.astype(F32)
        xhat, r = norm_stats(mid)
        dy = dn_s[here, :]
        act_ref[...] = (delta + (y_s[here, :] + vec_ref[7:8, :])).astype(BF16)
        dmid = cot + norm_back(xhat, r, dy, vec_ref[5:6, :])
        dmid_ref[...] = dmid
        d_one = dmid.astype(BF16)
        sums_ref[4:5, :] += jnp.sum(d_one.astype(F32), 0, keepdims=True)
        go = tn(mix, d_one)

        @pl.when(i == 0)
        def _():
            ao_s[...] = go

        @pl.when(i > 0)
        def _():
            ao_s[...] += go

        @pl.when(i == ni - 1)
        def _():
            go_ref[...] = ao_s[...].astype(BF16)

        sums_ref[5:6, :] += jnp.sum(dy * xhat, 0, keepdims=True)
        sums_ref[6:7, :] += jnp.sum(dy, 0, keepdims=True)
        sums_ref[7:8, :] += jnp.sum(cot, 0, keepdims=True)

    @pl.when((f == nf - 1) & (i == ni - 1))
    def _():
        points.finish()


def ffn(mix, xc, cot, expand, shrink, vec, rows, dp, blk, cid):
    total, width = xc.shape
    cube = Cube(dp, blk)
    ff = expand.shape[1] - width
    nf, ni = ff // width, total // rows
    letters = FFN_LETTERS
    early = len(letters)
    chunk = (width // (dp * blk), width)
    own = (ff // (dp * blk), width)
    first = lambda f, i: (jnp.where((f == 0) | (f == nf - 1), i, ni - 1), 0)
    last = lambda f, i: (jnp.where(f == nf - 1, i, 0), 0)
    once = pl.Buffered(1)
    whole = lambda f, i: (0, 0)
    return pl.pallas_call(
        functools.partial(ffn_kernel, cube, letters, FFN_PLAN),
        grid=(nf, ni),
        in_specs=[
            pl.BlockSpec((rows, width), first),
            pl.BlockSpec((rows, width), first),
            pl.BlockSpec((rows, width), lambda f, i: (i, 0)),
            pl.BlockSpec((width, width), whole, pipeline_mode=once),
            pl.BlockSpec((width, width), lambda f, i: (0, f + 1)),
            pl.BlockSpec((width, width), lambda f, i: (f, 0)),
            pl.BlockSpec(vec.shape, whole),
        ],
        out_specs=[
            pl.BlockSpec((rows, width), last),
            pl.BlockSpec((rows, width), last),
            pl.BlockSpec((width, width), lambda f, i: (0, jnp.maximum(f - early, 0)), pipeline_mode=once),
            pl.BlockSpec((width, width), lambda f, i: (jnp.maximum(f - early, 0), 0), pipeline_mode=once),
            pl.BlockSpec((width, width), whole, pipeline_mode=once),
            pl.BlockSpec((16, width), whole),
            pl.BlockSpec((chunk[0], width * early), whole, pipeline_mode=once),
            pl.BlockSpec(own, whole, pipeline_mode=once),
        ],
        out_shape=[
            jax.ShapeDtypeStruct((total, width), BF16),
            jax.ShapeDtypeStruct((total, width), F32),
            jax.ShapeDtypeStruct((width, ff - early * width), BF16),
            jax.ShapeDtypeStruct((ff - early * width, width), BF16),
            jax.ShapeDtypeStruct((width, width), BF16),
            jax.ShapeDtypeStruct((16, width), F32),
            jax.ShapeDtypeStruct((chunk[0], width * early), F32),
            jax.ShapeDtypeStruct(own, F32),
        ],
        scratch_shapes=[
            pltpu.VMEM((total, width), BF16),
            pltpu.VMEM((total, width), F32),
            pltpu.VMEM((total, width), F32),
            pltpu.VMEM((width, width), F32),
            pltpu.VMEM((width, width), F32),
            pltpu.VMEM((width, width), F32),
        ] + [pltpu.VMEM((2,) * cube.count + chunk, BF16) for _ in letters]
        + reduce_scratch(cube, [chunk] * early)
        + [pltpu.VMEM((2,) * (cube.count - bits_of(FF_CHUNKS)) + own, BF16) for _ in letters]
        + root_scratch(cube, early, FF_CHUNKS, own),
        compiler_params=pltpu.CompilerParams(
            dimension_semantics=("arbitrary", "arbitrary"), vmem_limit_bytes=LIMIT, collective_id=cid,
            has_side_effects=True),
        name="ffn",
    )(mix, xc, cot, expand, expand, shrink, vec)


def attn_fwd_kernel(cube, parts, plan, heads, xc_ref, dead_ref, mrg_ref, vec_ref, wide_in, shrink_in, cot_in,
                    n1_ref, qa_ref, kv_ref, mix_ref, wide_out, shrink_out, cot_out,
                    pk_s, send, recv, local, t_send, t_recv, t_local):
    width = xc_ref.shape[1]
    seq = xc_ref.shape[0]
    pairs = heads // 2
    cube.bind()
    clip = pl.program_id(0)
    own = [pltpu.make_async_copy(wide_in, wide_out.at[tuple(cube.mine)], local.at[0]),
           pltpu.make_async_copy(shrink_in, shrink_out.at[tuple(cube.mine)], local.at[1])]
    gathers = [Gather(cube, (wide_in, shrink_in)[a], (wide_out, shrink_out)[a], pl.ds(first, size), letters,
                      send.at[n], recv.at[n]) for n, (a, first, size, letters) in enumerate(parts)]
    exchange = Exchange(cube, cot_in, cot_out, False, t_send, t_recv, t_local)
    points = Points(plan, gathers, exchange)

    @pl.when(clip == 0)
    def _():
        cube.barrier()
        for gather in gathers:
            gather.start()
        for copy in own:
            copy.start()
        for copy in own:
            copy.wait()

    xc = xc_ref[...].astype(F32)
    xhat, _ = norm_stats(xc)
    n1 = (xhat * vec_ref[0:1, :] + vec_ref[1:2, :]).astype(BF16)
    n1_ref[...] = n1
    for third in range(3):
        cols = pl.ds(third * width, width)
        part = nn(n1, mrg_ref[:, cols])
        if third != 1:
            part = part + vec_ref[2 + third // 2:3 + third // 2, :]
        part = part.astype(BF16)
        pk_s[:, cols] = part
        if third:
            kv_ref[:, pl.ds((third - 1) * width, width)] = part
    lane = lax.broadcasted_iota(jnp.int32, (seq, LANES), 1)
    low = lane < HALF
    in_half = lane % HALF
    dead = dead_ref[...]
    ones = jnp.ones((seq, LANES), BF16)

    def pair(p, _):
        points.visit(clip * pairs + p)
        qcols = pl.ds(pl.multiple_of(p * LANES, LANES), LANES)
        kcols = pl.ds(pl.multiple_of(width + p * LANES, LANES), LANES)
        vcols = pl.ds(pl.multiple_of(2 * width + p * LANES, LANES), LANES)
        q = pk_s[:, qcols] * jnp.array(0.125, BF16)
        k = pk_s[:, kcols]
        v = pk_s[:, vcols]
        outs = []
        for side in range(2):
            mine = low if side == 0 else ~low
            qs = jnp.where(mine, q, jnp.where(in_half == 0, 1.0, 0.0).astype(BF16))
            ks = jnp.where(mine, k, dead)
            vs = jnp.where(mine, v, ones)
            s = nt(qs, ks)
            top = jnp.max(s, -1, keepdims=True)
            e = jnp.exp(s - top).astype(BF16)
            o = nn(e, vs)
            swapped = pltpu.roll(o, HALF, 1)
            outs.append(o / swapped)
            lse = top + jnp.log(jnp.where(mine, swapped, o))
            hi = (-lse).astype(BF16)
            rest = -lse - hi.astype(F32)
            mid_part = rest.astype(BF16)
            lo = (rest - mid_part.astype(F32)).astype(BF16)
            extra = jnp.where(in_half == 0, 1.0, 0.0).astype(BF16)
            extra = jnp.where(in_half == 1, hi, extra)
            extra = jnp.where(in_half == 2, mid_part, extra)
            extra = jnp.where(in_half == 3, lo, extra)
            qa_ref[2 * p + side] = jnp.where(mine, q, extra)
        mix_ref[:, qcols] = jnp.where(low, outs[0], outs[1]).astype(BF16)
        return 0

    lax.fori_loop(0, pairs, pair, 0)

    @pl.when(clip == pl.num_programs(0) - 1)
    def _():
        points.finish()
        for part in range(exchange.clips):
            exchange.wait(part)


class Points:
    def __init__(self, plan, movers, exchange):
        self.movers, self.exchange = movers, exchange
        self.plan, taken = {}, {}
        for point in sorted(plan, key=lambda p: p if p >= 0 else 1 << 20):
            self.plan[point] = []
            for which in plan[point]:
                self.plan[point].append((which, taken.get(which, 0)))
                taken[which] = taken.get(which, 0) + 1

    def act(self, point):
        for which, step in self.plan[point]:
            if which < 0:
                self.exchange.start(-1 - which)
            else:
                self.movers[which].advance(step)

    def visit(self, now, at=None, period=2, limit=1 << 20):
        for point in self.plan:
            if point < 0 or point >= limit or (at is not None and point % period != at):
                continue

            @pl.when(now == point)
            def _():
                self.act(point)

    def finish(self):
        self.act(-1)


def attn_fwd(xc, dead, merged, vec, wide, shrink, cot, clips, heads, dp, blk, cid):
    total, width = xc.shape
    seq = total // clips
    cube = Cube(dp, blk)
    whole = lambda c: (0, 0)
    row = lambda c: (c, 0)
    anywhere = pl.BlockSpec(memory_space=pl.ANY)
    fifth, third = wide.shape[1] // 5, shrink.shape[1] // 3
    parts = [(0, m * fifth, fifth, FWD_LETTERS[m]) for m in range(5)]
    parts += [(1, m * third, third, FWD_LETTERS[5 + m]) for m in range(3)]
    return pl.pallas_call(
        functools.partial(attn_fwd_kernel, cube, parts, FWD_PLAN, heads),
        grid=(clips,),
        in_specs=[
            pl.BlockSpec((seq, width), row),
            pl.BlockSpec((seq, LANES), row),
            pl.BlockSpec(merged.shape, whole),
            pl.BlockSpec(vec.shape, whole),
            pl.BlockSpec(wide.shape, whole),
            pl.BlockSpec(shrink.shape, whole),
            anywhere,
        ],
        out_specs=[
            pl.BlockSpec((seq, width), row),
            pl.BlockSpec((heads, seq, LANES), lambda c: (0, c, 0)),
            pl.BlockSpec((seq, 2 * width), row),
            pl.BlockSpec((seq, width), row),
            anywhere, anywhere, anywhere,
        ],
        out_shape=[
            jax.ShapeDtypeStruct((total, width), BF16),
            jax.ShapeDtypeStruct((heads, total, LANES), BF16),
            jax.ShapeDtypeStruct((total, 2 * width), BF16),
            jax.ShapeDtypeStruct((total, width), BF16),
            jax.ShapeDtypeStruct((2,) * cube.count + wide.shape, BF16),
            jax.ShapeDtypeStruct((2,) * cube.count + shrink.shape, BF16),
            jax.ShapeDtypeStruct((clips, blk) + cot.shape[1:], BF16),
        ],
        scratch_shapes=[
            pltpu.VMEM((seq, 3 * width), BF16),
            pltpu.SemaphoreType.DMA((len(parts), cube.count)),
            pltpu.SemaphoreType.DMA((len(parts), cube.count)),
            pltpu.SemaphoreType.DMA((2,)),
        ] + exchange_semaphores(clips, blk),
        compiler_params=pltpu.CompilerParams(
            dimension_semantics=("arbitrary",), vmem_limit_bytes=LIMIT, collective_id=cid, has_side_effects=True),
        name="attn_fwd",
    )(xc, dead, merged, vec, wide, shrink, cot)


def attn_bwd_kernel(cube, late, tail, plan, heads, xc_ref, cot_ref, dmid_ref, dead_ref, n1_ref, qa_ref, kv_ref, mix_ref,
                    mrg_ref, out_ref, vec_ref, early_ref, ge_early, gs_early,
                    ge_in, gs_in, go_in, act_in,
                    gm_out, gv_out, go_out, ge_out, gs_out, norm_ref, act_out, dlt_out,
                    dm_s, dp_s, nt_s, am_s, gm_s, gl_s, gw_s, gx_s, dlt_s, sums_ref, *refs):
    c = pl.program_id(0)
    n = pl.num_programs(0)
    seq, width = xc_ref.shape
    pairs = heads // 2
    cube.bind()

    def take(count):
        nonlocal refs
        taken, refs = refs[:count], refs[count:]
        return taken

    def sums_of(parts, sources, outs):
        count = len(parts)
        held = take(count)
        landed = [take(cube.count) for _ in parts]
        send, recv, local = take(3)
        return [Reduce(cube, sources[a], pl.ds(first, size), letters, held[m], landed[m], outs[a],
                       send.at[m], recv.at[m], local.at[m]) for m, (a, first, size, letters) in enumerate(parts)]

    reduces = sums_of(late, (ge_in, go_in), (gx_s, go_out))
    roots = FF_CHUNKS - gs_in.shape[0]
    count = gs_in.shape[0]
    reduces += root_reduces(cube, [gs_in.at[m] for m in range(count)], range(roots, FF_CHUNKS), FF_CHUNKS, BWD_ROOTS,
                            gl_s, take(4 * count + count * (cube.count - bits_of(FF_CHUNKS)) - count + 3))
    ends = sums_of(tail, (gm_s,), (gw_s,))
    exchange = Exchange(cube, act_in, act_out, True, *take(3))
    homeward = Exchange(cube, dlt_s, dlt_out, True, *take(3))
    sums, s_send, s_recv = refs
    points = Points(plan, reduces, exchange)
    finale = Points(END_PLAN, ends, None)

    @pl.when(c == 0)
    def _():
        cube.barrier()
        for reduce in reduces:
            reduce.start()
        gl_s[...] = jnp.zeros_like(gl_s)
        sums_ref[...] = early_ref[...]
        am_s[...] = jnp.zeros_like(am_s)

    d_one = dmid_ref[...].astype(BF16)
    dm_s[...] = nt(d_one, out_ref[...]).astype(BF16)
    nt_s[...] = jnp.transpose(n1_ref[...])
    group = 3 * LANES

    def by_device(values):
        return values.astype(BF16).reshape((2,) * cube.count + (width // (1 << cube.count), values.shape[1]))

    lane = lax.broadcasted_iota(jnp.int32, (seq, LANES), 1)
    low = lane < HALF
    in_half = lane % HALF
    dead = dead_ref[...]
    vone = jnp.where(in_half < 2, 1.0, 0.0).astype(BF16)

    def pair(p, _):
        points.visit(c * pairs + p)
        finale.visit(jnp.where(c == n - 1, p, -1), limit=pairs)
        qcols = pl.ds(pl.multiple_of(p * LANES, LANES), LANES)
        kcols = pl.ds(pl.multiple_of(width + p * LANES, LANES), LANES)
        vcols = pl.ds(pl.multiple_of(2 * width + p * LANES, LANES), LANES)
        k = kv_ref[:, qcols]
        v = kv_ref[:, kcols]
        dm = dm_s[:, qcols]
        prod = dm.astype(F32) * mix_ref[:, qcols].astype(F32)
        k_t = jnp.transpose(k)
        dks, dvs, dqs = [], [], []
        for side in range(2):
            mine = low if side == 0 else ~low
            qa = qa_ref[2 * p + side]
            ka = jnp.where(mine, k, dead)
            va = jnp.where(mine, v, vone)
            dd = -jnp.sum(jnp.where(mine, prod, 0.0), -1, keepdims=True)
            hi = dd.astype(BF16)
            lo = (dd - hi.astype(F32)).astype(BF16)
            da = jnp.where(mine, dm, jnp.where(in_half == 0, hi, lo))
            p_t = jnp.exp(nt(ka, qa))
            ds_t = (p_t * nt(va, da)).astype(BF16)
            dvs.append(nn(p_t.astype(BF16), da))
            dks.append(nn(ds_t, qa))
            dqs.append(nn(k_t[side * HALF:(side + 1) * HALF, :], ds_t))
        dq = jnp.transpose(jnp.concatenate(dqs, 0)) * 0.125
        dk = jnp.where(low, dks[0], dks[1])
        dv = jnp.where(low, dvs[0], dvs[1])
        sums_ref[2:3, qcols] += jnp.sum(dq, 0, keepdims=True)
        sums_ref[3:4, qcols] += jnp.sum(dv, 0, keepdims=True)
        three = jnp.concatenate([dq, dk, dv], 1).astype(BF16)
        dp_s[:, qcols] = three[:, :LANES]
        dp_s[:, kcols] = three[:, LANES:2 * LANES]
        dp_s[:, vcols] = three[:, 2 * LANES:]
        mine = pl.ds(pl.multiple_of(p * group, group), group)
        grad = am_s[:, mine] + nn(nt_s[...], three)
        am_s[:, mine] = grad

        @pl.when(c == n - 1)
        def _():
            gm_s[(slice(None),) * (cube.count + 1) + (mine,)] = by_device(grad)
            for m, (_, first, size, _) in enumerate(tail[:-1]):
                @pl.when(first + size == (p + 1) * group)
                def _():
                    ends[m].start()

        return 0

    lax.fori_loop(0, pairs, pair, 0)
    dp = dp_s[...]

    @pl.when(c == n - 1)
    def _():
        finale.act(pairs)

    dy = nt(dp, mrg_ref[:, :3 * width])
    xhat, r = norm_stats(xc_ref[...].astype(F32))
    sums_ref[0:1, :] += jnp.sum(dy * xhat, 0, keepdims=True)
    sums_ref[1:2, :] += jnp.sum(dy, 0, keepdims=True)
    delta = ((dmid_ref[...] - cot_ref[...].astype(F32)) + norm_back(xhat, r, dy, vec_ref[0:1, :])).astype(BF16)
    dlt_s[c] = delta.reshape(dlt_s.shape[1:])
    for clip in range(homeward.clips - 1):
        @pl.when(c == clip)
        def _():
            homeward.start(clip)

    @pl.when(c == n - 1)
    def _():
        columns = jnp.transpose(sums_ref[...])
        blank = jnp.zeros((width, LANES - columns.shape[1]), F32)
        gm_s[(slice(None),) * (cube.count + 1) + (pl.ds(3 * width, LANES),)] = by_device(
            jnp.concatenate([columns, blank], 1))
        ends[-1].start()
        finale.act(pairs + 1)
        homeward.start(homeward.clips - 1)
        points.finish()
        finale.finish()
        shrink = gs_early[...] + gl_s[...]
        gs_out[...] = shrink
        part = ge_early.shape[1]
        ge_out[:, :part] = ge_early[...]
        ge_out[:, part:] = gx_s[...]
        total = jnp.sum(shrink * shrink) + jnp.sum(go_out[...] * go_out[...])
        total = total + jnp.sum(ge_early[...] * ge_early[...]) + jnp.sum(gx_s[...] * gx_s[...])
        for p in range(pairs):
            for third in range(3):
                gm_out[:, third * width + p * LANES:third * width + (p + 1) * LANES] = (
                    gw_s[:, p * group + third * LANES:p * group + (third + 1) * LANES])
        gv_out[...] = gw_s[:, 3 * width:]
        total = total + jnp.sum(gw_s[...] * gw_s[...])
        norm_ref[...] = sum_everywhere(cube, total, sums, s_send, s_recv)
        for clip in range(homeward.clips):
            exchange.wait(clip)
            homeward.wait(clip)


def attn_bwd(xc, cot, dmid, dead, n1, qa, kv, mix, merged, output, vec, early, expand_early, shrink_early,
             grad_expand, grad_shrink, grad_output, act, clips, heads, dp, blk, cid):
    total, width = xc.shape
    seq = total // clips
    cube = Cube(dp, blk)
    whole = lambda c: (0, 0)
    row = lambda c: (c, 0)
    once = pl.Buffered(1)
    anywhere = pl.BlockSpec(memory_space=pl.ANY)
    rows, own = grad_expand.shape[-2], grad_shrink.shape[-2:]
    half = grad_expand.shape[-1] // 2
    late = [(0, 0, half, BWD_LETTERS[0]), (0, half, half, BWD_LETTERS[1]), (1, 0, width, BWD_LETTERS[2])]
    sixth = width // 2
    cuts = [0, 2 * sixth, 4 * sixth, 5 * sixth, 6 * sixth, merged.shape[1]]
    tail = [(0, cuts[m], cuts[m + 1] - cuts[m], END_LETTERS[m]) for m in range(5)]
    fixed = [(rows, 3 * width), (rows, merged.shape[1] - 3 * width), (rows, width),
             (rows, expand_early.shape[1] + 2 * half), own, (8, LANES)]
    home = (clips * blk,) + act.shape[2:]
    return pl.pallas_call(
        functools.partial(attn_bwd_kernel, cube, late, tail, BWD_PLAN, heads),
        grid=(clips,),
        in_specs=[
            pl.BlockSpec((seq, width), row),
            pl.BlockSpec((seq, width), row),
            pl.BlockSpec((seq, width), row),
            pl.BlockSpec((seq, LANES), row),
            pl.BlockSpec((seq, width), row),
            pl.BlockSpec((heads, seq, LANES), lambda c: (0, c, 0)),
            pl.BlockSpec((seq, 2 * width), row),
            pl.BlockSpec((seq, width), row),
            pl.BlockSpec(merged.shape, whole, pipeline_mode=once),
            pl.BlockSpec((width, width), whole, pipeline_mode=once),
            pl.BlockSpec(vec.shape, whole),
            pl.BlockSpec(early.shape, whole),
            pl.BlockSpec(expand_early.shape, whole, pipeline_mode=once),
            pl.BlockSpec(shrink_early.shape, whole, pipeline_mode=once),
            anywhere, anywhere, anywhere, anywhere,
        ],
        out_specs=[pl.BlockSpec(s, whole, pipeline_mode=once) for s in fixed] + [anywhere, anywhere],
        out_shape=[jax.ShapeDtypeStruct(s, F32) for s in fixed] + [jax.ShapeDtypeStruct(home, BF16)] * 2,
        scratch_shapes=[
            pltpu.VMEM((seq, width), BF16),
            pltpu.VMEM((seq, 3 * width), BF16),
            pltpu.VMEM((width, seq), BF16),
            pltpu.VMEM((width, 3 * width), F32),
            pltpu.VMEM((2,) * cube.count + (rows, merged.shape[1]), BF16),
            pltpu.VMEM(own, F32),
            pltpu.VMEM((rows, merged.shape[1]), F32),
            pltpu.VMEM((rows, 2 * half), F32),
            pltpu.VMEM(act.shape, BF16),
            pltpu.VMEM((16, width), F32),
        ] + reduce_scratch(cube, [(rows, size) for _, _, size, _ in late])
        + root_scratch(cube, grad_shrink.shape[0], FF_CHUNKS, own)
        + reduce_scratch(cube, [(rows, size) for _, _, size, _ in tail])
        + exchange_semaphores(clips, blk) + exchange_semaphores(clips, blk) + sum_scratch(dp, blk),
        compiler_params=pltpu.CompilerParams(
            dimension_semantics=("arbitrary",), vmem_limit_bytes=LIMIT, collective_id=cid, has_side_effects=True),
        name="attn_bwd",
    )(xc, cot, dmid, dead, n1, qa, kv, mix, merged, output, vec, early, expand_early, shrink_early,
      grad_expand, grad_shrink, grad_output, act)


def bits_of(size):
    return size.bit_length() - 1


class Cube:
    def __init__(self, dp, blk):
        self.sizes = (dp, blk)
        self.n_dp, self.n_blk = bits_of(dp), bits_of(blk)
        self.count = self.n_dp + self.n_blk
        far = list(range(self.n_dp - 1))
        self.letters = {"X": list(range(self.n_dp, self.count - 1)), "Y": [self.n_dp - 1],
                        "a": far[-1:], "b": far[:-1], "C": [self.count - 1]}

    def bind(self):
        self.at_dp, self.at_blk = lax.axis_index("dp"), lax.axis_index("blk")
        self.mine = [lax.rem(self.at_dp // (1 << (self.n_dp - 1 - k)), 2) for k in range(self.n_dp)]
        self.mine += [lax.rem(self.at_blk // (1 << (self.n_blk - 1 - k)), 2) for k in range(self.n_blk)]
        return self

    def partner(self, bit):
        if bit < self.n_dp:
            step = 1 << (self.n_dp - 1 - bit)
            return (self.at_dp + step - 2 * step * self.mine[bit], self.at_blk)
        step = 1 << (self.count - 1 - bit)
        return (self.at_dp, self.at_blk + step - 2 * step * self.mine[bit])

    def row_peer(self, offset):
        return (self.at_dp, lax.rem(self.at_blk + offset, self.sizes[1]))

    def column_peer(self, offset):
        return (lax.rem(self.at_dp + offset, self.sizes[0]), self.at_blk)

    def barrier(self):
        sem = pltpu.get_barrier_semaphore()
        others = [self.row_peer(k) for k in range(1, self.sizes[1])]
        others += [self.column_peer(k) for k in range(1, self.sizes[0])]
        for other in others:
            pl.semaphore_signal(sem, inc=1, device_id=other, device_id_type=MESH)
        pl.semaphore_wait(sem, len(others))


def remote(src, dst, send, recv, device):
    return pltpu.make_async_remote_copy(
        src_ref=src, dst_ref=dst, send_sem=send, recv_sem=recv, device_id=device, device_id_type=MESH)


class Gather:
    def __init__(self, cube, src, dst, cols, letters, send, recv):
        self.cube, self.src, self.dst, self.cols = cube, src, dst, cols
        self.steps = [cube.letters[letter] for letter in letters + "C"]
        self.order = sum(self.steps, [])
        self.send, self.recv = send, recv

    def copy(self, s):
        cube = self.cube
        sel = tuple(slice(None) if bit in self.order[:s] else cube.mine[bit] for bit in range(cube.count))
        there = self.dst.at[sel + (slice(None), self.cols)]
        here = self.src.at[:, self.cols] if s == 0 else there
        return remote(here, there, self.send.at[s], self.recv.at[s], cube.partner(self.order[s]))

    def start(self):
        self.copy(0).start()

    def advance(self, step):
        first = sum(len(bits) for bits in self.steps[:step])
        for s in range(first, first + len(self.steps[step])):
            self.copy(s).wait()
            if s + 1 < len(self.order):
                self.copy(s + 1).start()


class Reduce:
    def __init__(self, cube, src, cols, letters, held, landed, out, send, recv, local):
        self.cube, self.src, self.cols, self.held, self.landed = cube, src, cols, held, landed
        self.dims = range(cube.count)
        self.steps = [cube.letters[letter] for letter in "C" + letters]
        self.order = sum(self.steps, [])
        self.out = out
        self.send, self.recv, self.local = send, recv, local

    def part(self, s, kept):
        cube = self.cube
        sel = []
        for bit in self.dims:
            if bit in self.order[:s]:
                pick = cube.mine[bit]
            elif bit == self.order[s]:
                pick = cube.mine[bit] if kept else 1 - cube.mine[bit]
            else:
                pick = slice(None)
            sel.append(pick)
        return tuple(sel)

    def own(self):
        return pltpu.make_async_copy(
            self.src.at[self.part(0, True) + (slice(None), self.cols)], self.held, self.local)

    def copy(self, s):
        if s == 0:
            here = self.src.at[self.part(0, False) + (slice(None), self.cols)]
        else:
            here = self.held.at[self.part(s, False)[:-1]]
        return remote(here, self.landed[s], self.send.at[s], self.recv.at[s], self.cube.partner(self.order[s]))

    def start(self):
        self.own().start()
        self.copy(0).start()

    def add(self, s):
        keep = self.part(s, True)[:-1]
        width = self.held.shape[-1]
        if s + 1 == len(self.order):
            self.last(self.held[keep].astype(F32) + self.landed[s][...].astype(F32))
            return
        wide = (slice(None),) * (len(self.landed[s].shape) - 1)
        tile = LANES * max(k for k in (1, 2, 3) if width % (LANES * k) == 0)

        def some(j, _):
            cols = (pl.ds(pl.multiple_of(j * tile, tile), tile),)
            at = keep + (slice(None),) + cols
            self.held[at] = self.held[at] + self.landed[s][wide + cols]
            return 0

        lax.fori_loop(0, width // tile, some, 0)

    def last(self, total):
        self.out[:, self.cols] = total

    def advance(self, step):
        first = sum(len(bits) for bits in self.steps[:step])
        for s in range(first, first + len(self.steps[step])):
            self.copy(s).wait()
            if s == 0:
                self.own().wait()
            self.add(s)
            if s + 1 < len(self.order):
                self.copy(s + 1).start()


class RootReduce(Reduce):
    def __init__(self, cube, chunk, chunks, src, letters, held, landed, partial, arrived, out, send, recv, local):
        lead = bits_of(chunks)
        super().__init__(cube, src, slice(None), letters, held, landed, out, send, recv, local)
        self.dims = range(lead, cube.count)
        near = {"X": cube.letters["X"], "Y": [b for b in cube.letters["b"] + cube.letters["a"] if b >= lead] + cube.letters["Y"]}
        self.steps = [cube.letters["C"]] + [near[letter] for letter in letters]
        self.order = sum(self.steps, [])
        self.chunk, self.chunks, self.partial, self.arrived = chunk, chunks, partial, arrived
        self.group = cube.at_dp // (cube.sizes[0] // chunks)

    def owner(self):
        cube, size = self.cube, self.cube.sizes[0] // self.chunks
        slot = lax.rem(self.group + 2 * self.chunks - self.chunk - 1, self.chunks)
        base = len(self.order)
        return remote(self.partial, self.arrived.at[slot], self.send.at[base], self.recv.at[base + slot],
                      (cube.at_dp + (self.chunk - self.group) * size, cube.at_blk))

    def last(self, total):
        @pl.when(self.group == self.chunk)
        def _():
            self.out[...] = total

        @pl.when(self.group != self.chunk)
        def _():
            self.partial[...] = total.astype(BF16)
            self.owner().start()

    def advance(self, step):
        if step < len(self.steps):
            super().advance(step)
            return

        @pl.when(self.group == self.chunk)
        def _():
            base = len(self.order)
            total = self.out[...]
            for slot in range(self.chunks - 1):
                remote(self.partial, self.arrived.at[slot], self.send.at[base], self.recv.at[base + slot],
                       (self.cube.at_dp, self.cube.at_blk)).wait_recv()
                total = total + self.arrived[slot].astype(F32)
            self.out[...] = total

        @pl.when(self.group != self.chunk)
        def _():
            self.owner().wait_send()


def root_scratch(cube, count, chunks, tail):
    rest = cube.count - bits_of(chunks)
    kinds = []
    for _ in range(count):
        kinds.append(pltpu.VMEM((2,) * (rest - 1) + tail, BF16))
    for _ in range(count):
        kinds += [pltpu.VMEM((2,) * (rest - 1 - s) + tail, BF16) for s in range(rest)]
    for _ in range(count):
        kinds += [pltpu.VMEM(tail, BF16), pltpu.VMEM((chunks - 1,) + tail, BF16)]
    sems = rest + chunks
    return kinds + [pltpu.SemaphoreType.DMA((count, sems)), pltpu.SemaphoreType.DMA((count, sems)),
                    pltpu.SemaphoreType.DMA((count,))]


def root_reduces(cube, sources, names, chunks, letters, out, refs):
    count, rest = len(names), cube.count - bits_of(chunks)
    held = refs[:count]
    landed = [refs[count + n * rest:count + (n + 1) * rest] for n in range(count)]
    refs = refs[count * (1 + rest):]
    send, recv, local = refs[2 * count:2 * count + 3]
    return [RootReduce(cube, names[n], chunks, sources[n], letters[n], held[n], landed[n], refs[2 * n], refs[2 * n + 1],
                       out, send.at[n], recv.at[n], local.at[n]) for n in range(count)]


class Exchange:
    def __init__(self, cube, src, dst, back, send, recv, local):
        self.cube, self.src, self.dst, self.back = cube, src, dst, back
        self.clips = (src if back else dst).shape[0]
        self.send, self.recv, self.local = send, recv, local

    def ends(self, to, clip):
        if self.back:
            return self.src.at[clip, to], self.dst.at[self.cube.at_blk * self.clips + clip]
        return self.src.at[to * self.clips + clip], self.dst.at[clip, self.cube.at_blk]

    def copies(self, clip):
        found = [pltpu.make_async_copy(*self.ends(self.cube.at_blk, clip), self.local.at[clip])]
        for k in range(1, self.cube.sizes[1]):
            other = self.cube.row_peer(k)
            found.append(remote(*self.ends(other[1], clip), self.send.at[clip, k - 1], self.recv.at[clip, k - 1], other))
        return found

    def start(self, clip):
        for copy in self.copies(clip):
            copy.start()

    def wait(self, clip):
        for copy in self.copies(clip):
            copy.wait()


def exchange_semaphores(clips, blk):
    return [pltpu.SemaphoreType.DMA((clips, blk)), pltpu.SemaphoreType.DMA((clips, blk)),
            pltpu.SemaphoreType.DMA((clips,))]


def front_kernel(cube, parts, plan, *refs):
    merged_in, xc_in, merged_out, xc_out, send, recv, local, t_send, t_recv, t_local = refs
    cube.bind().barrier()
    gathers = [Gather(cube, merged_in, merged_out, pl.ds(first, size), letters, send.at[k], recv.at[k])
               for k, (first, size, letters) in enumerate(parts)]
    for gather in gathers:
        gather.start()
    own = pltpu.make_async_copy(merged_in, merged_out.at[tuple(cube.mine)], local)
    own.start()
    exchange = Exchange(cube, xc_in, xc_out, False, t_send, t_recv, t_local)
    own.wait()
    points = Points({-1: plan}, gathers, exchange)
    points.finish()
    for clip in range(exchange.clips):
        exchange.wait(clip)


def front(merged, xc, dp, blk, cid):
    cube = Cube(dp, blk)
    clips = xc.shape[0] // blk
    anywhere = pl.BlockSpec(memory_space=pl.ANY)
    half = (merged.shape[1] // LANES + 1) // 2 * LANES
    parts = [(0, half, "XbYa"), (half, merged.shape[1] - half, "XabY")]
    plan = [0, 1] + [-1 - clip for clip in range(clips)] + [0, 1] * 4
    return pl.pallas_call(
        functools.partial(front_kernel, cube, parts, plan),
        in_specs=[pl.BlockSpec(memory_space=pltpu.VMEM), anywhere],
        out_specs=[anywhere] * 2,
        out_shape=[jax.ShapeDtypeStruct((2,) * cube.count + merged.shape, BF16),
                   jax.ShapeDtypeStruct((clips, blk) + xc.shape[1:], BF16)],
        scratch_shapes=[pltpu.SemaphoreType.DMA((len(parts), cube.count)),
                        pltpu.SemaphoreType.DMA((len(parts), cube.count)),
                        pltpu.SemaphoreType.DMA] + exchange_semaphores(clips, blk),
        compiler_params=pltpu.CompilerParams(collective_id=cid, has_side_effects=True, vmem_limit_bytes=LIMIT),
        name="front",
    )(merged, xc)


def sum_everywhere(cube, total, sums, send, recv):
    dp, blk = cube.sizes
    for axis, (size, peer, at) in enumerate(((dp, cube.column_peer, cube.at_dp), (blk, cube.row_peer, cube.at_blk))):
        box = sums[axis]
        box[at] = jnp.full(box.shape[1:], total, F32)
        copies = [remote(box.at[at], box.at[at], send[axis].at[k - 1], recv[axis].at[k - 1], peer(k))
                  for k in range(1, size)]
        for copy in copies:
            copy.start()
        for copy in copies:
            copy.wait()
        whole = box[0]
        for k in range(1, size):
            whole = whole + box[k]
        total = whole[0, 0]
    return whole


def sum_scratch(dp, blk):
    return [[pltpu.VMEM((dp, 8, LANES), F32), pltpu.VMEM((blk, 8, LANES), F32)],
            [pltpu.SemaphoreType.DMA((dp,)), pltpu.SemaphoreType.DMA((blk,))],
            [pltpu.SemaphoreType.DMA((dp,)), pltpu.SemaphoreType.DMA((blk,))]]


def reduce_scratch(cube, shapes):
    held = [pltpu.VMEM((2,) * (cube.count - 1) + s, BF16) for s in shapes]
    landed = [pltpu.VMEM((2,) * (cube.count - 1 - k) + s, BF16) for s in shapes for k in range(cube.count)]
    return held + landed + [pltpu.SemaphoreType.DMA((len(shapes), cube.count)),
                            pltpu.SemaphoreType.DMA((len(shapes), cube.count)),
                            pltpu.SemaphoreType.DMA((len(shapes),))]


def key_columns(kept_time, kept_bands, blocks, own, segment, padded):
    clips = kept_time.shape[0] // blocks
    kept_time = lax.dynamic_slice_in_dim(kept_time, own * clips, clips)
    kept_bands = lax.dynamic_slice_in_dim(kept_bands, own * clips, clips)
    columns = kept_time.shape[1] // blocks
    patches = kept_time.reshape(clips, blocks, columns, 1) * kept_bands[:, None, None, :]
    patches = patches.reshape(clips, blocks, columns * kept_bands.shape[1])
    leading = (jnp.arange(blocks, dtype=jnp.int32) == 0).astype(jnp.int32)
    special = jnp.broadcast_to(leading[None, :, None], (clips, blocks, segment - patches.shape[2]))
    live = jnp.concatenate([special, patches, jnp.zeros((clips, blocks, padded - segment), jnp.int32)], 2)
    bias = jnp.where(live > 0, 0.0, -1e30).reshape(-1, 1)
    lane = jnp.arange(LANES, dtype=jnp.int32)[None, :] % HALF
    return jnp.where(lane == 0, bias, jnp.where(lane < 4, 1.0, 0.0)).astype(BF16)


def prepare_kernel(tok_ref, cot_ref, mrg_ref, col_ref, out_ref, exp_ref, shr_ref,
                   xc_ref, low_ref, merged_ref, wide_ref, shrink_ref):
    extra = xc_ref.shape[1] - tok_ref.shape[1]
    values = tok_ref[...]
    centred = (values - jnp.mean(values, -1, keepdims=True)).astype(BF16)
    blank = jnp.zeros((values.shape[0], extra, values.shape[2]), BF16)
    xc_ref[...] = jnp.concatenate([centred, blank], 1)
    low_ref[...] = jnp.concatenate([cot_ref[...].astype(BF16), blank], 1)

    @pl.when(pl.program_id(0) == 0)
    def _():
        first = mrg_ref.shape[1]
        merged_ref[:, :first] = mrg_ref[...].astype(BF16)
        merged_ref[:, first:] = col_ref[...].astype(BF16)
        first = out_ref.shape[1]
        wide_ref[:, :first] = out_ref[...].astype(BF16)
        wide_ref[:, first:] = exp_ref[...].astype(BF16)
        shrink_ref[...] = shr_ref[...].astype(BF16)


def prepare(tokens, cotangent, merged, columns, output, expand, shrink, padded):
    clips, segment, width = tokens.shape
    some = 3 if clips % 3 == 0 else 1
    wide = pl.BlockSpec((some, segment, width), lambda i: (i, 0, 0))
    out = pl.BlockSpec((some, padded, width), lambda i: (i, 0, 0))
    shape = jax.ShapeDtypeStruct((clips, padded, width), BF16)
    shards = [(merged.shape[0], merged.shape[1] + columns.shape[1]),
              (output.shape[0], output.shape[1] + expand.shape[1]), shrink.shape]
    return pl.pallas_call(
        prepare_kernel, grid=(clips // some,),
        in_specs=[wide, wide] + [pl.BlockSpec(w.shape, lambda i: (0, 0)) for w in (merged, columns, output, expand, shrink)],
        out_specs=[out, out] + [pl.BlockSpec(s, lambda i: (0, 0)) for s in shards],
        out_shape=[shape, shape] + [jax.ShapeDtypeStruct(s, BF16) for s in shards],
        compiler_params=pltpu.CompilerParams(dimension_semantics=("arbitrary",), vmem_limit_bytes=LIMIT),
        name="prepare")(tokens, cotangent, merged, columns, output, expand, shrink)


RATES = (MATRIX_RATE, MATRIX_RATE, MATRIX_RATE, MATRIX_RATE, VECTOR_RATE)
DECAYS = (MATRIX_DECAY, MATRIX_DECAY, MATRIX_DECAY, MATRIX_DECAY, 0.0)


def finish_kernel(tok_ref, cot_ref, act_ref, dlt_ref, norm_ref, *refs):
    refs, out_ref, grad_ref = refs[:-2], refs[-2], refs[-1]
    segment = tok_ref.shape[1]
    out_ref[...] = tok_ref[...] + act_ref[...].astype(F32)[:, :segment]
    grad_ref[...] = cot_ref[...] + dlt_ref[...].astype(F32)[:, :segment]

    @pl.when(pl.program_id(0) == 0)
    def _():
        adamw_step(norm_ref, *refs)


def adamw_step(norm_ref, *refs):
    weights, firsts, seconds, shares = refs[:5], refs[5:10], refs[10:15], refs[15:20]
    outs = refs[20:]
    factor = CLIP_LIMIT / jnp.maximum(jnp.sqrt(norm_ref[0:1, 0:1]), CLIP_LIMIT)
    for index in range(5):
        clipped = shares[index][...] * factor
        weight = weights[index][...]
        momentum = BETA_ONE * firsts[index][...] + (1.0 - BETA_ONE) * clipped
        variance = BETA_TWO * seconds[index][...] + (1.0 - BETA_TWO) * clipped * clipped
        mean_hat = momentum / (1.0 - BETA_ONE**STEP)
        var_hat = variance / (1.0 - BETA_TWO**STEP)
        updated = weight - RATES[index] * (
            mean_hat / (jnp.sqrt(var_hat) + ADAM_EPS) + DECAYS[index] * weight)
        for kind, value in enumerate((clipped, momentum, variance, updated)):
            outs[5 * kind + index][...] = value


def finish(tokens, cotangent, act, dlt, norm, weights, firsts, seconds, shares):
    clips, segment, width = tokens.shape
    some = 3 if clips % 3 == 0 else 1
    wide = pl.BlockSpec((some, segment, width), lambda i: (i, 0, 0))
    low = pl.BlockSpec((some,) + act.shape[1:], lambda i: (i, 0, 0))
    fixed = [pl.BlockSpec(a.shape, lambda i: (0, 0))
             for a in (norm, *weights, *firsts, *seconds, *shares)]
    outs = [jax.ShapeDtypeStruct(w.shape, F32) for w in weights] * 4 + [jax.ShapeDtypeStruct(tokens.shape, F32)] * 2
    return pl.pallas_call(
        finish_kernel, grid=(clips // some,), in_specs=[wide, wide, low, low] + fixed,
        out_specs=[pl.BlockSpec(w.shape, lambda i: (0, 0)) for w in weights] * 4 + [wide, wide], out_shape=outs,
        compiler_params=pltpu.CompilerParams(dimension_semantics=("arbitrary",), vmem_limit_bytes=LIMIT),
        name="finish")(tokens, cotangent, act, dlt, norm, *weights, *firsts, *seconds, *shares)


def shards(
    tokens, kept_time, kept_bands, cotangent,
    weight_merged, weight_output, weight_expand, weight_shrink, vectors,
    first_merged, first_output, first_expand, first_shrink, first_vectors,
    second_merged, second_output, second_expand, second_shrink, second_vectors,
):
    clip_count, segment, width = tokens.shape
    dp, blk = lax.axis_size("dp"), lax.axis_size("blk")
    own = lax.axis_index("blk")
    clips = clip_count // blk
    padded = -(-segment // 16) * 16
    total = clips * blk * padded
    rows = weight_merged.shape[0]
    ff = weight_expand.shape[1]
    cube = (2,) * (bits_of(dp) + bits_of(blk))

    columns = jnp.pad(vectors.T, ((0, 0), (0, LANES - vectors.shape[0])))
    xc_home, cot_home, merged_low, wide_low, shrink_low = prepare(
        tokens, cotangent, weight_merged, columns, weight_output, weight_expand, weight_shrink, padded)
    merged, xc = front(merged_low, xc_home, dp, blk, 0)
    merged = merged.reshape(width, merged_low.shape[1])
    xc = xc.reshape(total, width)
    vec = merged[:, 3 * width:3 * width + vectors.shape[0]].T.astype(F32)
    dead = key_columns(kept_time, kept_bands, blk, own, segment, padded)
    n1, qa, kv, mix, wide, shrink, cot = attn_fwd(
        xc, dead, merged, vec, wide_low, shrink_low, cot_home, clips, HEADS, dp, blk, 1)
    wide = wide.reshape(width, wide_low.shape[1])
    shrink = shrink.reshape(ff, width)
    cot = cot.reshape(total, width)
    act, dmid, grad_expand, grad_shrink, grad_output, early, expand_early, shrink_early = ffn(
        mix, xc, cot, wide, shrink, vec, blk * padded, dp, blk, 2)

    def by_device(grad):
        return grad.reshape(cube + (grad.shape[0] // (dp * blk), grad.shape[1]))

    sent = (clips, blk, padded, width)
    owners = (2,) * (len(cube) - bits_of(FF_CHUNKS))
    merged_share, vector_share, output_share, expand_share, shrink_share, norm, act_home, dlt_home = attn_bwd(
        xc, cot, dmid, dead, n1, qa, kv, mix, merged, wide, vec, early, expand_early, shrink_early,
        by_device(grad_expand), grad_shrink.reshape((-1,) + owners + weight_shrink.shape), by_device(grad_output),
        act.reshape(sent), clips, HEADS, dp, blk, 3)
    shares = [merged_share, output_share, expand_share, shrink_share, vector_share[:, :vectors.shape[0]].T]
    *steps_out, activations, token_grads = finish(
        tokens, cotangent, act_home, dlt_home, norm, (weight_merged, weight_output, weight_expand, weight_shrink, vectors),
        (first_merged, first_output, first_expand, first_shrink, first_vectors),
        (second_merged, second_output, second_expand, second_shrink, second_vectors), shares)
    return (activations, token_grads, jnp.sqrt(norm[0, 0]), *steps_out)


def solution(mesh):
    return jax.shard_map(
        shards,
        mesh=mesh,
        in_specs=(
            P("dp", "blk", None),
            P("dp", None),
            P("dp", None),
            P("dp", "blk", None),
            P(("dp", "blk"), None),
            P(("dp", "blk"), None),
            P(("dp", "blk"), None),
            P(("dp", "blk"), None),
            P(None, ("dp", "blk")),
            P(("dp", "blk"), None),
            P(("dp", "blk"), None),
            P(("dp", "blk"), None),
            P(("dp", "blk"), None),
            P(None, ("dp", "blk")),
            P(("dp", "blk"), None),
            P(("dp", "blk"), None),
            P(("dp", "blk"), None),
            P(("dp", "blk"), None),
            P(None, ("dp", "blk")),
        ),
        out_specs=(
            P("dp", "blk", None),
            P("dp", "blk", None),
            P(),
            P(("dp", "blk"), None),
            P(("dp", "blk"), None),
            P(("dp", "blk"), None),
            P(("dp", "blk"), None),
            P(None, ("dp", "blk")),
            P(("dp", "blk"), None),
            P(("dp", "blk"), None),
            P(("dp", "blk"), None),
            P(("dp", "blk"), None),
            P(None, ("dp", "blk")),
            P(("dp", "blk"), None),
            P(("dp", "blk"), None),
            P(("dp", "blk"), None),
            P(("dp", "blk"), None),
            P(None, ("dp", "blk")),
            P(("dp", "blk"), None),
            P(("dp", "blk"), None),
            P(("dp", "blk"), None),
            P(("dp", "blk"), None),
            P(None, ("dp", "blk")),
        ),
        check_vma=False,
    )
```
